512 devices in a mesh: dp: 32 (over y, x, core), group: 16 (over z).
Axes of the slice: x: 4, y: 4, z: 16, core: 2. Of those that a mesh axis runs over, the one named last changes fastest.
Arguments:
- patches: bfloat16 [65536, 2048], P(('dp', 'group')), may hold values from -6 to 6
- codes: float32 [65536, 8], P(('dp', 'group')), may hold values from -2 to 2
- support: int32 [65536, 8], P(('dp', 'group')), may hold values from 0 to 255
- block_shards: int32 [2048, 2], P(('dp', 'group')), may hold values from 0 to 15, all different within a row; in each aligned block of 4 rows (0 to 3, 4 to 7, ...) at most 2 rows name the same one
- dictionary: bfloat16 [2048, 2048], P('group'), may hold values from -6 to 6
Outputs:
- new_dictionary: bfloat16 [2048, 2048], P('group')
- new_codes: float32 [65536, 8], P(('dp', 'group'))
- residual: bfloat16 [65536, 2048], P(('dp', 'group'))
The draws below stay inside these ranges and needn't reach their ends.
Inputs may be any that keep to these rules, and one draw needn't show every extreme that they name: `block_shards`: the two shards of a row differ; within the 4 rows of one device no shard is named more than 2 times, a bound that some block reaches.
All inputs are finite; a program needn't handle non-finite values.
Results may differ from the reference program's by a relative error of at most 0.0077.
Values may be sent and summed in bfloat16 or wider, within the bound.
No kernel may reach another device: no remote copies, remote signals or barrier semaphores. Data moves between devices by JAX's collectives and lax.ppermute only.
A program may use at most 64 MiB of HBM per device.

```python
import math
import jax
import jax.numpy as jnp
import numpy as np
from jax import lax

P_SIZE = 2048
ATOM_DEV = 128
K = 8
NB = 4
CAP = 2
ITERS = 2
BLK = 32
ATOMS = 2048
ROWS = 128
NBLOCKS = 2048
NPATCH = 65536
N_GROUP = 16


def with_ends(entries, rng, low, largest):
    dims = entries.shape
    index_at = [jax.random.randint(jax.random.fold_in(rng, axis), (), 0, dims[axis]) for axis in range(len(dims))]
    entries = entries.at[tuple(index_at)].set(low)
    longest = dims.index(max(dims))
    index_at[longest] = (index_at[longest] + 1) % dims[longest]
    return entries.at[tuple(index_at)].set(largest)


def shard_levels(key, extent, split, low, top_value):
    level, own = 1.0, jax.random.fold_in(key, 6)
    for axis_at, shards_of in split:
        draws = jnp.exp(jax.random.uniform(jax.random.fold_in(own, axis_at), (shards_of,), jnp.float32, low / len(split), top_value / len(split)))
        level = level * jnp.repeat(draws, extent[axis_at] // shards_of).reshape([-1 if axis == axis_at else 1 for axis in range(len(extent))])
    return level


def deal_out(rng, own, number, rows, count, top, limit, slope):
    sequence = jax.random.permutation(rng, count)
    heavy_load, common = load_shares(count, rows * top, limit, slope, True), load_shares(count, rows * top, limit, slope, False)
    places = jnp.arange(count)

    def named(tallies, offset_by):
        used = int((tallies > 0).sum())
        fixed = max(1, used // 4)
        passed = fixed + (places - fixed + offset_by * (used - fixed)) % max(1, count - fixed)
        return jnp.zeros((count,), jnp.int32).at[sequence[jnp.where(places < fixed, places, passed)]].set(jnp.asarray(tallies, jnp.int32))

    tallies = jnp.where(number % 4 == 0, named(heavy_load, number // 4), named(common, number - number // 4 - 1))
    mixed = jax.random.permutation(jax.random.fold_in(own, 3), count)
    donor, sink = mixed[0:count // 2 * 2:2], mixed[1:count // 2 * 2:2]
    slack = jnp.minimum(tallies[donor] - 1, limit - tallies[sink]) // 2
    slack = jnp.where((donor == sequence[0]) | (sink == sequence[0]) | (tallies[sink] == 0), 0, jnp.maximum(slack, 0))
    passed = jax.random.randint(jax.random.fold_in(own, 4), (count // 2,), 0, 1 << 20) % (slack + 1)
    tallies = tallies.at[donor].add(-passed).at[sink].add(passed)
    labels = jnp.searchsorted(jnp.cumsum(tallies), jnp.arange(rows * top), side="right").astype(jnp.int32)
    listing = labels.reshape(top, rows).T
    listing = listing[jax.random.permutation(jax.random.fold_in(own, 1), rows)]
    offset_by = jax.random.randint(jax.random.fold_in(own, 2), (rows, 1), 0, top)
    return jnp.take_along_axis(listing, (jnp.arange(top)[None, :] + offset_by) % top, axis=1)


def load_shares(number_of, total, most, lean, full):
    weights = [(1 << 20) // math.isqrt(rank ** lean) + 1 for rank in range(1, number_of + 1)]
    largest = most if full else min(most, max(-(-total // number_of), total * weights[0] // sum(weights)))
    least = 1 if total - largest >= number_of - 1 else 0
    counts, rest = [largest] + [least] * (number_of - 1), total - largest - least * (number_of - 1)
    while rest > 0:
        candidates = [i for i in range(1, number_of) if counts[i] < largest] or [i for i in range(1, number_of) if counts[i] < most]
        whole, remaining = sum([weights[i] for i in candidates]), rest
        for i in candidates:
            extra = min(most - counts[i], max(1, remaining * weights[i] // whole), rest)
            counts[i] = counts[i] + extra
            rest = rest - extra
    return np.array(counts)


def scatter_about(key, dims, scale, reach, cuts=(), held_as=jnp.bfloat16):
    drawn = scale * jax.random.normal(key, dims, jnp.float32)
    if cuts:
        drawn = drawn * shard_levels(key, dims, cuts, -0.22, 0.18)
    return jnp.clip(drawn, -reach, reach).astype(held_as)


def setup_inputs(seed: int = 0) -> dict:
    keys = jax.random.split(jax.random.key(seed), 6)
    patches = scatter_about(keys[0], (NPATCH, P_SIZE), 1.0, 6.0, ((0, 512),))
    codes = scatter_about(keys[1], (NPATCH, K), 0.3, 2.0, ((0, 512),), jnp.float32)
    support = with_ends(jax.random.randint(keys[2], (NPATCH, K), 0, 2 * ATOM_DEV), jax.random.fold_in(keys[2], 1), 0, (2 * ATOM_DEV) - 1).astype(jnp.int32)
    block_shards_keys = jax.random.split(jax.random.fold_in(keys[3], 1), NBLOCKS // NB)
    block_shards_turns = jax.random.permutation(jax.random.fold_in(keys[3], 3), NBLOCKS // NB)
    block_shards = jax.vmap(lambda own, number: deal_out(jax.random.fold_in(keys[3], 2), own, number, NB, N_GROUP, 2, CAP, 2))(block_shards_keys, block_shards_turns).reshape((NBLOCKS, 2))
    dictionary = scatter_about(keys[4], (ATOMS, P_SIZE), 1.0, 6.0, ((0, 16),))
    return {"patches": patches, "codes": codes, "support": support, "block_shards": block_shards, "dictionary": dictionary}


def atom_index(support, block_shards):
    shard_rows = jnp.repeat(block_shards, BLK, axis=0)
    which_shard = support // ATOM_DEV
    owner_shard = jnp.where(which_shard == 0, shard_rows[:, 0:1], shard_rows[:, 1:2])
    return (owner_shard * ATOM_DEV + support % ATOM_DEV).astype(jnp.int32)

def slot_weights(values, index_rows):
    same_atom = index_rows[:, :, None] == index_rows[:, None, :]
    merged = lax.optimization_barrier(jnp.sum(jnp.where(same_atom, values[:, None, :], jnp.zeros_like(values)[:, None, :]), axis=2))
    earlier = jnp.tril(jnp.ones((K, K), dtype=bool), -1)
    repeated = jnp.any(same_atom & earlier[None], axis=2)
    rounded = lax.optimization_barrier(merged.astype(jnp.bfloat16)).astype(jnp.float32)
    return jnp.where(repeated, jnp.zeros_like(rounded), rounded)

def refine(rows_in, codes_in, index_rows, dict_wide):
    picked = dict_wide[index_rows]
    signal = rows_in.astype(jnp.float32)

    def resid_of(values):
        weights = slot_weights(values, index_rows)
        rebuilt = jnp.einsum('nk,nkp->np', weights, picked, precision=lax.Precision.HIGHEST)
        return (weights, (signal - rebuilt).astype(jnp.bfloat16))
    current = codes_in
    for iteration in range(ITERS):
        weights, resid_rows = resid_of(current)
        gradient = jnp.einsum('np,nkp->nk', resid_rows.astype(jnp.float32), picked, precision=lax.Precision.HIGHEST) / P_SIZE
        current = current + 1.5 * gradient
    weights, resid_rows = resid_of(current)
    return (current, resid_rows, weights)

def reference(patches, codes, support, block_shards, dictionary):
    index_all = atom_index(support, block_shards)
    blocks_total = NPATCH // ROWS
    dict_wide = dictionary.astype(jnp.float32)

    def one_block(carry, item):
        rows_in, codes_in, index_rows = item
        new_rows, resid_rows, weights = refine(rows_in, codes_in, index_rows, dict_wide)
        flat_index = index_rows.reshape(-1)
        terms = (weights[:, :, None] * resid_rows.astype(jnp.float32)[:, None, :]).reshape(-1, P_SIZE)
        stats = carry[0] + jax.ops.segment_sum(terms, flat_index, num_segments=ATOMS)
        usage = carry[1] + jax.ops.segment_sum((weights * weights).reshape(-1), flat_index, num_segments=ATOMS)
        return ((stats, usage), (new_rows, resid_rows))
    start = (jnp.zeros((ATOMS, P_SIZE), jnp.float32), jnp.zeros((ATOMS,), jnp.float32))
    items = (patches.reshape(blocks_total, ROWS, P_SIZE), codes.reshape(blocks_total, ROWS, K), index_all.reshape(blocks_total, ROWS, K))
    (stats, usage), (new_rows, resid_rows) = lax.scan(one_block, start, items)
    moved = dict_wide + 3.0 * stats / (usage + 1.0)[:, None]
    new_dictionary = (moved * lax.rsqrt(lax.optimization_barrier(jnp.mean(moved * moved, axis=1, keepdims=True)) + 1e-05)).astype(jnp.bfloat16)
    return (new_dictionary, new_rows.reshape(NPATCH, K), resid_rows.reshape(NPATCH, P_SIZE))
```

```python
import functools

import jax
import jax.numpy as jnp
from jax import lax
from jax.experimental import pallas as pl
from jax.experimental.pallas import tpu as pltpu
from jax.sharding import PartitionSpec as P

ITERS = 2
F32 = jnp.float32
BF16 = jnp.bfloat16
NT = (((1,), (1,)), ((), ()))
VMEM_LIMIT = 56 * 1024 * 1024
MAIN = 64
MSG = 80


def refine_kernel(
    blocks, chunk, shards_ref, core_ref, x_ref, codes_ref, sup_ref, mine_ref, other_ref,
    codes_out, resid_out, msg_ref, usage_ref, rebuilt_scr,
):
    rows, plen = x_ref.shape
    half = plen // 2
    blk = rows // blocks
    slots = codes_ref.shape[1]
    chunks = half // chunk
    lane = lax.broadcasted_iota(jnp.int32, (blk, 256), 1)
    slot_lane = lax.broadcasted_iota(jnp.int32, (blk, slots), 1)
    usage_ref[...] = jnp.zeros_like(usage_ref)
    side = jnp.zeros((rows, 128), F32)
    side_parts = []
    my_off = core_ref[0] * half
    for b in range(blocks):
        r0 = b * blk
        sup = sup_ref[r0 : r0 + blk, :]
        row_a = pl.multiple_of(shards_ref[b, 0] * 128, 128)
        row_b = pl.multiple_of(shards_ref[b, 1] * 128, 128)
        hits = [sup[:, k : k + 1] == lane for k in range(slots)]

        def code_matrix(values):
            summed = jnp.zeros((blk, 256), F32)
            for k in range(slots):
                summed = summed + jnp.where(hits[k], values[:, k : k + 1], 0.0)
            return summed.astype(BF16)

        def pick(matrix):
            out = jnp.zeros((blk, slots), F32)
            for k in range(slots):
                col = jnp.sum(jnp.where(hits[k], matrix, 0.0), axis=1, keepdims=True)
                out = jnp.where(slot_lane == k, col, out)
            return out

        def atoms(ref, c0):
            return jnp.concatenate(
                [ref[pl.ds(row_a, 128), c0 : c0 + chunk], ref[pl.ds(row_b, 128), c0 : c0 + chunk]],
                axis=0,
            )

        def resid_chunk(matrix, ref, off, c0):
            d = atoms(ref, c0)
            rebuilt = jnp.dot(matrix, d, preferred_element_type=F32)
            at = pl.multiple_of(off + c0, 128)
            x = x_ref[r0 : r0 + blk, pl.ds(at, chunk)].astype(F32)
            return d, at, (x - rebuilt).astype(BF16)

        current = codes_ref[r0 : r0 + blk, :]
        for _ in range(ITERS):
            matrix = code_matrix(current)
            scores = jnp.zeros((blk, 256), F32)
            for ref, off in ((mine_ref, my_off), (other_ref, half - my_off)):
                for j in range(chunks):
                    d, _at, r = resid_chunk(matrix, ref, off, j * chunk)
                    scores = scores + lax.dot_general(r, d, NT, preferred_element_type=F32)
            current = current + 1.5 * (pick(scores) / plen)
        codes_out[r0 : r0 + blk, :] = current
        matrix = code_matrix(current)
        for ref, off in ((mine_ref, my_off), (other_ref, half - my_off)):
            for j in range(chunks):
                _d, at, r = resid_chunk(matrix, ref, off, j * chunk)
                resid_out[r0 : r0 + blk, pl.ds(at, chunk)] = r
        wide = matrix.astype(F32)
        squares = jnp.sum(wide * wide, axis=0, keepdims=True)
        usage_ref[pl.ds(shards_ref[b, 0], 1), :] += squares[:, :128]
        usage_ref[pl.ds(shards_ref[b, 1], 1), :] += squares[:, 128:]
        side_parts.append(
            jnp.concatenate(
                [pick(wide), sup.astype(F32), jnp.zeros((blk, 128 - 2 * slots), F32)], axis=1
            )
        )
    side = jnp.concatenate(side_parts, axis=0)
    side_t = jnp.transpose(side)[: 2 * slots, :].astype(BF16)
    low = lax.broadcasted_iota(jnp.int32, (MAIN, 128), 1) < 64
    for t in range(plen // 128):
        top = resid_out[:MAIN, t * 128 : (t + 1) * 128].astype(F32)
        bottom = resid_out[MAIN:, t * 128 : (t + 1) * 128].astype(F32)
        even = jnp.where(low, top, pltpu.roll(bottom, 64, 1))
        odd = jnp.where(low, pltpu.roll(top, 64, 1), bottom)
        msg_ref[2 * t, :MAIN, :] = even.astype(BF16)
        msg_ref[2 * t + 1, :MAIN, :] = odd.astype(BF16)
        msg_ref[2 * t, MAIN:, :] = side_t
        msg_ref[2 * t + 1, MAIN:, :] = side_t


def stats_kernel(sources, shards_ref, msg_ref, usage_ref, out_ref, acc_ref):
    groups = out_ref.shape[0]
    acc_ref[...] = jnp.zeros_like(acc_ref)
    atom = lax.broadcasted_iota(jnp.int32, (256, 128), 0)
    low = lax.broadcasted_iota(jnp.int32, (32, 128), 1) < 64
    low_all = lax.broadcasted_iota(jnp.int32, (128, 128), 1) < 64

    def one(q, carry):
        weights = msg_ref[q, MAIN : MAIN + 8, :].astype(F32)
        places = msg_ref[q, MAIN + 8 : MAIN + 16, :].astype(F32).astype(jnp.int32)
        matrix = jnp.zeros((256, 128), F32)
        for k in range(8):
            matrix = jnp.where(places[k : k + 1, :] == atom, weights[k : k + 1, :], matrix)
        matrix = matrix.astype(BF16)
        x0 = msg_ref[q, :32, :].astype(F32)
        x1 = msg_ref[q, 32:MAIN, :].astype(F32)
        none = jnp.zeros((32, 128), F32)
        for pair, x in ((0, x0), (1, x1)):
            first, second = jnp.where(low, x, 0.0), jnp.where(low, 0.0, x)
            parts = [none, none, none, none]
            parts[pair], parts[pair + 2] = first, second
            wide = jnp.concatenate(parts, axis=0).astype(BF16)
            out = jnp.dot(matrix, wide, preferred_element_type=F32)
            for h in range(2):
                piece = out[h * 128 : (h + 1) * 128, :]
                at0 = pl.multiple_of(shards_ref[q * 8 + pair * 2 + h] * 128, 128)
                at1 = pl.multiple_of(shards_ref[q * 8 + (pair + 2) * 2 + h] * 128, 128)
                acc_ref[pl.ds(at0, 128), :] += jnp.where(low_all, piece, 0.0)
                acc_ref[pl.ds(at1, 128), :] += jnp.where(low_all, 0.0, piece)
        return carry

    lax.fori_loop(0, sources, one, 0)
    low = lax.broadcasted_iota(jnp.int32, (MAIN, 128), 1) < 64
    row = lax.broadcasted_iota(jnp.int32, (16, 128), 0)
    for s in range(groups):
        full = acc_ref[s * 128 : (s + 1) * 128, :]
        full = full + pltpu.roll(full, 64, 1)
        out_ref[s, :MAIN, :] = jnp.where(low, full[:MAIN], full[MAIN:]).astype(BF16)
        used = usage_ref[s : s + 1, :]
        high = used.astype(BF16).astype(F32)
        rest = used - high
        out_ref[s, MAIN:, :] = jnp.where(
            row == 0, high, jnp.where(row == 1, rest, 0.0)
        ).astype(BF16)


def total_kernel(parts_ref, out_ref):
    total = parts_ref[0].astype(F32)
    for z in range(1, parts_ref.shape[0]):
        total = total + parts_ref[z].astype(F32)
    used = total[MAIN : MAIN + 1, :] + total[MAIN + 1 : MAIN + 2, :]
    high = used.astype(BF16).astype(F32)
    rest = used - high
    row = lax.broadcasted_iota(jnp.int32, (16, 128), 0)
    side = jnp.where(row == 0, high, jnp.where(row == 1, rest, 0.0))
    message = jnp.concatenate([total[:MAIN], side], axis=0).astype(BF16)
    for q in range(out_ref.shape[0]):
        out_ref[q] = message


def renew_kernel(parts_ref, dict_ref, out_ref, moved_ref):
    count = parts_ref.shape[0]
    plen = dict_ref.shape[1]
    used = jnp.zeros((16, 128), F32)
    for q in range(count):
        used = used + parts_ref[q, MAIN:, :].astype(F32)
    used = used[0:1, :] + used[1:2, :]
    column = jnp.transpose(jnp.broadcast_to(used, (128, 128)))
    gain = 3.0 / (column + 1.0)
    low = lax.broadcasted_iota(jnp.int32, (MAIN, 128), 1) < 64
    squares = jnp.zeros((128, 128), F32)
    for t in range(plen // 128):
        even = parts_ref[2 * t, :MAIN, :].astype(F32)
        odd = parts_ref[2 * t + 1, :MAIN, :].astype(F32)
        top = jnp.where(low, even, pltpu.roll(odd, 64, 1))
        bottom = jnp.where(low, pltpu.roll(even, 64, 1), odd)
        stats = jnp.concatenate([top, bottom], axis=0)
        moved = dict_ref[:, t * 128 : (t + 1) * 128].astype(F32) + gain * stats
        moved_ref[:, t * 128 : (t + 1) * 128] = moved
        squares = squares + moved * moved
    scale = lax.rsqrt(jnp.sum(squares, axis=1, keepdims=True) / plen + 1e-05)
    for t in range(plen // 128):
        out_ref[:, t * 128 : (t + 1) * 128] = (
            moved_ref[:, t * 128 : (t + 1) * 128] * scale
        ).astype(BF16)


def vmem():
    return pl.BlockSpec(memory_space=pltpu.VMEM)


def smem():
    return pl.BlockSpec(memory_space=pltpu.SMEM)


def call(kernel, ins, outs, scratch, *args):
    return pl.pallas_call(
        kernel,
        out_shape=outs,
        in_specs=ins,
        out_specs=jax.tree.map(lambda _: vmem(), outs),
        scratch_shapes=scratch,
        compiler_params=pltpu.CompilerParams(vmem_limit_bytes=VMEM_LIMIT),
    )(*args)


def body(patches, codes, support, block_shards, dictionary):
    rows, plen = patches.shape
    n_dp = lax.axis_size("dp")
    n_z = lax.axis_size("group")
    blocks = block_shards.shape[0]
    half = plen // 2
    core = lax.axis_index("dp") % 2
    part = lax.dynamic_slice(dictionary, (0, core * half), (dictionary.shape[0], half))
    mine = lax.all_gather(part, "group", axis=0, tiled=True)
    shards_all = lax.all_gather(block_shards.reshape(-1), "dp", axis=0, tiled=True)
    other = lax.ppermute(mine, "dp", [(i, i ^ 1) for i in range(n_dp)])
    sds = jax.ShapeDtypeStruct
    new_codes, resid, msg, usage = call(
        functools.partial(refine_kernel, blocks, min(256, half)),
        [smem(), smem(), vmem(), vmem(), vmem(), vmem(), vmem()],
        (
            sds(codes.shape, F32),
            sds(patches.shape, BF16),
            sds((n_dp, MSG, 128), BF16),
            sds((n_z, 128), F32),
        ),
        [pltpu.VMEM((8, 128), F32)],
        block_shards, core.reshape(1), patches, codes, support, mine, other,
    )
    got = lax.all_to_all(msg, "dp", split_axis=0, concat_axis=0, tiled=True)
    to_owner = call(
        functools.partial(stats_kernel, n_dp),
        [smem(), vmem(), vmem()],
        sds((n_z, MSG, 128), BF16),
        [pltpu.VMEM((n_z * 128, 128), F32)],
        shards_all, got, usage,
    )
    at_owner = lax.all_to_all(to_owner, "group", split_axis=0, concat_axis=0, tiled=True)
    spread = call(total_kernel, [vmem()], sds((n_dp, MSG, 128), BF16), [], at_owner)
    parts = lax.all_to_all(spread, "dp", split_axis=0, concat_axis=0, tiled=True)
    new_dictionary = call(
        renew_kernel,
        [vmem(), vmem()],
        sds(dictionary.shape, BF16),
        [pltpu.VMEM(dictionary.shape, F32)],
        parts, dictionary,
    )
    return (new_dictionary, new_codes, resid)


def solution(mesh):
    row = P(("dp", "group"), None)
    placed = (row, row, row, row, P("group", None))
    return jax.shard_map(
        body,
        mesh=mesh,
        in_specs=placed,
        out_specs=(P("group", None), row, row),
        check_vma=False,
    )
```

```python
import functools

import jax
import jax.numpy as jnp
from jax import lax
from jax.experimental import pallas as pl
from jax.experimental.pallas import tpu as pltpu
from jax.sharding import Mesh, PartitionSpec as P

F32 = jnp.float32
BF16 = jnp.bfloat16
NT = (((1,), (1,)), ((), ()))
VMEM_LIMIT = 56 * 1024 * 1024
DP_SPLIT = (4, 4, 2)
GROUP_SPLIT = (4, 4)
SHARD = 128
SLOTS = 8
MAIN = 64
MSG = 80


def pack_kernel(x_ref, codes_ref, sup_ref, names_ref, out_ref):
    rows = x_ref.shape[0]
    count, _height, width = out_ref.shape
    for j in range(count):
        out_ref[j, :rows, :] = x_ref[:, j * width : (j + 1) * width]
    side = jnp.concatenate(
        [codes_ref[...], sup_ref[...].astype(F32), jnp.zeros((rows, 128 - 2 * SLOTS), F32)], axis=1
    )
    side = jnp.transpose(side)
    codes, sup = side[:SLOTS], side[SLOTS : 2 * SLOTS]
    first = codes.astype(BF16)
    rest = codes - first.astype(F32)
    second = rest.astype(BF16)
    third = (rest - second.astype(F32)).astype(BF16)
    top = jnp.concatenate([first.astype(F32), second.astype(F32)], axis=0).astype(BF16)
    low = jnp.concatenate([third.astype(F32), sup], axis=0).astype(BF16)
    for j in range(count):
        out_ref[j, rows : rows + 16, :128] = top
        out_ref[j, rows : rows + 16, 128:256] = low
        out_ref[j, rows : rows + 16, 256:384] = names_ref[...].astype(BF16)
        for t in range(384, width, 128):
            out_ref[j, rows : rows + 16, t : t + 128] = jnp.zeros((16, 128), BF16)


def read_side(x_ref, src, rows):
    top = x_ref[src, rows : rows + 16, :128].astype(F32)
    low = x_ref[src, rows : rows + 16, 128:256].astype(F32)
    return top[:SLOTS] + top[SLOTS:] + low[:SLOTS], low[SLOTS:]


def to_rows(codes_t, sup_t):
    side = jnp.concatenate([codes_t, sup_t, jnp.zeros((128 - 2 * SLOTS, 128), F32)], axis=0)
    return jnp.transpose(side)


def atom_lanes(rows, core, piece):
    lane = lax.broadcasted_iota(jnp.int32, (rows, 256), 1)
    shift = piece.bit_length() - 1
    spot = lane & 127
    other = spot >> 6
    half = spot & 63
    place = ((half >> shift) * 2 + (core ^ other)) * piece + (half & (piece - 1))
    return ((lane & 128) + place).astype(F32)


def masks_of(side, lanes):
    return [side[:, SLOTS + k : SLOTS + k + 1] == lanes for k in range(SLOTS)]


def code_matrix(values, hits):
    summed = jnp.where(hits[0], values[:, 0:1], 0.0)
    for k in range(1, SLOTS):
        summed = summed + jnp.where(hits[k], values[:, k : k + 1], 0.0)
    return summed.astype(BF16)


def pick(matrix, hits, slot_lane):
    out = jnp.zeros(slot_lane.shape, F32)
    for k in range(SLOTS):
        col = jnp.sum(jnp.where(hits[k], matrix, 0.0), axis=1, keepdims=True)
        out = jnp.where(slot_lane == k, col, out)
    return out


def shard_row(shard, zh, zl):
    shift = zl.bit_length() - 1
    return (shard & (zl - 1)) * zh + (shard >> shift)


def refine_kernel(step, sizes, shards_ref, ids_ref, x_ref, mine_ref, other_ref, *refs):
    ny, zh, zl, plen = sizes
    count, height, width = x_ref.shape
    rows = height - 16
    piece = mine_ref.shape[2]
    blocks = rows // 32
    chunk = min(256, width)
    core = ids_ref[2]
    lanes = atom_lanes(rows, core, piece)
    slot_lane = lax.broadcasted_iota(jnp.int32, (rows, 128), 1)
    if step == 0:
        (grad_out,) = refs
    elif step == 1:
        parts_ref, grad_out, codes_out = refs
    else:
        parts_ref, codes_ref, home_out, msg_out, usage_out, codes_out = refs
        usage_out[...] = jnp.zeros_like(usage_out)
    if step > 0:
        moved = parts_ref[0]
        for j in range(1, count):
            moved = moved + parts_ref[j]
        moved = 1.5 * (moved / plen)
    low = lax.broadcasted_iota(jnp.int32, (MAIN, 128), 1) < 64
    for s in range(count):
        codes_t, sup_t = read_side(x_ref, s, rows)
        if step == 1:
            codes_t = codes_t + moved[:, s * 128 : (s + 1) * 128]
            codes_out[:, s * 128 : (s + 1) * 128] = codes_t
        if step == 2:
            codes_t = codes_ref[:, s * 128 : (s + 1) * 128] + moved[:, s * 128 : (s + 1) * 128]
            codes_out[s] = codes_t
        side = to_rows(codes_t, sup_t)
        hits = masks_of(side, lanes)
        matrix = code_matrix(side, hits)
        scores = []
        outs = [[] for _ in range(width // chunk)]
        for b in range(blocks):
            base = (ids_ref[0] * count + s) * 2 * blocks + 2 * b
            at_a = shard_row(shards_ref[base], zh, zl)
            at_b = shard_row(shards_ref[base + 1], zh, zl)
            part = matrix[b * 32 : (b + 1) * 32]
            total = None
            for j in range(width // chunk):
                c0 = j * chunk
                atoms = jnp.concatenate(
                    [
                        ref[:, at, :, c0 : c0 + chunk].reshape(ny * piece, chunk)
                        for at in (at_a, at_b)
                        for ref in (mine_ref, other_ref)
                    ],
                    axis=0,
                )
                rebuilt = jnp.dot(part, atoms, preferred_element_type=F32)
                x = x_ref[s, b * 32 : (b + 1) * 32, c0 : c0 + chunk].astype(F32)
                resid = (x - rebuilt).astype(BF16)
                if step < 2:
                    score = lax.dot_general(resid, atoms, NT, preferred_element_type=F32)
                    total = score if total is None else total + score
                else:
                    outs[j].append(resid)
            scores.append(total)
        if step < 2:
            grad = pick(jnp.concatenate(scores, axis=0), hits, slot_lane)
            grad_t = jnp.transpose(grad)[:SLOTS]
            for j in range(count):
                grad_out[j, :, s * 128 : (s + 1) * 128] = grad_t
            continue
        merged = pick(matrix.astype(F32), hits, slot_lane)
        merged_t = jnp.transpose(merged)[:SLOTS]
        side_t = jnp.concatenate([merged_t, sup_t], axis=0).astype(BF16)
        for j in range(width // chunk):
            full = jnp.concatenate(outs[j], axis=0)
            home_out[s, :, j * chunk : (j + 1) * chunk] = full
            for t in range(chunk // 128):
                u = (j * chunk) // 128 + t
                tile = full[:, t * 128 : (t + 1) * 128].astype(F32)
                top, bottom = tile[:MAIN], tile[MAIN:]
                even = jnp.where(low, top, pltpu.roll(bottom, 64, 1))
                odd = jnp.where(low, pltpu.roll(top, 64, 1), bottom)
                msg_out[2 * u, s, :MAIN, :] = even.astype(BF16)
                msg_out[2 * u + 1, s, :MAIN, :] = odd.astype(BF16)
                msg_out[2 * u, s, MAIN:, :] = side_t
                msg_out[2 * u + 1, s, MAIN:, :] = side_t

        @pl.when(ids_ref[1] == s)
        def _(side=side):
            plain = lax.broadcasted_iota(jnp.int32, (rows, 256), 1).astype(F32)
            wide = code_matrix(side, masks_of(side, plain)).astype(F32)
            wide = wide * wide
            for b in range(blocks):
                base = (ids_ref[0] * count + s) * 2 * blocks + 2 * b
                squares = jnp.sum(wide[b * 32 : (b + 1) * 32], axis=0, keepdims=True)
                usage_out[pl.ds(shards_ref[base], 1), :] += squares[:, :128]
                usage_out[pl.ds(shards_ref[base + 1], 1), :] += squares[:, 128:]


def stats_kernel(sizes, shards_ref, ids_ref, msg_ref, usage_ref, out_ref, acc_ref):
    ny, nx, zh, zl = sizes
    acc_ref[...] = jnp.zeros_like(acc_ref)
    atom = lax.broadcasted_iota(jnp.int32, (256, 128), 0).astype(F32)
    low = lax.broadcasted_iota(jnp.int32, (32, 128), 1) < 64
    low_all = lax.broadcasted_iota(jnp.int32, (128, 128), 1) < 64
    core = ids_ref[2]

    def one(q, carry):
        weights = msg_ref[q, MAIN : MAIN + 16, :].astype(F32)
        matrix = jnp.zeros((256, 128), F32)
        for k in range(SLOTS):
            matrix = jnp.where(
                weights[SLOTS + k : SLOTS + k + 1, :] == atom, weights[k : k + 1, :], matrix
            )
        matrix = matrix.astype(BF16)
        source = q // nx
        base = ((((source & 1) ^ core) * ny + (source >> 1)) * nx + q % nx) * 8
        none = jnp.zeros((32, 128), F32)
        for pair in range(2):
            x = msg_ref[q, pair * 32 : pair * 32 + 32, :].astype(F32)
            parts = [none, none, none, none]
            parts[pair], parts[pair + 2] = jnp.where(low, x, 0.0), jnp.where(low, 0.0, x)
            wide = jnp.concatenate(parts, axis=0).astype(BF16)
            out = jnp.dot(matrix, wide, preferred_element_type=F32)
            for h in range(2):
                values = out[h * 128 : (h + 1) * 128, :]
                at0 = pl.multiple_of(shards_ref[base + pair * 2 + h] * 128, 128)
                at1 = pl.multiple_of(shards_ref[base + pair * 2 + 4 + h] * 128, 128)
                acc_ref[pl.ds(at0, 128), :] += jnp.where(low_all, values, 0.0)
                acc_ref[pl.ds(at1, 128), :] += jnp.where(low_all, 0.0, values)
        return carry

    lax.fori_loop(0, msg_ref.shape[0], one, 0)
    low = lax.broadcasted_iota(jnp.int32, (MAIN, 128), 1) < 64
    row = lax.broadcasted_iota(jnp.int32, (16, 128), 0)
    for lo in range(zl):
        for hi in range(zh):
            s = hi * zl + lo
            full = acc_ref[s * 128 : (s + 1) * 128, :]
            full = full + pltpu.roll(full, 64, 1)
            out_ref[lo, hi, :MAIN, :] = jnp.where(low, full[:MAIN], full[MAIN:]).astype(BF16)
            out_ref[lo, hi, MAIN:, :] = two_parts(usage_ref[s : s + 1, :], row)


def two_parts(used, row):
    high = used.astype(BF16).astype(F32)
    return jnp.where(row == 0, high, jnp.where(row == 1, used - high, 0.0)).astype(BF16)


def summed(parts_ref, at):
    total = parts_ref[(0,) + at].astype(F32)
    for z in range(1, parts_ref.shape[0]):
        total = total + parts_ref[(z,) + at].astype(F32)
    return total


def partial_kernel(parts_ref, out_ref):
    row = lax.broadcasted_iota(jnp.int32, (16, 128), 0)
    for hi in range(out_ref.shape[0]):
        total = summed(parts_ref, (hi,))
        out_ref[hi, :MAIN, :] = total[:MAIN].astype(BF16)
        out_ref[hi, MAIN:, :] = two_parts(total[MAIN : MAIN + 1] + total[MAIN + 1 : MAIN + 2], row)


def total_kernel(parts_ref, out_ref):
    total = summed(parts_ref, ())
    row = lax.broadcasted_iota(jnp.int32, (16, 128), 0)
    main = total[:MAIN].astype(BF16)
    side = two_parts(total[MAIN : MAIN + 1] + total[MAIN + 1 : MAIN + 2], row)
    for q in range(out_ref.shape[0]):
        out_ref[q, :MAIN, :] = main
        out_ref[q, MAIN:, :] = side


def renew_kernel(sizes, parts_ref, dict_ref, out_ref, moved_ref):
    ny, nx = sizes
    plen = dict_ref.shape[1]
    used = jnp.zeros((16, 128), F32)
    for q in range(parts_ref.shape[0]):
        used = used + parts_ref[q, MAIN:, :].astype(F32)
    column = jnp.transpose(jnp.broadcast_to(used[0:1, :] + used[1:2, :], (128, 128)))
    gain = 3.0 / (column + 1.0)
    low = lax.broadcasted_iota(jnp.int32, (MAIN, 128), 1) < 64
    squares = jnp.zeros((128, 128), F32)
    for t in range(plen // 128):
        q = ((t % ny) * nx + t // ny) * 2
        even = parts_ref[q, :MAIN, :].astype(F32)
        odd = parts_ref[q + 1, :MAIN, :].astype(F32)
        top = jnp.where(low, even, pltpu.roll(odd, 64, 1))
        bottom = jnp.where(low, pltpu.roll(even, 64, 1), odd)
        stats = jnp.concatenate([top, bottom], axis=0)
        moved = dict_ref[:, t * 128 : (t + 1) * 128].astype(F32) + gain * stats
        moved_ref[:, t * 128 : (t + 1) * 128] = moved
        squares = squares + moved * moved
    scale = lax.rsqrt(jnp.sum(squares, axis=1, keepdims=True) / plen + 1e-05)
    for t in range(plen // 128):
        out_ref[:, t * 128 : (t + 1) * 128] = (
            moved_ref[:, t * 128 : (t + 1) * 128] * scale
        ).astype(BF16)


def call(kernel, ins, outs, scratch, *args, us=1):
    spaces = {"v": pltpu.VMEM, "s": pltpu.SMEM}
    return pl.pallas_call(
        kernel,
        out_shape=outs,
        in_specs=[pl.BlockSpec(memory_space=spaces[i]) for i in ins],
        out_specs=jax.tree.map(lambda _: pl.BlockSpec(memory_space=pltpu.VMEM), outs),
        scratch_shapes=scratch,
        cost_estimate=pl.CostEstimate(
            flops=us * 10**9, bytes_accessed=us * 3 * 10**6, transcendentals=0
        ),
        compiler_params=pltpu.CompilerParams(vmem_limit_bytes=VMEM_LIMIT),
    )(*args)


def exchange(x, axes):
    return lax.all_to_all(x, axes, split_axis=0, concat_axis=0, tiled=True)


def spread(x, axes, count):
    return exchange(jnp.broadcast_to(x[None], (count, *x.shape)), axes)


def body(ny, nx, zh, zl, patches, codes, support, block_shards, dictionary):
    rows, plen = patches.shape
    blocks = block_shards.shape[0]
    width = plen // nx
    nc = 2
    piece = SHARD // (ny * nc)
    sds = jax.ShapeDtypeStruct
    y, x, c = (lax.axis_index(a) for a in ("y", "x", "c"))
    ids = jnp.stack([y, x, c]).astype(jnp.int32)
    names = jnp.pad(block_shards.reshape(1, -1), ((0, 15), (0, 128 - 2 * blocks))).astype(F32)
    packed = call(
        pack_kernel,
        "vvvv",
        sds((nx, rows + 16, width), BF16),
        [],
        patches, codes, support, names,
    )
    held = exchange(packed, "x")
    names = held[:, rows, 256 : 256 + 2 * blocks].reshape(1, -1)
    own = lax.dynamic_slice(dictionary, ((y * nc + c) * piece, x * width), (piece, width))
    by_hi = spread(own, "zh", zh)
    by_z = spread(by_hi, "zl", zl).reshape(zh * zl, piece, width)
    extra = jnp.pad(names, ((0, piece - 1), (0, width - names.shape[1])))
    mine = spread(jnp.concatenate([by_z, extra[None]], axis=0), "y", ny)
    other = lax.ppermute(mine, "c", [(0, 1), (1, 0)])
    cut = 2 * blocks * nx
    shards = jnp.concatenate([mine[:, zh * zl, 0, :cut], other[:, zh * zl, 0, :cut]], axis=0)
    shards = shards.astype(jnp.int32).reshape(-1)
    common = (shards, ids, held, mine, other)
    grads = sds((nx, SLOTS, nx * rows), F32)
    first = call(
        lambda *r: refine_kernel(0, (ny, zh, zl, plen), *r), "ssvvv", grads, [], *common
    )
    second, codes_1 = call(
        lambda *r: refine_kernel(1, (ny, zh, zl, plen), *r),
        "ssvvvv",
        (grads, sds((SLOTS, nx * rows), F32)),
        [],
        *common,
        exchange(first, "x"),
    )
    home, msg, usage, codes_2 = call(
        lambda *r: refine_kernel(2, (ny, zh, zl, plen), *r),
        "ssvvvvv",
        (
            sds((nx, rows, width), BF16),
            sds((ny * nc, nx, MSG, 128), BF16),
            sds((zh * zl, 128), F32),
            sds((nx, SLOTS, rows), F32),
        ),
        [],
        *common,
        exchange(second, "x"),
        codes_1,
    )
    new_codes = jnp.transpose(lax.dynamic_index_in_dim(codes_2, x, 0, keepdims=False))
    got = exchange(msg, ("y", "c")).reshape(ny * nc * nx, MSG, 128)
    resid = jnp.transpose(exchange(home, "x"), (1, 0, 2)).reshape(rows, plen)
    to_owner = call(
        lambda *r: stats_kernel((ny, nx, zh, zl), *r),
        "ssvv",
        sds((zl, zh, MSG, 128), BF16),
        [pltpu.VMEM((zh * zl * SHARD, 128), F32)],
        shards, ids, got, usage, us=10,
    )
    nearer = call(partial_kernel, "v", sds((zh, MSG, 128), BF16), [], exchange(to_owner, "zl"))
    final = call(
        total_kernel, "v", sds((ny * nx * nc, MSG, 128), BF16), [], exchange(nearer, "zh")
    )
    new_dictionary = call(
        lambda *r: renew_kernel((ny, nx), *r),
        "vv",
        sds(dictionary.shape, BF16),
        [pltpu.VMEM(dictionary.shape, F32)],
        exchange(final, ("y", "x", "c")), dictionary,
    )
    return (new_dictionary, new_codes, resid)


def solution(mesh):
    fine = Mesh(mesh.devices.reshape(DP_SPLIT + GROUP_SPLIT), ("y", "x", "c", "zh", "zl"))
    row = P(("y", "x", "c", "zh", "zl"), None)
    shard = P(("zh", "zl"), None)
    return jax.shard_map(
        functools.partial(body, DP_SPLIT[0], DP_SPLIT[1], *GROUP_SPLIT),
        mesh=fine,
        in_specs=(row, row, row, row, shard),
        out_specs=(shard, row, row),
        check_vma=False,
    )
```

```python
import functools

import jax
import jax.numpy as jnp
from jax import lax
from jax.experimental import pallas as pl
from jax.experimental.pallas import tpu as pltpu
from jax.sharding import Mesh, PartitionSpec as P

F32 = jnp.float32
BF16 = jnp.bfloat16
NT = (((1,), (1,)), ((), ()))
VMEM_LIMIT = 56 * 1024 * 1024
DP_SPLIT = (4, 4, 2)
GROUP_SPLIT = (4, 4)
SHARD = 128
SLOTS = 8
MAIN = 64
MSG = 80


def pack_kernel(x_ref, codes_ref, sup_ref, names_ref, out_ref):
    rows = x_ref.shape[0]
    count, _height, width = out_ref.shape
    for j in range(count):
        out_ref[j, :rows, :] = x_ref[:, j * width : (j + 1) * width]
    side = jnp.concatenate(
        [codes_ref[...], sup_ref[...].astype(F32), jnp.zeros((rows, 128 - 2 * SLOTS), F32)], axis=1
    )
    side = jnp.transpose(side)
    codes, sup = side[:SLOTS], side[SLOTS : 2 * SLOTS]
    first = codes.astype(BF16)
    rest = codes - first.astype(F32)
    second = rest.astype(BF16)
    third = (rest - second.astype(F32)).astype(BF16)
    top = jnp.concatenate([first.astype(F32), second.astype(F32)], axis=0).astype(BF16)
    low = jnp.concatenate([third.astype(F32), sup], axis=0).astype(BF16)
    for j in range(count):
        out_ref[j, rows : rows + 16, :128] = top
        out_ref[j, rows : rows + 16, 128:256] = low
        out_ref[j, rows : rows + 16, 256:384] = names_ref[...].astype(BF16)
        for t in range(384, width, 128):
            out_ref[j, rows : rows + 16, t : t + 128] = jnp.zeros((16, 128), BF16)


def read_side(x_ref, src, rows):
    top = x_ref[src, rows : rows + 16, :128].astype(F32)
    low = x_ref[src, rows : rows + 16, 128:256].astype(F32)
    return top[:SLOTS] + top[SLOTS:] + low[:SLOTS], low[SLOTS:]


def to_rows(codes_t, sup_t):
    side = jnp.concatenate([codes_t, sup_t, jnp.zeros((128 - 2 * SLOTS, 128), F32)], axis=0)
    return jnp.transpose(side)


def atom_lanes(rows, core, piece):
    lane = lax.broadcasted_iota(jnp.int32, (rows, 256), 1)
    shift = piece.bit_length() - 1
    spot = lane & 127
    other = spot >> 6
    half = spot & 63
    place = ((half >> shift) * 2 + (core ^ other)) * piece + (half & (piece - 1))
    return ((lane & 128) + place).astype(F32)


def masks_of(side, lanes):
    return [side[:, SLOTS + k : SLOTS + k + 1] == lanes for k in range(SLOTS)]


def code_matrix(values, hits):
    summed = jnp.where(hits[0], values[:, 0:1], 0.0)
    for k in range(1, SLOTS):
        summed = summed + jnp.where(hits[k], values[:, k : k + 1], 0.0)
    return summed.astype(BF16)


def pick(matrix, hits, slot_lane):
    out = jnp.zeros(slot_lane.shape, F32)
    for k in range(SLOTS):
        col = jnp.sum(jnp.where(hits[k], matrix, 0.0), axis=1, keepdims=True)
        out = jnp.where(slot_lane == k, col, out)
    return out


def shard_row(shard, zh, zl):
    shift = zl.bit_length() - 1
    return (shard & (zl - 1)) * zh + (shard >> shift)


def refine_kernel(step, sizes, shards_ref, ids_ref, x_ref, mine_ref, other_ref, *refs):
    ny, zh, zl, plen = sizes
    count, height, width = x_ref.shape
    rows = height - 16
    piece = mine_ref.shape[2]
    blocks = rows // 32
    chunk = min(256, width)
    core = ids_ref[2]
    lanes = atom_lanes(rows, core, piece)
    slot_lane = lax.broadcasted_iota(jnp.int32, (rows, 128), 1)
    if step == 0:
        (grad_out,) = refs
    elif step == 1:
        parts_ref, grad_out, codes_out = refs
    else:
        parts_ref, codes_ref, home_out, msg_out, usage_out, codes_out = refs
        usage_out[...] = jnp.zeros_like(usage_out)
    if step > 0:
        moved = parts_ref[0]
        for j in range(1, count):
            moved = moved + parts_ref[j]
        moved = 1.5 * (moved / plen)
    low = lax.broadcasted_iota(jnp.int32, (MAIN, 128), 1) < 64
    for s in range(count):
        codes_t, sup_t = read_side(x_ref, s, rows)
        if step == 1:
            codes_t = codes_t + moved[:, s * 128 : (s + 1) * 128]
            codes_out[:, s * 128 : (s + 1) * 128] = codes_t
        if step == 2:
            codes_t = codes_ref[:, s * 128 : (s + 1) * 128] + moved[:, s * 128 : (s + 1) * 128]
            codes_out[s] = codes_t
        side = to_rows(codes_t, sup_t)
        hits = masks_of(side, lanes)
        matrix = code_matrix(side, hits)
        scores = []
        outs = [[] for _ in range(width // chunk)]
        for b in range(blocks):
            base = (ids_ref[0] * count + s) * 2 * blocks + 2 * b
            at_a = shard_row(shards_ref[base], zh, zl)
            at_b = shard_row(shards_ref[base + 1], zh, zl)
            part = matrix[b * 32 : (b + 1) * 32]
            total = None
            for j in range(width // chunk):
                c0 = j * chunk
                atoms = jnp.concatenate(
                    [
                        ref[:, at, :, c0 : c0 + chunk].reshape(ny * piece, chunk)
                        for at in (at_a, at_b)
                        for ref in (mine_ref, other_ref)
                    ],
                    axis=0,
                )
                rebuilt = jnp.dot(part, atoms, preferred_element_type=F32)
                x = x_ref[s, b * 32 : (b + 1) * 32, c0 : c0 + chunk].astype(F32)
                resid = (x - rebuilt).astype(BF16)
                if step < 2:
                    score = lax.dot_general(resid, atoms, NT, preferred_element_type=F32)
                    total = score if total is None else total + score
                else:
                    outs[j].append(resid)
            scores.append(total)
        if step < 2:
            grad = pick(jnp.concatenate(scores, axis=0), hits, slot_lane)
            grad_t = jnp.transpose(grad)[:SLOTS]
            for j in range(count):
                grad_out[j, :, s * 128 : (s + 1) * 128] = grad_t
            continue
        merged = pick(matrix.astype(F32), hits, slot_lane)
        merged_t = jnp.transpose(merged)[:SLOTS]
        side_t = jnp.concatenate([merged_t, sup_t], axis=0).astype(BF16)
        for j in range(width // chunk):
            full = jnp.concatenate(outs[j], axis=0)
            home_out[s, :, j * chunk : (j + 1) * chunk] = full
            for t in range(chunk // 128):
                u = (j * chunk) // 128 + t
                tile = full[:, t * 128 : (t + 1) * 128].astype(F32)
                top, bottom = tile[:MAIN], tile[MAIN:]
                even = jnp.where(low, top, pltpu.roll(bottom, 64, 1))
                odd = jnp.where(low, pltpu.roll(top, 64, 1), bottom)
                msg_out[2 * u, s, :MAIN, :] = even.astype(BF16)
                msg_out[2 * u + 1, s, :MAIN, :] = odd.astype(BF16)
                msg_out[2 * u, s, MAIN:, :] = side_t
                msg_out[2 * u + 1, s, MAIN:, :] = side_t

        @pl.when(ids_ref[1] == s)
        def _(side=side):
            plain = lax.broadcasted_iota(jnp.int32, (rows, 256), 1).astype(F32)
            wide = code_matrix(side, masks_of(side, plain)).astype(F32)
            wide = wide * wide
            for b in range(blocks):
                base = (ids_ref[0] * count + s) * 2 * blocks + 2 * b
                squares = jnp.sum(wide[b * 32 : (b + 1) * 32], axis=0, keepdims=True)
                usage_out[pl.ds(shards_ref[base], 1), :] += squares[:, :128]
                usage_out[pl.ds(shards_ref[base + 1], 1), :] += squares[:, 128:]


def stats_kernel(sizes, shards_ref, ids_ref, msg_ref, usage_ref, out_ref, acc_ref):
    ny, nx, zh, zl = sizes
    acc_ref[...] = jnp.zeros_like(acc_ref)
    atom = lax.broadcasted_iota(jnp.int32, (256, 128), 0).astype(F32)
    low = lax.broadcasted_iota(jnp.int32, (32, 128), 1) < 64
    low_all = lax.broadcasted_iota(jnp.int32, (128, 128), 1) < 64
    core = ids_ref[2]

    def one(q, carry):
        weights = msg_ref[q, MAIN : MAIN + 16, :].astype(F32)
        matrix = jnp.zeros((256, 128), F32)
        for k in range(SLOTS):
            matrix = jnp.where(
                weights[SLOTS + k : SLOTS + k + 1, :] == atom, weights[k : k + 1, :], matrix
            )
        matrix = matrix.astype(BF16)
        source = q // nx
        base = ((((source & 1) ^ core) * ny + (source >> 1)) * nx + q % nx) * 8
        none = jnp.zeros((32, 128), F32)
        for pair in range(2):
            x = msg_ref[q, pair * 32 : pair * 32 + 32, :].astype(F32)
            parts = [none, none, none, none]
            parts[pair], parts[pair + 2] = jnp.where(low, x, 0.0), jnp.where(low, 0.0, x)
            wide = jnp.concatenate(parts, axis=0).astype(BF16)
            out = jnp.dot(matrix, wide, preferred_element_type=F32)
            for h in range(2):
                values = out[h * 128 : (h + 1) * 128, :]
                at0 = pl.multiple_of(shards_ref[base + pair * 2 + h] * 128, 128)
                at1 = pl.multiple_of(shards_ref[base + pair * 2 + 4 + h] * 128, 128)
                acc_ref[pl.ds(at0, 128), :] += jnp.where(low_all, values, 0.0)
                acc_ref[pl.ds(at1, 128), :] += jnp.where(low_all, 0.0, values)
        return carry

    lax.fori_loop(0, msg_ref.shape[0], one, 0)
    low = lax.broadcasted_iota(jnp.int32, (MAIN, 128), 1) < 64
    row = lax.broadcasted_iota(jnp.int32, (16, 128), 0)
    for lo in range(zl):
        for hi in range(zh):
            s = hi * zl + lo
            full = acc_ref[s * 128 : (s + 1) * 128, :]
            full = full + pltpu.roll(full, 64, 1)
            out_ref[s, :MAIN, :] = jnp.where(low, full[:MAIN], full[MAIN:]).astype(BF16)
            out_ref[s, MAIN:, :] = two_parts(usage_ref[s : s + 1, :], row)


def two_parts(used, row):
    high = used.astype(BF16).astype(F32)
    return jnp.where(row == 0, high, jnp.where(row == 1, used - high, 0.0)).astype(BF16)


def summed(parts_ref, at):
    total = parts_ref[(0,) + at].astype(F32)
    for z in range(1, parts_ref.shape[0]):
        total = total + parts_ref[(z,) + at].astype(F32)
    return total


def total_kernel(parts_ref, out_ref):
    total = summed(parts_ref, ())
    row = lax.broadcasted_iota(jnp.int32, (16, 128), 0)
    main = total[:MAIN].astype(BF16)
    side = two_parts(total[MAIN : MAIN + 1] + total[MAIN + 1 : MAIN + 2], row)
    for q in range(out_ref.shape[0]):
        out_ref[q, :MAIN, :] = main
        out_ref[q, MAIN:, :] = side


def renew_kernel(sizes, parts_ref, dict_ref, out_ref, moved_ref):
    ny, nx = sizes
    plen = dict_ref.shape[1]
    used = jnp.zeros((16, 128), F32)
    for q in range(parts_ref.shape[0]):
        used = used + parts_ref[q, MAIN:, :].astype(F32)
    column = jnp.transpose(jnp.broadcast_to(used[0:1, :] + used[1:2, :], (128, 128)))
    gain = 3.0 / (column + 1.0)
    low = lax.broadcasted_iota(jnp.int32, (MAIN, 128), 1) < 64
    squares = jnp.zeros((128, 128), F32)
    for t in range(plen // 128):
        q = ((t % ny) * nx + t // ny) * 2
        even = parts_ref[q, :MAIN, :].astype(F32)
        odd = parts_ref[q + 1, :MAIN, :].astype(F32)
        top = jnp.where(low, even, pltpu.roll(odd, 64, 1))
        bottom = jnp.where(low, pltpu.roll(even, 64, 1), odd)
        stats = jnp.concatenate([top, bottom], axis=0)
        moved = dict_ref[:, t * 128 : (t + 1) * 128].astype(F32) + gain * stats
        moved_ref[:, t * 128 : (t + 1) * 128] = moved
        squares = squares + moved * moved
    scale = lax.rsqrt(jnp.sum(squares, axis=1, keepdims=True) / plen + 1e-05)
    for t in range(plen // 128):
        out_ref[:, t * 128 : (t + 1) * 128] = (
            moved_ref[:, t * 128 : (t + 1) * 128] * scale
        ).astype(BF16)


def call(kernel, ins, outs, scratch, *args, us=1):
    spaces = {"v": pltpu.VMEM, "s": pltpu.SMEM}
    return pl.pallas_call(
        kernel,
        out_shape=outs,
        in_specs=[pl.BlockSpec(memory_space=spaces[i]) for i in ins],
        out_specs=jax.tree.map(lambda _: pl.BlockSpec(memory_space=pltpu.VMEM), outs),
        scratch_shapes=scratch,
        cost_estimate=pl.CostEstimate(
            flops=us * 10**9, bytes_accessed=us * 3 * 10**6, transcendentals=0
        ),
        compiler_params=pltpu.CompilerParams(vmem_limit_bytes=VMEM_LIMIT),
    )(*args)


def exchange(x, axes):
    return lax.all_to_all(x, axes, split_axis=0, concat_axis=0, tiled=True)


def spread(x, axes, count):
    return exchange(jnp.broadcast_to(x[None], (count, *x.shape)), axes)


def body(ny, nx, zh, zl, patches, codes, support, block_shards, dictionary):
    rows, plen = patches.shape
    blocks = block_shards.shape[0]
    width = plen // nx
    nc = 2
    piece = SHARD // (ny * nc)
    sds = jax.ShapeDtypeStruct
    y, x, c = (lax.axis_index(a) for a in ("y", "x", "c"))
    ids = jnp.stack([y, x, c]).astype(jnp.int32)
    names = jnp.pad(block_shards.reshape(1, -1), ((0, 15), (0, 128 - 2 * blocks))).astype(F32)
    packed = call(
        pack_kernel,
        "vvvv",
        sds((nx, rows + 16, width), BF16),
        [],
        patches, codes, support, names,
    )
    held = exchange(packed, "x")
    names = held[:, rows, 256 : 256 + 2 * blocks].reshape(1, -1)
    own = lax.dynamic_slice(dictionary, ((y * nc + c) * piece, x * width), (piece, width))
    by_hi = spread(own, "zh", zh)
    by_z = spread(by_hi, "zl", zl).reshape(zh * zl, piece, width)
    extra = jnp.pad(names, ((0, piece - 1), (0, width - names.shape[1])))
    mine = spread(jnp.concatenate([by_z, extra[None]], axis=0), "y", ny)
    other = lax.ppermute(mine, "c", [(0, 1), (1, 0)])
    cut = 2 * blocks * nx
    shards = jnp.concatenate([mine[:, zh * zl, 0, :cut], other[:, zh * zl, 0, :cut]], axis=0)
    shards = shards.astype(jnp.int32).reshape(-1)
    common = (shards, ids, held, mine, other)
    grads = sds((nx, SLOTS, nx * rows), F32)
    first = call(
        lambda *r: refine_kernel(0, (ny, zh, zl, plen), *r), "ssvvv", grads, [], *common
    )
    second, codes_1 = call(
        lambda *r: refine_kernel(1, (ny, zh, zl, plen), *r),
        "ssvvvv",
        (grads, sds((SLOTS, nx * rows), F32)),
        [],
        *common,
        exchange(first, "x"),
    )
    home, msg, usage, codes_2 = call(
        lambda *r: refine_kernel(2, (ny, zh, zl, plen), *r),
        "ssvvvvv",
        (
            sds((nx, rows, width), BF16),
            sds((ny * nc, nx, MSG, 128), BF16),
            sds((zh * zl, 128), F32),
            sds((nx, SLOTS, rows), F32),
        ),
        [],
        *common,
        exchange(second, "x"),
        codes_1,
    )
    new_codes = jnp.transpose(lax.dynamic_index_in_dim(codes_2, x, 0, keepdims=False))
    got = exchange(msg, ("y", "c")).reshape(ny * nc * nx, MSG, 128)
    at_home = exchange(home, "x")
    to_owner = call(
        lambda *r: stats_kernel((ny, nx, zh, zl), *r),
        "ssvv",
        sds((zh * zl, MSG, 128), BF16),
        [pltpu.VMEM((zh * zl * SHARD, 128), F32)],
        shards, ids, got, usage, us=10,
    )
    to_owner, at_home = lax.optimization_barrier((to_owner, at_home))
    resid = jnp.transpose(at_home, (1, 0, 2)).reshape(rows, plen)
    final = call(
        total_kernel,
        "v",
        sds((ny * nx * nc, MSG, 128), BF16),
        [],
        exchange(to_owner, ("zh", "zl")),
    )
    new_dictionary = call(
        lambda *r: renew_kernel((ny, nx), *r),
        "vv",
        sds(dictionary.shape, BF16),
        [pltpu.VMEM(dictionary.shape, F32)],
        exchange(final, ("y", "x", "c")), dictionary,
    )
    return (new_dictionary, new_codes, resid)


def solution(mesh):
    fine = Mesh(mesh.devices.reshape(DP_SPLIT + GROUP_SPLIT), ("y", "x", "c", "zh", "zl"))
    row = P(("y", "x", "c", "zh", "zl"), None)
    shard = P(("zh", "zl"), None)
    return jax.shard_map(
        functools.partial(body, DP_SPLIT[0], DP_SPLIT[1], *GROUP_SPLIT),
        mesh=fine,
        in_specs=(row, row, row, row, shard),
        out_specs=(shard, row, row),
        check_vma=False,
    )
```

```python
import functools

import jax
import jax.numpy as jnp
from jax import lax
from jax.experimental import pallas as pl
from jax.experimental.pallas import tpu as pltpu
from jax.sharding import Mesh, PartitionSpec as P

F32 = jnp.float32
BF16 = jnp.bfloat16
NT = (((1,), (1,)), ((), ()))
VMEM_LIMIT = 56 * 1024 * 1024
DP_SPLIT = (4, 4, 2)
GROUP_SPLIT = (4, 4)
SHARD = 128
SLOTS = 8
MAIN = 64
MSG = 80


def pack_kernel(names_ref, ids_ref, x_ref, codes_ref, sup_ref, *outs):
    rows = x_ref.shape[0]
    width = outs[0].shape[1]
    count = len(outs)
    codes = codes_ref[...]
    first = codes.astype(BF16).astype(F32)
    rest = codes - first
    second = rest.astype(BF16).astype(F32)
    third = rest - second
    top = jnp.concatenate([first, second], axis=0).astype(BF16)
    low = jnp.concatenate([third, sup_ref[...].astype(F32)], axis=0).astype(BF16)
    lane = lax.broadcasted_iota(jnp.int32, (16, 128), 1)
    names = jnp.zeros((16, 128), jnp.int32)
    for b in range(names_ref.shape[1]):
        for h in range(2):
            names = jnp.where(lane == 2 * b + h, names_ref[h, b], names)
    names = names.astype(F32).astype(BF16)
    for j in range(count):
        start = pl.multiple_of(((ids_ref[1] + j) & (count - 1)) * width, 128)
        outs[j][:rows, :] = x_ref[:, pl.ds(start, width)]
        outs[j][rows : rows + 16, :128] = top
        outs[j][rows : rows + 16, 128:256] = low
        outs[j][rows : rows + 16, 256:384] = names
        for t in range(384, width, 128):
            outs[j][rows : rows + 16, t : t + 128] = jnp.zeros((16, 128), BF16)


def read_side(x_ref, rows):
    top = x_ref[rows : rows + 16, :128].astype(F32)
    low = x_ref[rows : rows + 16, 128:256].astype(F32)
    return top[:SLOTS] + top[SLOTS:] + low[:SLOTS], low[SLOTS:]


def to_rows(codes_t, sup_t):
    side = jnp.concatenate([codes_t, sup_t, jnp.zeros((128 - 2 * SLOTS, 128), F32)], axis=0)
    return jnp.transpose(side)


def atom_lanes(rows, core, piece):
    lane = lax.broadcasted_iota(jnp.int32, (rows, 256), 1)
    shift = piece.bit_length() - 1
    spot = lane & 127
    other = spot >> 6
    half = spot & 63
    place = ((half >> shift) * 2 + (core ^ other)) * piece + (half & (piece - 1))
    return ((lane & 128) + place).astype(F32)


def masks_of(side, lanes):
    return [side[:, SLOTS + k : SLOTS + k + 1] == lanes for k in range(SLOTS)]


def code_matrix(values, hits):
    summed = jnp.where(hits[0], values[:, 0:1], 0.0)
    for k in range(1, SLOTS):
        summed = summed + jnp.where(hits[k], values[:, k : k + 1], 0.0)
    return summed.astype(BF16)


def pick(matrix, hits, slot_lane):
    out = jnp.zeros(slot_lane.shape, F32)
    for k in range(SLOTS):
        col = jnp.sum(jnp.where(hits[k], matrix, 0.0), axis=1, keepdims=True)
        out = jnp.where(slot_lane == k, col, out)
    return out


def shard_row(shard, zh, zl):
    shift = zl.bit_length() - 1
    return (shard & (zl - 1)) * zh + (shard >> shift)


def refine_kernel(step, sizes, shards_ref, ids_ref, *refs):
    ny, nx, zh, zl, plen = sizes
    x_refs, (mine_ref, other_ref), refs = refs[:nx], refs[nx : nx + 2], refs[nx + 2 :]
    height, width = x_refs[0].shape
    rows = height - 16
    piece = mine_ref.shape[2]
    blocks = rows // 32
    chunk = min(256, width)
    core = ids_ref[2]
    lanes = atom_lanes(rows, core, piece)
    slot_lane = lax.broadcasted_iota(jnp.int32, (rows, 128), 1)
    if step == 0:
        (grad_out,) = refs
    elif step == 1:
        parts_ref, grad_out, codes_out = refs
    else:
        parts_ref, codes_ref, home_out, msg_out, usage_out, codes_out = refs
    low = lax.broadcasted_iota(jnp.int32, (MAIN, 128), 1) < 64
    for s in range(nx):
        source = (ids_ref[1] - s) & (nx - 1)
        at = pl.ds(pl.multiple_of(source * 128, 128), 128)
        mine = slice(s * 128, (s + 1) * 128)
        codes_t, sup_t = read_side(x_refs[s], rows)
        if step > 0:
            moved = parts_ref[0, :, at]
            for j in range(1, nx):
                moved = moved + parts_ref[j, :, at]
            moved = 1.5 * (moved / plen)
        if step == 1:
            codes_t = codes_t + moved
            codes_out[:, mine] = codes_t
        if step == 2:
            codes_t = codes_ref[:, mine] + moved
            if s == 0:
                codes_out[...] = codes_t
        side = to_rows(codes_t, sup_t)
        hits = masks_of(side, lanes)
        matrix = code_matrix(side, hits)
        scores = []
        outs = [[] for _ in range(width // chunk)]
        for b in range(blocks):
            base = (ids_ref[0] * nx + s) * 2 * blocks + 2 * b
            at_a = shard_row(shards_ref[base], zh, zl)
            at_b = shard_row(shards_ref[base + 1], zh, zl)
            part = matrix[b * 32 : (b + 1) * 32]
            total = None
            for j in range(width // chunk):
                c0 = j * chunk
                atoms = jnp.concatenate(
                    [
                        ref[:, z, :, c0 : c0 + chunk].reshape(ny * piece, chunk)
                        for z in (at_a, at_b)
                        for ref in (mine_ref, other_ref)
                    ],
                    axis=0,
                )
                rebuilt = jnp.dot(part, atoms, preferred_element_type=F32)
                x = x_refs[s][b * 32 : (b + 1) * 32, c0 : c0 + chunk].astype(F32)
                resid = (x - rebuilt).astype(BF16)
                if step < 2:
                    score = lax.dot_general(resid, atoms, NT, preferred_element_type=F32)
                    total = score if total is None else total + score
                else:
                    outs[j].append(resid)
            scores.append(total)
        if step < 2:
            grad = pick(jnp.concatenate(scores, axis=0), hits, slot_lane)
            grad_t = jnp.transpose(grad)[:SLOTS]
            for j in range(nx):
                grad_out[j, :, at] = grad_t
            continue
        merged_t = jnp.transpose(pick(matrix.astype(F32), hits, slot_lane))[:SLOTS]
        side_t = jnp.concatenate([merged_t, sup_t], axis=0).astype(BF16)
        for j in range(width // chunk):
            full = jnp.concatenate(outs[j], axis=0)
            home_out[source, :, j * chunk : (j + 1) * chunk] = full
            for t in range(chunk // 128):
                u = (j * chunk) // 128 + t
                tile = full[:, t * 128 : (t + 1) * 128].astype(F32)
                top, bottom = tile[:MAIN], tile[MAIN:]
                even = jnp.where(low, top, pltpu.roll(bottom, 64, 1))
                odd = jnp.where(low, pltpu.roll(top, 64, 1), bottom)
                msg_out[2 * u, source, :MAIN, :] = even.astype(BF16)
                msg_out[2 * u + 1, source, :MAIN, :] = odd.astype(BF16)
                msg_out[2 * u, source, MAIN:, :] = side_t
                msg_out[2 * u + 1, source, MAIN:, :] = side_t
        if s == 0:
            usage_out[...] = jnp.zeros_like(usage_out)
            plain = lax.broadcasted_iota(jnp.int32, (rows, 256), 1).astype(F32)
            wide = code_matrix(side, masks_of(side, plain)).astype(F32)
            wide = wide * wide
            for b in range(blocks):
                base = (ids_ref[0] * nx + s) * 2 * blocks + 2 * b
                squares = jnp.sum(wide[b * 32 : (b + 1) * 32], axis=0, keepdims=True)
                usage_out[pl.ds(shards_ref[base], 1), :] += squares[:, :128]
                usage_out[pl.ds(shards_ref[base + 1], 1), :] += squares[:, 128:]


def stats_kernel(sizes, shards_ref, ids_ref, msg_ref, usage_ref, out_ref, acc_ref):
    ny, nx, zh, zl = sizes
    acc_ref[...] = jnp.zeros_like(acc_ref)
    atom = lax.broadcasted_iota(jnp.int32, (256, 128), 0).astype(F32)
    low = lax.broadcasted_iota(jnp.int32, (32, 128), 1) < 64
    low_all = lax.broadcasted_iota(jnp.int32, (128, 128), 1) < 64
    core = ids_ref[2]

    def one(q, carry):
        weights = msg_ref[q, MAIN : MAIN + 16, :].astype(F32)
        matrix = jnp.zeros((256, 128), F32)
        for k in range(SLOTS):
            matrix = jnp.where(
                weights[SLOTS + k : SLOTS + k + 1, :] == atom, weights[k : k + 1, :], matrix
            )
        matrix = matrix.astype(BF16)
        source = q // nx
        away = (ids_ref[1] - q) & (nx - 1)
        base = ((((source & 1) ^ core) * ny + (source >> 1)) * nx + away) * 8
        none = jnp.zeros((32, 128), F32)
        for pair in range(2):
            x = msg_ref[q, pair * 32 : pair * 32 + 32, :].astype(F32)
            parts = [none, none, none, none]
            parts[pair], parts[pair + 2] = jnp.where(low, x, 0.0), jnp.where(low, 0.0, x)
            wide = jnp.concatenate(parts, axis=0).astype(BF16)
            out = jnp.dot(matrix, wide, preferred_element_type=F32)
            for h in range(2):
                values = out[h * 128 : (h + 1) * 128, :]
                at0 = pl.multiple_of(shards_ref[base + pair * 2 + h] * 128, 128)
                at1 = pl.multiple_of(shards_ref[base + pair * 2 + 4 + h] * 128, 128)
                acc_ref[pl.ds(at0, 128), :] += jnp.where(low_all, values, 0.0)
                acc_ref[pl.ds(at1, 128), :] += jnp.where(low_all, 0.0, values)
        return carry

    lax.fori_loop(0, msg_ref.shape[0], one, 0)
    low = lax.broadcasted_iota(jnp.int32, (MAIN, 128), 1) < 64
    row = lax.broadcasted_iota(jnp.int32, (16, 128), 0)
    for lo in range(zl):
        for hi in range(zh):
            s = hi * zl + lo
            full = acc_ref[s * 128 : (s + 1) * 128, :]
            full = full + pltpu.roll(full, 64, 1)
            out_ref[s, :MAIN, :] = jnp.where(low, full[:MAIN], full[MAIN:]).astype(BF16)
            out_ref[s, MAIN:, :] = two_parts(usage_ref[s : s + 1, :], row)


def two_parts(used, row):
    high = used.astype(BF16).astype(F32)
    return jnp.where(row == 0, high, jnp.where(row == 1, used - high, 0.0)).astype(BF16)


def summed(parts_ref, at):
    total = parts_ref[(0,) + at].astype(F32)
    for z in range(1, parts_ref.shape[0]):
        total = total + parts_ref[(z,) + at].astype(F32)
    return total


def total_kernel(parts_ref, out_ref):
    total = summed(parts_ref, ())
    row = lax.broadcasted_iota(jnp.int32, (16, 128), 0)
    main = total[:MAIN].astype(BF16)
    side = two_parts(total[MAIN : MAIN + 1] + total[MAIN + 1 : MAIN + 2], row)
    for q in range(out_ref.shape[0]):
        out_ref[q, :MAIN, :] = main
        out_ref[q, MAIN:, :] = side


def renew_kernel(sizes, parts_ref, dict_ref, out_ref, moved_ref):
    ny, nx = sizes
    plen = dict_ref.shape[1]
    used = jnp.zeros((16, 128), F32)
    for q in range(parts_ref.shape[0]):
        used = used + parts_ref[q, MAIN:, :].astype(F32)
    column = jnp.transpose(jnp.broadcast_to(used[0:1, :] + used[1:2, :], (128, 128)))
    gain = 3.0 / (column + 1.0)
    low = lax.broadcasted_iota(jnp.int32, (MAIN, 128), 1) < 64
    squares = jnp.zeros((128, 128), F32)
    for t in range(plen // 128):
        q = ((t % ny) * nx + t // ny) * 2
        even = parts_ref[q, :MAIN, :].astype(F32)
        odd = parts_ref[q + 1, :MAIN, :].astype(F32)
        top = jnp.where(low, even, pltpu.roll(odd, 64, 1))
        bottom = jnp.where(low, pltpu.roll(even, 64, 1), odd)
        stats = jnp.concatenate([top, bottom], axis=0)
        moved = dict_ref[:, t * 128 : (t + 1) * 128].astype(F32) + gain * stats
        moved_ref[:, t * 128 : (t + 1) * 128] = moved
        squares = squares + moved * moved
    scale = lax.rsqrt(jnp.sum(squares, axis=1, keepdims=True) / plen + 1e-05)
    for t in range(plen // 128):
        out_ref[:, t * 128 : (t + 1) * 128] = (
            moved_ref[:, t * 128 : (t + 1) * 128] * scale
        ).astype(BF16)


def call(kernel, ins, outs, scratch, *args, us=1):
    spaces = {"v": pltpu.VMEM, "s": pltpu.SMEM}
    return pl.pallas_call(
        kernel,
        out_shape=outs,
        in_specs=[pl.BlockSpec(memory_space=spaces[i]) for i in ins],
        out_specs=jax.tree.map(lambda _: pl.BlockSpec(memory_space=pltpu.VMEM), outs),
        scratch_shapes=scratch,
        cost_estimate=pl.CostEstimate(
            flops=us * 10**9, bytes_accessed=us * 3 * 10**6, transcendentals=0
        ),
        compiler_params=pltpu.CompilerParams(vmem_limit_bytes=VMEM_LIMIT),
    )(*args)


def exchange(x, axes):
    return lax.all_to_all(x, axes, split_axis=0, concat_axis=0, tiled=True)


def spread(x, axes, count):
    return exchange(jnp.broadcast_to(x[None], (count, *x.shape)), axes)


def body(ny, nx, zh, zl, patches, codes, support, block_shards, dictionary):
    rows, plen = patches.shape
    blocks = block_shards.shape[0]
    width = plen // nx
    nc = 2
    piece = SHARD // (ny * nc)
    sds = jax.ShapeDtypeStruct
    y, x, c = (lax.axis_index(a) for a in ("y", "x", "c"))
    ids = jnp.stack([y, x, c]).astype(jnp.int32)
    packed = call(
        pack_kernel,
        "ssvvv",
        tuple(sds((rows + 16, width), BF16) for _ in range(nx)),
        [],
        block_shards.T, ids, patches, codes.T, support.T,
    )
    held = [packed[0]]
    for j in range(1, nx):
        held.append(lax.ppermute(packed[j], "x", [(i, (i + j) % nx) for i in range(nx)]))
    names = jnp.concatenate([h[rows : rows + 1, 256 : 256 + 2 * blocks] for h in held], axis=1)
    own = lax.dynamic_slice(dictionary, ((y * nc + c) * piece, x * width), (piece, width))
    by_hi = spread(own, "zh", zh)
    by_z = spread(by_hi, "zl", zl).reshape(zh * zl, piece, width)
    extra = jnp.pad(names, ((0, piece - 1), (0, width - names.shape[1])))
    mine = spread(jnp.concatenate([by_z, extra[None]], axis=0), "y", ny)
    other = lax.ppermute(mine, "c", [(0, 1), (1, 0)])
    cut = 2 * blocks * nx
    shards = jnp.concatenate([mine[:, zh * zl, 0, :cut], other[:, zh * zl, 0, :cut]], axis=0)
    shards = shards.astype(jnp.int32).reshape(-1)
    common = (shards, ids, *held, mine, other)
    sizes = (ny, nx, zh, zl, plen)
    takes = "ss" + "v" * (nx + 2)
    grads = sds((nx, SLOTS, nx * rows), F32)
    first = call(
        lambda *r: refine_kernel(0, sizes, *r), takes, grads, [], *common
    )
    second, codes_1 = call(
        lambda *r: refine_kernel(1, sizes, *r),
        takes + "v",
        (grads, sds((SLOTS, nx * rows), F32)),
        [],
        *common,
        exchange(first, "x"),
    )
    home, msg, usage, codes_2 = call(
        lambda *r: refine_kernel(2, sizes, *r),
        takes + "vv",
        (
            sds((nx, rows, width), BF16),
            sds((ny * nc, nx, MSG, 128), BF16),
            sds((zh * zl, 128), F32),
            sds((SLOTS, rows), F32),
        ),
        [],
        *common,
        exchange(second, "x"),
        codes_1,
    )
    new_codes = codes_2.T
    got = exchange(msg, ("y", "c")).reshape(ny * nc * nx, MSG, 128)
    at_home = exchange(home, "x")
    to_owner = call(
        lambda *r: stats_kernel((ny, nx, zh, zl), *r),
        "ssvv",
        sds((zh * zl, MSG, 128), BF16),
        [pltpu.VMEM((zh * zl * SHARD, 128), F32)],
        shards, ids, got, usage, us=10,
    )
    to_owner, at_home = lax.optimization_barrier((to_owner, at_home))
    resid = jnp.transpose(at_home, (1, 0, 2)).reshape(rows, plen)
    final = call(
        total_kernel,
        "v",
        sds((ny * nx * nc, MSG, 128), BF16),
        [],
        exchange(to_owner, ("zh", "zl")),
    )
    new_dictionary = call(
        lambda *r: renew_kernel((ny, nx), *r),
        "vv",
        sds(dictionary.shape, BF16),
        [pltpu.VMEM(dictionary.shape, F32)],
        exchange(final, ("y", "x", "c")), dictionary,
    )
    return (new_dictionary, new_codes, resid)


def solution(mesh):
    fine = Mesh(mesh.devices.reshape(DP_SPLIT + GROUP_SPLIT), ("y", "x", "c", "zh", "zl"))
    row = P(("y", "x", "c", "zh", "zl"), None)
    shard = P(("zh", "zl"), None)
    return jax.shard_map(
        functools.partial(body, DP_SPLIT[0], DP_SPLIT[1], *GROUP_SPLIT),
        mesh=fine,
        in_specs=(row, row, row, row, shard),
        out_specs=(shard, row, row),
        check_vma=False,
    )
```

```python
import functools

import jax
import jax.numpy as jnp
from jax import lax
from jax.experimental import pallas as pl
from jax.experimental.pallas import tpu as pltpu
from jax.sharding import Mesh, PartitionSpec as P

F32 = jnp.float32
BF16 = jnp.bfloat16
NT = (((1,), (1,)), ((), ()))
VMEM_LIMIT = 56 * 1024 * 1024
DP_SPLIT = (4, 4, 2)
SHARD = 128
SLOTS = 8
MAIN = 64
MSG = 80


def pack_kernel(names_ref, ids_ref, x_ref, codes_ref, sup_ref, *outs):
    rows = x_ref.shape[0]
    width = outs[0].shape[1]
    count = len(outs)
    codes = codes_ref[...]
    first = codes.astype(BF16).astype(F32)
    rest = codes - first
    second = rest.astype(BF16).astype(F32)
    third = rest - second
    top = jnp.concatenate([first, second], axis=0).astype(BF16)
    low = jnp.concatenate([third, sup_ref[...].astype(F32)], axis=0).astype(BF16)
    lane = lax.broadcasted_iota(jnp.int32, (16, 128), 1)
    names = jnp.zeros((16, 128), jnp.int32)
    for b in range(names_ref.shape[1]):
        for h in range(2):
            names = jnp.where(lane == 2 * b + h, names_ref[h, b], names)
    names = names.astype(F32).astype(BF16)
    for j in range(count):
        start = pl.multiple_of(((ids_ref[1] + j) & (count - 1)) * width, 128)
        outs[j][:rows, :] = x_ref[:, pl.ds(start, width)]
        outs[j][rows : rows + 16, :128] = top
        outs[j][rows : rows + 16, 128:256] = low
        outs[j][rows : rows + 16, 256:384] = names
        for t in range(384, width, 128):
            outs[j][rows : rows + 16, t : t + 128] = jnp.zeros((16, 128), BF16)


def read_side(x_ref, rows):
    top = x_ref[rows : rows + 16, :128].astype(F32)
    low = x_ref[rows : rows + 16, 128:256].astype(F32)
    return top[:SLOTS] + top[SLOTS:] + low[:SLOTS], low[SLOTS:]


def atom_rows(core, piece):
    row = lax.broadcasted_iota(jnp.int32, (256, 128), 0)
    shift = piece.bit_length() - 1
    spot = row & 127
    other = spot >> 6
    half = spot & 63
    place = ((half >> shift) * 2 + (core ^ other)) * piece + (half & (piece - 1))
    return ((row & 128) + place).astype(F32)


def code_matrix(codes_t, sup_t, atoms):
    total = jnp.where(sup_t[0:1] == atoms, codes_t[0:1], 0.0)
    for k in range(1, SLOTS):
        total = total + jnp.where(sup_t[k : k + 1] == atoms, codes_t[k : k + 1], 0.0)
    return total


def pick(matrix, sup_t, atoms):
    return jnp.concatenate(
        [
            jnp.sum(jnp.where(sup_t[k : k + 1] == atoms, matrix, 0.0), axis=0, keepdims=True)
            for k in range(SLOTS)
        ],
        axis=0,
    )


def refine_kernel(step, sizes, shards_ref, ids_ref, *refs):
    ny, nx, plen = sizes
    x_refs, (mine_ref, other_ref), refs = refs[:nx], refs[nx : nx + 2], refs[nx + 2 :]
    height, width = x_refs[0].shape
    rows = height - 16
    piece = mine_ref.shape[2]
    blocks = rows // 32
    chunk = min(256, width)
    core = ids_ref[2]
    order = atom_rows(core, piece)
    if step == 0:
        (grad_out,) = refs
    elif step == 1:
        parts_ref, grad_out, codes_out = refs
    else:
        parts_ref, codes_ref, home_out, msg_out, usage_out, codes_out = refs
    low = lax.broadcasted_iota(jnp.int32, (MAIN, 128), 1) < 64
    for s in range(nx):
        source = (ids_ref[1] - s) & (nx - 1)
        at = pl.ds(pl.multiple_of(source * 128, 128), 128)
        mine = slice(s * 128, (s + 1) * 128)
        codes_t, sup_t = read_side(x_refs[s], rows)
        if step > 0:
            moved = parts_ref[0, :, at]
            for j in range(1, nx):
                moved = moved + parts_ref[j, :, at]
            moved = 1.5 * (moved / plen)
        if step == 1:
            codes_t = codes_t + moved
            codes_out[:, mine] = codes_t
        if step == 2:
            codes_t = codes_ref[:, mine] + moved
            if s == 0:
                codes_out[...] = codes_t
        upright = code_matrix(codes_t, sup_t, order)
        matrix = jnp.transpose(upright).astype(BF16)
        scores = []
        outs = [[] for _ in range(width // chunk)]
        for b in range(blocks):
            base = (ids_ref[0] * nx + s) * 2 * blocks + 2 * b
            at_a = shards_ref[base]
            at_b = shards_ref[base + 1]
            part = matrix[b * 32 : (b + 1) * 32]
            total = None
            for j in range(width // chunk):
                c0 = j * chunk
                atoms = jnp.concatenate(
                    [
                        ref[:, z, :, c0 : c0 + chunk].reshape(ny * piece, chunk)
                        for z in (at_a, at_b)
                        for ref in (mine_ref, other_ref)
                    ],
                    axis=0,
                )
                rebuilt = jnp.dot(part, atoms, preferred_element_type=F32)
                x = x_refs[s][b * 32 : (b + 1) * 32, c0 : c0 + chunk].astype(F32)
                resid = (x - rebuilt).astype(BF16)
                if step < 2:
                    score = lax.dot_general(resid, atoms, NT, preferred_element_type=F32)
                    total = score if total is None else total + score
                else:
                    outs[j].append(resid)
            scores.append(total)
        if step < 2:
            grad_t = pick(jnp.transpose(jnp.concatenate(scores, axis=0)), sup_t, order)
            for j in range(nx):
                grad_out[j, :, at] = grad_t
            continue
        merged_t = pick(upright.astype(BF16).astype(F32), sup_t, order)
        side_t = jnp.concatenate([merged_t, sup_t], axis=0).astype(BF16)
        for j in range(width // chunk):
            full = jnp.concatenate(outs[j], axis=0)
            home_out[source, :, j * chunk : (j + 1) * chunk] = full
            for t in range(chunk // 128):
                u = (j * chunk) // 128 + t
                tile = full[:, t * 128 : (t + 1) * 128].astype(F32)
                top, bottom = tile[:MAIN], tile[MAIN:]
                even = jnp.where(low, top, pltpu.roll(bottom, 64, 1))
                odd = jnp.where(low, pltpu.roll(top, 64, 1), bottom)
                msg_out[2 * u, source, :MAIN, :] = even.astype(BF16)
                msg_out[2 * u + 1, source, :MAIN, :] = odd.astype(BF16)
                msg_out[2 * u, source, MAIN:, :] = side_t
                msg_out[2 * u + 1, source, MAIN:, :] = side_t
        if s == 0:
            usage_out[...] = jnp.zeros_like(usage_out)
            plain = lax.broadcasted_iota(jnp.int32, (256, 128), 0).astype(F32)
            wide = code_matrix(codes_t, sup_t, plain).astype(BF16).astype(F32)
            wide = jnp.transpose(wide * wide)
            for b in range(blocks):
                base = (ids_ref[0] * nx + s) * 2 * blocks + 2 * b
                squares = jnp.sum(wide[b * 32 : (b + 1) * 32], axis=0, keepdims=True)
                usage_out[pl.ds(shards_ref[base], 1), :] += squares[:, :128]
                usage_out[pl.ds(shards_ref[base + 1], 1), :] += squares[:, 128:]


def stats_kernel(sizes, shards_ref, ids_ref, msg_ref, usage_ref, out_ref, acc_ref):
    ny, nx = sizes
    acc_ref[...] = jnp.zeros_like(acc_ref)
    atom = lax.broadcasted_iota(jnp.int32, (256, 128), 0).astype(F32)
    low = lax.broadcasted_iota(jnp.int32, (32, 128), 1) < 64
    low_all = lax.broadcasted_iota(jnp.int32, (128, 128), 1) < 64
    core = ids_ref[2]

    def one(q, carry):
        weights = msg_ref[q, MAIN : MAIN + 16, :].astype(F32)
        matrix = jnp.zeros((256, 128), F32)
        for k in range(SLOTS):
            matrix = jnp.where(
                weights[SLOTS + k : SLOTS + k + 1, :] == atom, weights[k : k + 1, :], matrix
            )
        matrix = matrix.astype(BF16)
        source = q // nx
        away = (ids_ref[1] - q) & (nx - 1)
        base = ((((source & 1) ^ core) * ny + (source >> 1)) * nx + away) * 8
        none = jnp.zeros((32, 128), F32)
        for pair in range(2):
            x = msg_ref[q, pair * 32 : pair * 32 + 32, :].astype(F32)
            parts = [none, none, none, none]
            parts[pair], parts[pair + 2] = jnp.where(low, x, 0.0), jnp.where(low, 0.0, x)
            wide = jnp.concatenate(parts, axis=0).astype(BF16)
            out = jnp.dot(matrix, wide, preferred_element_type=F32)
            for h in range(2):
                values = out[h * 128 : (h + 1) * 128, :]
                at0 = pl.multiple_of(shards_ref[base + pair * 2 + h] * 128, 128)
                at1 = pl.multiple_of(shards_ref[base + pair * 2 + 4 + h] * 128, 128)
                acc_ref[pl.ds(at0, 128), :] += jnp.where(low_all, values, 0.0)
                acc_ref[pl.ds(at1, 128), :] += jnp.where(low_all, 0.0, values)
        return carry

    lax.fori_loop(0, msg_ref.shape[0], one, 0, unroll=4)
    low = lax.broadcasted_iota(jnp.int32, (MAIN, 128), 1) < 64
    row = lax.broadcasted_iota(jnp.int32, (16, 128), 0)
    for s in range(out_ref.shape[0]):
        full = acc_ref[s * 128 : (s + 1) * 128, :]
        full = full + pltpu.roll(full, 64, 1)
        out_ref[s, :MAIN, :] = jnp.where(low, full[:MAIN], full[MAIN:]).astype(BF16)
        out_ref[s, MAIN:, :] = two_parts(usage_ref[s : s + 1, :], row)


def two_parts(used, row):
    high = used.astype(BF16).astype(F32)
    return jnp.where(row == 0, high, jnp.where(row == 1, used - high, 0.0)).astype(BF16)


def summed(parts_ref, at):
    total = parts_ref[(0,) + at].astype(F32)
    for z in range(1, parts_ref.shape[0]):
        total = total + parts_ref[(z,) + at].astype(F32)
    return total


def total_kernel(parts_ref, out_ref):
    total = summed(parts_ref, ())
    row = lax.broadcasted_iota(jnp.int32, (16, 128), 0)
    main = total[:MAIN].astype(BF16)
    side = two_parts(total[MAIN : MAIN + 1] + total[MAIN + 1 : MAIN + 2], row)
    for q in range(out_ref.shape[0]):
        out_ref[q, :MAIN, :] = main
        out_ref[q, MAIN:, :] = side


def renew_kernel(sizes, parts_ref, dict_ref, out_ref, moved_ref):
    ny, nx = sizes
    plen = dict_ref.shape[1]
    used = jnp.zeros((16, 128), F32)
    for q in range(parts_ref.shape[0]):
        used = used + parts_ref[q, MAIN:, :].astype(F32)
    column = jnp.transpose(jnp.broadcast_to(used[0:1, :] + used[1:2, :], (128, 128)))
    gain = 3.0 / (column + 1.0)
    low = lax.broadcasted_iota(jnp.int32, (MAIN, 128), 1) < 64
    squares = jnp.zeros((128, 128), F32)
    for t in range(plen // 128):
        q = ((t % ny) * nx + t // ny) * 2
        even = parts_ref[q, :MAIN, :].astype(F32)
        odd = parts_ref[q + 1, :MAIN, :].astype(F32)
        top = jnp.where(low, even, pltpu.roll(odd, 64, 1))
        bottom = jnp.where(low, pltpu.roll(even, 64, 1), odd)
        stats = jnp.concatenate([top, bottom], axis=0)
        moved = dict_ref[:, t * 128 : (t + 1) * 128].astype(F32) + gain * stats
        moved_ref[:, t * 128 : (t + 1) * 128] = moved
        squares = squares + moved * moved
    scale = lax.rsqrt(jnp.sum(squares, axis=1, keepdims=True) / plen + 1e-05)
    for t in range(plen // 128):
        out_ref[:, t * 128 : (t + 1) * 128] = (
            moved_ref[:, t * 128 : (t + 1) * 128] * scale
        ).astype(BF16)


def call(kernel, ins, outs, scratch, *args, us=1):
    spaces = {"v": pltpu.VMEM, "s": pltpu.SMEM}
    return pl.pallas_call(
        kernel,
        out_shape=outs,
        in_specs=[pl.BlockSpec(memory_space=spaces[i]) for i in ins],
        out_specs=jax.tree.map(lambda _: pl.BlockSpec(memory_space=pltpu.VMEM), outs),
        scratch_shapes=scratch,
        cost_estimate=pl.CostEstimate(
            flops=us * 10**9, bytes_accessed=us * 3 * 10**6, transcendentals=0
        ),
        compiler_params=pltpu.CompilerParams(vmem_limit_bytes=VMEM_LIMIT),
    )(*args)


def exchange(x, axes):
    return lax.all_to_all(x, axes, split_axis=0, concat_axis=0, tiled=True)


def spread(x, axes, count):
    return exchange(jnp.broadcast_to(x[None], (count, *x.shape)), axes)


def body(ny, nx, nz, patches, codes, support, block_shards, dictionary):
    rows, plen = patches.shape
    blocks = block_shards.shape[0]
    width = plen // nx
    nc = 2
    piece = SHARD // (ny * nc)
    sds = jax.ShapeDtypeStruct
    y, x, c = (lax.axis_index(a) for a in ("y", "x", "c"))
    ids = jnp.stack([y, x, c]).astype(jnp.int32)
    packed = call(
        pack_kernel,
        "ssvvv",
        tuple(sds((rows + 16, width), BF16) for _ in range(nx)),
        [],
        block_shards.T, ids, patches, codes.T, support.T,
    )
    held = [packed[0]]
    for j in range(1, nx):
        held.append(lax.ppermute(packed[j], "x", [(i, (i + j) % nx) for i in range(nx)]))
    names = jnp.concatenate([h[rows : rows + 1, 256 : 256 + 2 * blocks] for h in held], axis=1)
    own = lax.dynamic_slice(dictionary, ((y * nc + c) * piece, x * width), (piece, width))
    by_z = spread(own, "z", nz).reshape(nz, piece, width)
    extra = jnp.pad(names, ((0, piece - 1), (0, width - names.shape[1])))
    mine = spread(jnp.concatenate([by_z, extra[None]], axis=0), "y", ny)
    other = lax.ppermute(mine, "c", [(0, 1), (1, 0)])
    cut = 2 * blocks * nx
    shards = jnp.concatenate([mine[:, nz, 0, :cut], other[:, nz, 0, :cut]], axis=0)
    shards = shards.astype(jnp.int32).reshape(-1)
    common = (shards, ids, *held, mine, other)
    sizes = (ny, nx, plen)
    takes = "ss" + "v" * (nx + 2)
    grads = sds((nx, SLOTS, nx * rows), F32)
    first = call(
        lambda *r: refine_kernel(0, sizes, *r), takes, grads, [], *common
    )
    second, codes_1 = call(
        lambda *r: refine_kernel(1, sizes, *r),
        takes + "v",
        (grads, sds((SLOTS, nx * rows), F32)),
        [],
        *common,
        exchange(first, "x"),
    )
    home, msg, usage, codes_2 = call(
        lambda *r: refine_kernel(2, sizes, *r),
        takes + "vv",
        (
            sds((nx, rows, width), BF16),
            sds((ny * nc, nx, MSG, 128), BF16),
            sds((nz, 128), F32),
            sds((SLOTS, rows), F32),
        ),
        [],
        *common,
        exchange(second, "x"),
        codes_1,
    )
    new_codes = codes_2.T
    got = exchange(msg, ("y", "c")).reshape(ny * nc * nx, MSG, 128)
    at_home = exchange(home, "x")
    to_owner = call(
        lambda *r: stats_kernel((ny, nx), *r),
        "ssvv",
        sds((nz, MSG, 128), BF16),
        [pltpu.VMEM((nz * SHARD, 128), F32)],
        shards, ids, got, usage, us=10,
    )
    to_owner, at_home = lax.optimization_barrier((to_owner, at_home))
    resid = jnp.transpose(at_home, (1, 0, 2)).reshape(rows, plen)
    final = call(
        total_kernel,
        "v",
        sds((ny * nx * nc, MSG, 128), BF16),
        [],
        exchange(to_owner, "z"),
    )
    new_dictionary = call(
        lambda *r: renew_kernel((ny, nx), *r),
        "vv",
        sds(dictionary.shape, BF16),
        [pltpu.VMEM(dictionary.shape, F32)],
        exchange(final, ("y", "x", "c")), dictionary,
    )
    return (new_dictionary, new_codes, resid)


def solution(mesh):
    fine = Mesh(mesh.devices.reshape(DP_SPLIT + (-1,)), ("y", "x", "c", "z"))
    row = P(("y", "x", "c", "z"), None)
    shard = P("z", None)
    return jax.shard_map(
        functools.partial(body, DP_SPLIT[0], DP_SPLIT[1], mesh.shape["group"]),
        mesh=fine,
        in_specs=(row, row, row, row, shard),
        out_specs=(shard, row, row),
        check_vma=False,
    )
```

```python
import functools

import jax
import jax.numpy as jnp
from jax import lax
from jax.experimental import pallas as pl
from jax.experimental.pallas import tpu as pltpu
from jax.sharding import Mesh, PartitionSpec as P

F32 = jnp.float32
BF16 = jnp.bfloat16
NT = (((1,), (1,)), ((), ()))
VMEM_LIMIT = 16 * 1024 * 1024
DP_SPLIT = (4, 4, 2)
SHARD = 128
SLOTS = 8
MAIN = 64
MSG = 80


def pack_kernel(names_ref, ids_ref, x_ref, codes_ref, sup_ref, *outs):
    rows = x_ref.shape[0]
    width = outs[0].shape[1]
    count = len(outs)
    codes = codes_ref[...]
    first = codes.astype(BF16).astype(F32)
    rest = codes - first
    second = rest.astype(BF16).astype(F32)
    third = rest - second
    top = jnp.concatenate([first, second], axis=0).astype(BF16)
    low = jnp.concatenate([third, sup_ref[...].astype(F32)], axis=0).astype(BF16)
    lane = lax.broadcasted_iota(jnp.int32, (16, 128), 1)
    names = jnp.zeros((16, 128), jnp.int32)
    for b in range(names_ref.shape[1]):
        for h in range(2):
            names = jnp.where(lane == 2 * b + h, names_ref[h, b], names)
    names = names.astype(F32).astype(BF16)
    for j in range(count):
        start = pl.multiple_of(((ids_ref[1] + j) & (count - 1)) * width, 128)
        outs[j][:rows, :] = x_ref[:, pl.ds(start, width)]
        outs[j][rows : rows + 16, :128] = top
        outs[j][rows : rows + 16, 128:256] = low
        outs[j][rows : rows + 16, 256:384] = names
        for t in range(384, width, 128):
            outs[j][rows : rows + 16, t : t + 128] = jnp.zeros((16, 128), BF16)


def read_side(x_ref, rows):
    top = x_ref[rows : rows + 16, :128].astype(F32)
    low = x_ref[rows : rows + 16, 128:256].astype(F32)
    return top[:SLOTS] + top[SLOTS:] + low[:SLOTS], low[SLOTS:]


def atom_rows(core, piece):
    row = lax.broadcasted_iota(jnp.int32, (256, 128), 0)
    shift = piece.bit_length() - 1
    spot = row & 127
    other = spot >> 6
    half = spot & 63
    place = ((half >> shift) * 2 + (core ^ other)) * piece + (half & (piece - 1))
    return ((row & 128) + place).astype(F32)


def code_matrix(codes_t, sup_t, atoms):
    total = jnp.where(sup_t[0:1] == atoms, codes_t[0:1], 0.0)
    for k in range(1, SLOTS):
        total = total + jnp.where(sup_t[k : k + 1] == atoms, codes_t[k : k + 1], 0.0)
    return total


def pick(matrix, sup_t, atoms):
    return jnp.concatenate(
        [
            jnp.sum(jnp.where(sup_t[k : k + 1] == atoms, matrix, 0.0), axis=0, keepdims=True)
            for k in range(SLOTS)
        ],
        axis=0,
    )


def refine_kernel(step, sizes, shards_ref, ids_ref, *refs):
    ny, nx, plen = sizes
    x_refs, (mine_ref, other_ref), refs = refs[:nx], refs[nx : nx + 2], refs[nx + 2 :]
    height, width = x_refs[0].shape
    rows = height - 16
    piece = mine_ref.shape[2]
    blocks = rows // 32
    chunk = min(256, width)
    core = ids_ref[2]
    order = atom_rows(core, piece)
    if step == 0:
        (grad_out,) = refs
    elif step == 1:
        parts_ref, grad_out, codes_out = refs
    else:
        parts_ref, codes_ref, home_out, msg_out, usage_out, codes_out = refs
    low = lax.broadcasted_iota(jnp.int32, (MAIN, 128), 1) < 64
    for s in range(nx):
        source = (ids_ref[1] - s) & (nx - 1)
        at = pl.ds(pl.multiple_of(source * 128, 128), 128)
        mine = slice(s * 128, (s + 1) * 128)
        codes_t, sup_t = read_side(x_refs[s], rows)
        if step > 0:
            moved = parts_ref[0, :, at]
            for j in range(1, nx):
                moved = moved + parts_ref[j, :, at]
            moved = 1.5 * (moved / plen)
        if step == 1:
            codes_t = codes_t + moved
            codes_out[:, mine] = codes_t
        if step == 2:
            codes_t = codes_ref[:, mine] + moved
            if s == 0:
                codes_out[...] = codes_t
        upright = code_matrix(codes_t, sup_t, order)
        matrix = jnp.transpose(upright).astype(BF16)
        scores = []
        outs = [[] for _ in range(width // chunk)]
        for b in range(blocks):
            base = s * 2 * blocks + 2 * b
            at_a = shards_ref[base]
            at_b = shards_ref[base + 1]
            part = matrix[b * 32 : (b + 1) * 32]
            total = None
            for j in range(width // chunk):
                c0 = j * chunk
                atoms = jnp.concatenate(
                    [
                        ref[:, z, :, c0 : c0 + chunk].reshape(ny * piece, chunk)
                        for z in (at_a, at_b)
                        for ref in (mine_ref, other_ref)
                    ],
                    axis=0,
                )
                rebuilt = jnp.dot(part, atoms, preferred_element_type=F32)
                x = x_refs[s][b * 32 : (b + 1) * 32, c0 : c0 + chunk].astype(F32)
                resid = (x - rebuilt).astype(BF16)
                if step < 2:
                    score = lax.dot_general(resid, atoms, NT, preferred_element_type=F32)
                    total = score if total is None else total + score
                else:
                    outs[j].append(resid)
            scores.append(total)
        if step < 2:
            grad_t = pick(jnp.transpose(jnp.concatenate(scores, axis=0)), sup_t, order)
            for j in range(nx):
                grad_out[j, :, at] = grad_t
            continue
        merged_t = pick(upright.astype(BF16).astype(F32), sup_t, order)
        side_t = jnp.concatenate([merged_t, sup_t], axis=0).astype(BF16)
        for j in range(width // chunk):
            full = jnp.concatenate(outs[j], axis=0)
            home_out[source, :, j * chunk : (j + 1) * chunk] = full
            for t in range(chunk // 128):
                u = (j * chunk) // 128 + t
                tile = full[:, t * 128 : (t + 1) * 128].astype(F32)
                top, bottom = tile[:MAIN], tile[MAIN:]
                even = jnp.where(low, top, pltpu.roll(bottom, 64, 1))
                odd = jnp.where(low, pltpu.roll(top, 64, 1), bottom)
                msg_out[2 * u, source, :MAIN, :] = even.astype(BF16)
                msg_out[2 * u + 1, source, :MAIN, :] = odd.astype(BF16)
                msg_out[2 * u, source, MAIN:, :] = side_t
                msg_out[2 * u + 1, source, MAIN:, :] = side_t
        if s == 0:
            usage_out[...] = jnp.zeros_like(usage_out)
            plain = lax.broadcasted_iota(jnp.int32, (256, 128), 0).astype(F32)
            wide = code_matrix(codes_t, sup_t, plain).astype(BF16).astype(F32)
            wide = jnp.transpose(wide * wide)
            for b in range(blocks):
                base = s * 2 * blocks + 2 * b
                squares = jnp.sum(wide[b * 32 : (b + 1) * 32], axis=0, keepdims=True)
                usage_out[pl.ds(shards_ref[base], 1), :] += squares[:, :128]
                usage_out[pl.ds(shards_ref[base + 1], 1), :] += squares[:, 128:]


def stats_kernel(nx, shards_ref, ids_ref, msg_ref, usage_ref, out_ref, acc_ref):
    acc_ref[...] = jnp.zeros_like(acc_ref)
    atom = lax.broadcasted_iota(jnp.int32, (256, 128), 0).astype(F32)
    low = lax.broadcasted_iota(jnp.int32, (32, 128), 1) < 64
    low_all = lax.broadcasted_iota(jnp.int32, (128, 128), 1) < 64

    def one(q, carry):
        weights = msg_ref[q, MAIN : MAIN + 16, :].astype(F32)
        matrix = jnp.zeros((256, 128), F32)
        for k in range(SLOTS):
            matrix = jnp.where(
                weights[SLOTS + k : SLOTS + k + 1, :] == atom, weights[k : k + 1, :], matrix
            )
        matrix = matrix.astype(BF16)
        base = (q - q % nx + ((ids_ref[1] - q) & (nx - 1))) * 8
        none = jnp.zeros((32, 128), F32)
        for pair in range(2):
            x = msg_ref[q, pair * 32 : pair * 32 + 32, :].astype(F32)
            parts = [none, none, none, none]
            parts[pair], parts[pair + 2] = jnp.where(low, x, 0.0), jnp.where(low, 0.0, x)
            wide = jnp.concatenate(parts, axis=0).astype(BF16)
            out = jnp.dot(matrix, wide, preferred_element_type=F32)
            for h in range(2):
                values = out[h * 128 : (h + 1) * 128, :]
                at0 = pl.multiple_of(shards_ref[base + pair * 2 + h] * 128, 128)
                at1 = pl.multiple_of(shards_ref[base + pair * 2 + 4 + h] * 128, 128)
                acc_ref[pl.ds(at0, 128), :] += jnp.where(low_all, values, 0.0)
                acc_ref[pl.ds(at1, 128), :] += jnp.where(low_all, 0.0, values)
        return carry

    lax.fori_loop(0, msg_ref.shape[0], one, 0, unroll=4)
    low = lax.broadcasted_iota(jnp.int32, (MAIN, 128), 1) < 64
    row = lax.broadcasted_iota(jnp.int32, (16, 128), 0)
    for s in range(out_ref.shape[0]):
        full = acc_ref[s * 128 : (s + 1) * 128, :]
        full = full + pltpu.roll(full, 64, 1)
        out_ref[s, :MAIN, :] = jnp.where(low, full[:MAIN], full[MAIN:]).astype(BF16)
        out_ref[s, MAIN:, :] = two_parts(usage_ref[s : s + 1, :], row)


def two_parts(used, row):
    high = used.astype(BF16).astype(F32)
    return jnp.where(row == 0, high, jnp.where(row == 1, used - high, 0.0)).astype(BF16)


def summed(parts_ref, at):
    total = parts_ref[(0,) + at].astype(F32)
    for z in range(1, parts_ref.shape[0]):
        total = total + parts_ref[(z,) + at].astype(F32)
    return total


def total_kernel(parts_ref, out_ref):
    total = summed(parts_ref, ())
    row = lax.broadcasted_iota(jnp.int32, (16, 128), 0)
    main = total[:MAIN].astype(BF16)
    side = two_parts(total[MAIN : MAIN + 1] + total[MAIN + 1 : MAIN + 2], row)
    for q in range(out_ref.shape[0]):
        out_ref[q, :MAIN, :] = main
        out_ref[q, MAIN:, :] = side


def renew_kernel(sizes, parts_ref, dict_ref, out_ref, moved_ref):
    ny, nx = sizes
    plen = dict_ref.shape[1]
    used = jnp.zeros((16, 128), F32)
    for q in range(parts_ref.shape[0]):
        used = used + parts_ref[q, MAIN:, :].astype(F32)
    column = jnp.transpose(jnp.broadcast_to(used[0:1, :] + used[1:2, :], (128, 128)))
    gain = 3.0 / (column + 1.0)
    low = lax.broadcasted_iota(jnp.int32, (MAIN, 128), 1) < 64
    squares = jnp.zeros((128, 128), F32)
    for t in range(plen // 128):
        q = ((t % ny) * nx + t // ny) * 2
        even = parts_ref[q, :MAIN, :].astype(F32)
        odd = parts_ref[q + 1, :MAIN, :].astype(F32)
        top = jnp.where(low, even, pltpu.roll(odd, 64, 1))
        bottom = jnp.where(low, pltpu.roll(even, 64, 1), odd)
        stats = jnp.concatenate([top, bottom], axis=0)
        moved = dict_ref[:, t * 128 : (t + 1) * 128].astype(F32) + gain * stats
        moved_ref[:, t * 128 : (t + 1) * 128] = moved
        squares = squares + moved * moved
    scale = lax.rsqrt(jnp.sum(squares, axis=1, keepdims=True) / plen + 1e-05)
    for t in range(plen // 128):
        out_ref[:, t * 128 : (t + 1) * 128] = (
            moved_ref[:, t * 128 : (t + 1) * 128] * scale
        ).astype(BF16)


def call(kernel, ins, outs, scratch, *args, us=1):
    spaces = {"v": pltpu.VMEM, "s": pltpu.SMEM}
    return pl.pallas_call(
        kernel,
        out_shape=outs,
        in_specs=[pl.BlockSpec(memory_space=spaces[i]) for i in ins],
        out_specs=jax.tree.map(lambda _: pl.BlockSpec(memory_space=pltpu.VMEM), outs),
        scratch_shapes=scratch,
        cost_estimate=pl.CostEstimate(
            flops=us * 10**9, bytes_accessed=us * 3 * 10**6, transcendentals=0
        ),
        compiler_params=pltpu.CompilerParams(vmem_limit_bytes=VMEM_LIMIT),
    )(*args)


def exchange(x, axes):
    return lax.all_to_all(x, axes, split_axis=0, concat_axis=0, tiled=True)


def spread(x, axes, count):
    return exchange(jnp.broadcast_to(x[None], (count, *x.shape)), axes)


def body(ny, nx, nz, patches, codes, support, block_shards, dictionary):
    rows, plen = patches.shape
    blocks = block_shards.shape[0]
    width = plen // nx
    nc = 2
    piece = SHARD // (ny * nc)
    sds = jax.ShapeDtypeStruct
    y, x, c = (lax.axis_index(a) for a in ("y", "x", "c"))
    ids = jnp.stack([y, x, c]).astype(jnp.int32)
    packed = call(
        pack_kernel,
        "ssvvv",
        tuple(sds((rows + 16, width), BF16) for _ in range(nx)),
        [],
        block_shards.T, ids, patches, codes.T, support.T,
    )
    own = lax.dynamic_slice(dictionary, ((y * nc + c) * piece, x * width), (piece, width))
    by_z = spread(own, "z", nz).reshape(nz, piece, width)
    def ahead(sent, j):
        return lax.ppermute(sent, "x", [(i, (i + j) % nx) for i in range(nx)])

    by_z, near, *later = lax.optimization_barrier((by_z, ahead(packed[1], 1), *packed[2:]))
    mine = spread(by_z, "y", ny)
    held = [packed[0], near, *(ahead(sent, j + 2) for j, sent in enumerate(later))]
    mine, *held = lax.optimization_barrier((mine, *held))
    other = lax.ppermute(mine, "c", [(0, 1), (1, 0)])
    names = jnp.concatenate([h[rows : rows + 1, 256 : 256 + 2 * blocks] for h in held], axis=1)
    near_shards = names.astype(jnp.int32).reshape(-1)
    plane = spread(names, ("y", "c"), ny * nc)
    common = (near_shards, ids, *held, mine, other)
    sizes = (ny, nx, plen)
    takes = "ss" + "v" * (nx + 2)
    grads = sds((nx, SLOTS, nx * rows), F32)
    first = call(
        lambda *r: refine_kernel(0, sizes, *r), takes, grads, [], *common
    )
    first, plane = lax.optimization_barrier((first, plane))
    shards = plane.astype(jnp.int32).reshape(-1)
    second, codes_1 = call(
        lambda *r: refine_kernel(1, sizes, *r),
        takes + "v",
        (grads, sds((SLOTS, nx * rows), F32)),
        [],
        *common,
        exchange(first, "x"),
    )
    home, msg, usage, codes_2 = call(
        lambda *r: refine_kernel(2, sizes, *r),
        takes + "vv",
        (
            sds((nx, rows, width), BF16),
            sds((ny * nc, nx, MSG, 128), BF16),
            sds((nz, 128), F32),
            sds((SLOTS, rows), F32),
        ),
        [],
        *common,
        exchange(second, "x"),
        codes_1,
    )
    new_codes = codes_2.T
    got = exchange(msg, ("y", "c")).reshape(ny * nc * nx, MSG, 128)
    at_home = exchange(home, "x")
    to_owner = call(
        lambda *r: stats_kernel(nx, *r),
        "ssvv",
        sds((nz, MSG, 128), BF16),
        [pltpu.VMEM((nz * SHARD, 128), F32)],
        shards, ids, got, usage, us=10,
    )
    to_owner, at_home = lax.optimization_barrier((to_owner, at_home))
    resid = jnp.transpose(at_home, (1, 0, 2)).reshape(rows, plen)
    final = call(
        total_kernel,
        "v",
        sds((ny * nx * nc, MSG, 128), BF16),
        [],
        exchange(to_owner, "z"),
    )
    new_dictionary = call(
        lambda *r: renew_kernel((ny, nx), *r),
        "vv",
        sds(dictionary.shape, BF16),
        [pltpu.VMEM(dictionary.shape, F32)],
        exchange(final, ("y", "x", "c")), dictionary,
    )
    return (new_dictionary, new_codes, resid)


def solution(mesh):
    fine = Mesh(mesh.devices.reshape(DP_SPLIT + (-1,)), ("y", "x", "c", "z"))
    row = P(("y", "x", "c", "z"), None)
    shard = P("z", None)
    return jax.shard_map(
        functools.partial(body, DP_SPLIT[0], DP_SPLIT[1], mesh.shape["group"]),
        mesh=fine,
        in_specs=(row, row, row, row, shard),
        out_specs=(shard, row, row),
        check_vma=False,
    )
```

```python
import functools

import jax
import jax.numpy as jnp
from jax import lax
from jax.experimental import pallas as pl
from jax.experimental.pallas import tpu as pltpu
from jax.sharding import Mesh, PartitionSpec as P

F32 = jnp.float32
BF16 = jnp.bfloat16
NT = (((1,), (1,)), ((), ()))
VMEM_LIMIT = 16 * 1024 * 1024
DP_SPLIT = (4, 4, 2)
SHARD = 128
SLOTS = 8
MAIN = 64
MSG = 80


def pack_kernel(names_ref, ids_ref, x_ref, codes_ref, sup_ref, *outs):
    rows = x_ref.shape[0]
    width = outs[0].shape[1]
    count = len(outs)
    codes = codes_ref[...]
    first = codes.astype(BF16).astype(F32)
    rest = codes - first
    second = rest.astype(BF16).astype(F32)
    third = rest - second
    top = jnp.concatenate([first, second], axis=0).astype(BF16)
    low = jnp.concatenate([third, sup_ref[...].astype(F32)], axis=0).astype(BF16)
    lane = lax.broadcasted_iota(jnp.int32, (16, 128), 1)
    names = jnp.zeros((16, 128), jnp.int32)
    for b in range(names_ref.shape[1]):
        for h in range(2):
            names = jnp.where(lane == 2 * b + h, names_ref[h, b], names)
    names = names.astype(F32).astype(BF16)
    for j in range(count):
        start = pl.multiple_of(((ids_ref[1] + j) & (count - 1)) * width, 128)
        outs[j][:rows, :] = x_ref[:, pl.ds(start, width)]
        outs[j][rows : rows + 16, :128] = top
        outs[j][rows : rows + 16, 128:256] = low
        outs[j][rows : rows + 16, 256:384] = names
        for t in range(384, width, 128):
            outs[j][rows : rows + 16, t : t + 128] = jnp.zeros((16, 128), BF16)


def read_side(x_ref, rows):
    top = x_ref[rows : rows + 16, :128].astype(F32)
    low = x_ref[rows : rows + 16, 128:256].astype(F32)
    return top[:SLOTS] + top[SLOTS:] + low[:SLOTS], low[SLOTS:]


def atom_rows(core, piece):
    row = lax.broadcasted_iota(jnp.int32, (256, 128), 0)
    shift = piece.bit_length() - 1
    spot = row & 127
    other = spot >> 6
    half = spot & 63
    place = ((half >> shift) * 2 + (core ^ other)) * piece + (half & (piece - 1))
    return ((row & 128) + place).astype(F32)


def code_matrix(codes_t, sup_t, atoms):
    total = jnp.where(sup_t[0:1] == atoms, codes_t[0:1], 0.0)
    for k in range(1, SLOTS):
        total = total + jnp.where(sup_t[k : k + 1] == atoms, codes_t[k : k + 1], 0.0)
    return total


def pick(matrix, sup_t, atoms):
    return jnp.concatenate(
        [
            jnp.sum(jnp.where(sup_t[k : k + 1] == atoms, matrix, 0.0), axis=0, keepdims=True)
            for k in range(SLOTS)
        ],
        axis=0,
    )


def refine_kernel(step, sizes, shards_ref, ids_ref, *refs):
    ny, nx, plen = sizes
    x_refs, (mine_ref, other_ref), refs = refs[:nx], refs[nx : nx + 2], refs[nx + 2 :]
    height, width = x_refs[0].shape
    rows = height - 16
    piece = mine_ref.shape[2]
    blocks = rows // 32
    chunk = min(256, width)
    core = ids_ref[2]
    order = atom_rows(core, piece)
    if step == 0:
        (grad_out,) = refs
    elif step == 1:
        parts_ref, grad_out, codes_out = refs
    else:
        parts_ref, codes_ref, *home_outs, msg_out, usage_out, codes_out = refs
    low = lax.broadcasted_iota(jnp.int32, (MAIN, 128), 1) < 64
    for s in range(nx):
        source = (ids_ref[1] - s) & (nx - 1)
        at = pl.ds(pl.multiple_of(source * 128, 128), 128)
        mine = slice(s * 128, (s + 1) * 128)
        codes_t, sup_t = read_side(x_refs[s], rows)
        if step > 0:
            moved = parts_ref[0, :, at]
            for j in range(1, nx):
                moved = moved + parts_ref[j, :, at]
            moved = 1.5 * (moved / plen)
        if step == 1:
            codes_t = codes_t + moved
            codes_out[:, mine] = codes_t
        if step == 2:
            codes_t = codes_ref[:, mine] + moved
            if s == 0:
                codes_out[...] = codes_t
        upright = code_matrix(codes_t, sup_t, order)
        matrix = jnp.transpose(upright).astype(BF16)
        scores = []
        outs = [[] for _ in range(width // chunk)]
        for b in range(blocks):
            base = s * 2 * blocks + 2 * b
            at_a = shards_ref[base]
            at_b = shards_ref[base + 1]
            part = matrix[b * 32 : (b + 1) * 32]
            total = None
            for j in range(width // chunk):
                c0 = j * chunk
                atoms = jnp.concatenate(
                    [
                        ref[:, z, :, c0 : c0 + chunk].reshape(ny * piece, chunk)
                        for z in (at_a, at_b)
                        for ref in (mine_ref, other_ref)
                    ],
                    axis=0,
                )
                rebuilt = jnp.dot(part, atoms, preferred_element_type=F32)
                x = x_refs[s][b * 32 : (b + 1) * 32, c0 : c0 + chunk].astype(F32)
                resid = (x - rebuilt).astype(BF16)
                if step < 2:
                    score = lax.dot_general(resid, atoms, NT, preferred_element_type=F32)
                    total = score if total is None else total + score
                else:
                    outs[j].append(resid)
            scores.append(total)
        if step < 2:
            grad_t = pick(jnp.transpose(jnp.concatenate(scores, axis=0)), sup_t, order)
            for j in range(nx):
                grad_out[j, :, at] = grad_t
            continue
        merged_t = pick(upright.astype(BF16).astype(F32), sup_t, order)
        side_t = jnp.concatenate([merged_t, sup_t], axis=0).astype(BF16)
        for j in range(width // chunk):
            full = jnp.concatenate(outs[j], axis=0)
            home_outs[s][:, j * chunk : (j + 1) * chunk] = full
            for t in range(chunk // 128):
                u = (j * chunk) // 128 + t
                tile = full[:, t * 128 : (t + 1) * 128].astype(F32)
                top, bottom = tile[:MAIN], tile[MAIN:]
                even = jnp.where(low, top, pltpu.roll(bottom, 64, 1))
                odd = jnp.where(low, pltpu.roll(top, 64, 1), bottom)
                msg_out[2 * u, source, :MAIN, :] = even.astype(BF16)
                msg_out[2 * u + 1, source, :MAIN, :] = odd.astype(BF16)
                msg_out[2 * u, source, MAIN:, :] = side_t
                msg_out[2 * u + 1, source, MAIN:, :] = side_t
        if s == 0:
            usage_out[...] = jnp.zeros_like(usage_out)
            plain = lax.broadcasted_iota(jnp.int32, (256, 128), 0).astype(F32)
            wide = code_matrix(codes_t, sup_t, plain).astype(BF16).astype(F32)
            wide = jnp.transpose(wide * wide)
            for b in range(blocks):
                base = s * 2 * blocks + 2 * b
                squares = jnp.sum(wide[b * 32 : (b + 1) * 32], axis=0, keepdims=True)
                usage_out[pl.ds(shards_ref[base], 1), :] += squares[:, :128]
                usage_out[pl.ds(shards_ref[base + 1], 1), :] += squares[:, 128:]


def stats_kernel(nx, shards_ref, ids_ref, msg_ref, usage_ref, out_ref, acc_ref):
    acc_ref[...] = jnp.zeros_like(acc_ref)
    atom = lax.broadcasted_iota(jnp.int32, (256, 128), 0).astype(F32)
    low = lax.broadcasted_iota(jnp.int32, (32, 128), 1) < 64
    low_all = lax.broadcasted_iota(jnp.int32, (128, 128), 1) < 64

    def one(q, carry):
        weights = msg_ref[q, MAIN : MAIN + 16, :].astype(F32)
        matrix = jnp.zeros((256, 128), F32)
        for k in range(SLOTS):
            matrix = jnp.where(
                weights[SLOTS + k : SLOTS + k + 1, :] == atom, weights[k : k + 1, :], matrix
            )
        matrix = matrix.astype(BF16)
        base = (q - q % nx + ((ids_ref[1] - q) & (nx - 1))) * 8
        none = jnp.zeros((32, 128), F32)
        for pair in range(2):
            x = msg_ref[q, pair * 32 : pair * 32 + 32, :].astype(F32)
            parts = [none, none, none, none]
            parts[pair], parts[pair + 2] = jnp.where(low, x, 0.0), jnp.where(low, 0.0, x)
            wide = jnp.concatenate(parts, axis=0).astype(BF16)
            out = jnp.dot(matrix, wide, preferred_element_type=F32)
            for h in range(2):
                values = out[h * 128 : (h + 1) * 128, :]
                at0 = pl.multiple_of(shards_ref[base + pair * 2 + h] * 128, 128)
                at1 = pl.multiple_of(shards_ref[base + pair * 2 + 4 + h] * 128, 128)
                acc_ref[pl.ds(at0, 128), :] += jnp.where(low_all, values, 0.0)
                acc_ref[pl.ds(at1, 128), :] += jnp.where(low_all, 0.0, values)
        return carry

    lax.fori_loop(0, msg_ref.shape[0], one, 0, unroll=4)
    low = lax.broadcasted_iota(jnp.int32, (MAIN, 128), 1) < 64
    row = lax.broadcasted_iota(jnp.int32, (16, 128), 0)
    for s in range(out_ref.shape[0]):
        full = acc_ref[s * 128 : (s + 1) * 128, :]
        full = full + pltpu.roll(full, 64, 1)
        out_ref[s, :MAIN, :] = jnp.where(low, full[:MAIN], full[MAIN:]).astype(BF16)
        out_ref[s, MAIN:, :] = two_parts(usage_ref[s : s + 1, :], row)


def two_parts(used, row):
    high = used.astype(BF16).astype(F32)
    return jnp.where(row == 0, high, jnp.where(row == 1, used - high, 0.0)).astype(BF16)


def summed(parts_ref, at):
    total = parts_ref[(0,) + at].astype(F32)
    for z in range(1, parts_ref.shape[0]):
        total = total + parts_ref[(z,) + at].astype(F32)
    return total


def total_kernel(parts_ref, out_ref):
    total = summed(parts_ref, ())
    row = lax.broadcasted_iota(jnp.int32, (16, 128), 0)
    main = total[:MAIN].astype(BF16)
    side = two_parts(total[MAIN : MAIN + 1] + total[MAIN + 1 : MAIN + 2], row)
    for q in range(out_ref.shape[0]):
        out_ref[q, :MAIN, :] = main
        out_ref[q, MAIN:, :] = side


def home_kernel(ids_ref, *refs):
    *parts, out_ref = refs
    width = parts[0].shape[1]
    for j, part in enumerate(parts):
        start = pl.multiple_of(((ids_ref[1] + j) & (len(parts) - 1)) * width, 128)
        out_ref[:, pl.ds(start, width)] = part[...]


def renew_kernel(sizes, parts_ref, dict_ref, out_ref, moved_ref):
    ny, nx = sizes
    plen = dict_ref.shape[1]
    used = jnp.zeros((16, 128), F32)
    for q in range(parts_ref.shape[0]):
        used = used + parts_ref[q, MAIN:, :].astype(F32)
    column = jnp.transpose(jnp.broadcast_to(used[0:1, :] + used[1:2, :], (128, 128)))
    gain = 3.0 / (column + 1.0)
    low = lax.broadcasted_iota(jnp.int32, (MAIN, 128), 1) < 64
    squares = jnp.zeros((128, 128), F32)
    for t in range(plen // 128):
        q = ((t % ny) * nx + t // ny) * 2
        even = parts_ref[q, :MAIN, :].astype(F32)
        odd = parts_ref[q + 1, :MAIN, :].astype(F32)
        top = jnp.where(low, even, pltpu.roll(odd, 64, 1))
        bottom = jnp.where(low, pltpu.roll(even, 64, 1), odd)
        stats = jnp.concatenate([top, bottom], axis=0)
        moved = dict_ref[:, t * 128 : (t + 1) * 128].astype(F32) + gain * stats
        moved_ref[:, t * 128 : (t + 1) * 128] = moved
        squares = squares + moved * moved
    scale = lax.rsqrt(jnp.sum(squares, axis=1, keepdims=True) / plen + 1e-05)
    for t in range(plen // 128):
        out_ref[:, t * 128 : (t + 1) * 128] = (
            moved_ref[:, t * 128 : (t + 1) * 128] * scale
        ).astype(BF16)


def call(kernel, ins, outs, scratch, *args, us=1):
    spaces = {"v": pltpu.VMEM, "s": pltpu.SMEM}
    return pl.pallas_call(
        kernel,
        out_shape=outs,
        in_specs=[pl.BlockSpec(memory_space=spaces[i]) for i in ins],
        out_specs=jax.tree.map(lambda _: pl.BlockSpec(memory_space=pltpu.VMEM), outs),
        scratch_shapes=scratch,
        cost_estimate=pl.CostEstimate(
            flops=us * 10**9, bytes_accessed=us * 3 * 10**6, transcendentals=0
        ),
        compiler_params=pltpu.CompilerParams(vmem_limit_bytes=VMEM_LIMIT),
    )(*args)


def exchange(x, axes):
    return lax.all_to_all(x, axes, split_axis=0, concat_axis=0, tiled=True)


def spread(x, axes, count):
    return exchange(jnp.broadcast_to(x[None], (count, *x.shape)), axes)


def body(ny, nx, nz, patches, codes, support, block_shards, dictionary):
    rows, plen = patches.shape
    blocks = block_shards.shape[0]
    width = plen // nx
    nc = 2
    piece = SHARD // (ny * nc)
    sds = jax.ShapeDtypeStruct
    y, x, c = (lax.axis_index(a) for a in ("y", "x", "c"))
    ids = jnp.stack([y, x, c]).astype(jnp.int32)
    packed = call(
        pack_kernel,
        "ssvvv",
        tuple(sds((rows + 16, width), BF16) for _ in range(nx)),
        [],
        block_shards.T, ids, patches, codes.T, support.T,
    )
    own = lax.dynamic_slice(dictionary, ((y * nc + c) * piece, x * width), (piece, width))
    by_z = spread(own, "z", nz).reshape(nz, piece, width)
    def ahead(sent, j):
        return lax.ppermute(sent, "x", [(i, (i + j) % nx) for i in range(nx)])

    held = [packed[0]] + [None if j == nx // 2 else ahead(packed[j], j) for j in range(1, nx)]
    by_z, far, *near = lax.optimization_barrier(
        (by_z, packed[nx // 2], *(h for h in held[1:] if h is not None))
    )
    mine = spread(by_z, "y", ny)
    near.insert(nx // 2 - 1, ahead(far, nx // 2))
    held = [packed[0], *near]
    mine, *held = lax.optimization_barrier((mine, *held))
    other = lax.ppermute(mine, "c", [(0, 1), (1, 0)])
    names = jnp.concatenate([h[rows : rows + 1, 256 : 256 + 2 * blocks] for h in held], axis=1)
    near_shards = names.astype(jnp.int32).reshape(-1)
    plane = spread(names, ("y", "c"), ny * nc)
    common = (near_shards, ids, *held, mine, other)
    sizes = (ny, nx, plen)
    takes = "ss" + "v" * (nx + 2)
    grads = sds((nx, SLOTS, nx * rows), F32)
    first = call(
        lambda *r: refine_kernel(0, sizes, *r), takes, grads, [], *common
    )
    first, plane = lax.optimization_barrier((first, plane))
    shards = plane.astype(jnp.int32).reshape(-1)
    second, codes_1 = call(
        lambda *r: refine_kernel(1, sizes, *r),
        takes + "v",
        (grads, sds((SLOTS, nx * rows), F32)),
        [],
        *common,
        exchange(first, "x"),
    )
    *home, msg, usage, codes_2 = call(
        lambda *r: refine_kernel(2, sizes, *r),
        takes + "vv",
        (
            *(sds((rows, width), BF16) for _ in range(nx)),
            sds((ny * nc, nx, MSG, 128), BF16),
            sds((nz, 128), F32),
            sds((SLOTS, rows), F32),
        ),
        [],
        *common,
        exchange(second, "x"),
        codes_1,
    )
    new_codes = codes_2.T
    got = exchange(msg, ("y", "c")).reshape(ny * nc * nx, MSG, 128)
    to_owner = call(
        lambda *r: stats_kernel(nx, *r),
        "ssvv",
        sds((nz, MSG, 128), BF16),
        [pltpu.VMEM((nz * SHARD, 128), F32)],
        shards, ids, got, usage, us=10,
    )
    to_owner, *home = lax.optimization_barrier((to_owner, *home))
    at_owner = exchange(to_owner, "z")
    home = [home[0]] + [
        lax.ppermute(home[j], "x", [(i, (i - j) % nx) for i in range(nx)]) for j in range(1, nx)
    ]
    at_owner, *home = lax.optimization_barrier((at_owner, *home))
    final = call(total_kernel, "v", sds((ny * nx * nc, MSG, 128), BF16), [], at_owner)
    resid = call(home_kernel, "s" + "v" * nx, sds((rows, plen), BF16), [], ids, *home)
    new_dictionary = call(
        lambda *r: renew_kernel((ny, nx), *r),
        "vv",
        sds(dictionary.shape, BF16),
        [pltpu.VMEM(dictionary.shape, F32)],
        exchange(final, ("y", "x", "c")), dictionary,
    )
    return (new_dictionary, new_codes, resid)


def solution(mesh):
    fine = Mesh(mesh.devices.reshape(DP_SPLIT + (-1,)), ("y", "x", "c", "z"))
    row = P(("y", "x", "c", "z"), None)
    shard = P("z", None)
    return jax.shard_map(
        functools.partial(body, DP_SPLIT[0], DP_SPLIT[1], mesh.shape["group"]),
        mesh=fine,
        in_specs=(row, row, row, row, shard),
        out_specs=(shard, row, row),
        check_vma=False,
    )
```

```python
import functools

import jax
import jax.numpy as jnp
from jax import lax
from jax.experimental import pallas as pl
from jax.experimental.pallas import tpu as pltpu
from jax.sharding import Mesh, PartitionSpec as P

F32 = jnp.float32
BF16 = jnp.bfloat16
NT = (((1,), (1,)), ((), ()))
VMEM_LIMIT = 16 * 1024 * 1024
DP_SPLIT = (4, 4, 2)
SHARD = 128
SLOTS = 8
MAIN = 64
MSG = 80


def pack_kernel(names_ref, ids_ref, x_ref, codes_ref, sup_ref, *outs):
    rows = x_ref.shape[0]
    width = outs[0].shape[1]
    count = len(outs)
    codes = codes_ref[...]
    first = codes.astype(BF16).astype(F32)
    rest = codes - first
    second = rest.astype(BF16).astype(F32)
    third = rest - second
    top = jnp.concatenate([first, second], axis=0).astype(BF16)
    low = jnp.concatenate([third, sup_ref[...].astype(F32)], axis=0).astype(BF16)
    lane = lax.broadcasted_iota(jnp.int32, (16, 128), 1)
    names = jnp.zeros((16, 128), jnp.int32)
    for b in range(names_ref.shape[1]):
        for h in range(2):
            names = jnp.where(lane == 2 * b + h, names_ref[h, b], names)
    names = names.astype(F32).astype(BF16)
    for j in range(count):
        start = pl.multiple_of(((ids_ref[1] + j) & (count - 1)) * width, 128)
        outs[j][:rows, :] = x_ref[:, pl.ds(start, width)]
        outs[j][rows : rows + 16, :128] = top
        outs[j][rows : rows + 16, 128:256] = low
        outs[j][rows : rows + 16, 256:384] = names
        for t in range(384, width, 128):
            outs[j][rows : rows + 16, t : t + 128] = jnp.zeros((16, 128), BF16)


def read_side(x_ref, rows):
    top = x_ref[rows : rows + 16, :128].astype(F32)
    low = x_ref[rows : rows + 16, 128:256].astype(F32)
    return top[:SLOTS] + top[SLOTS:] + low[:SLOTS], low[SLOTS:]


def atom_rows(core, piece):
    row = lax.broadcasted_iota(jnp.int32, (256, 128), 0)
    shift = piece.bit_length() - 1
    spot = row & 127
    other = spot >> 6
    half = spot & 63
    place = ((half >> shift) * 2 + (core ^ other)) * piece + (half & (piece - 1))
    return ((row & 128) + place).astype(F32)


def code_matrix(codes_t, sup_t, atoms):
    total = jnp.where(sup_t[0:1] == atoms, codes_t[0:1], 0.0)
    for k in range(1, SLOTS):
        total = total + jnp.where(sup_t[k : k + 1] == atoms, codes_t[k : k + 1], 0.0)
    return total


def pick(matrix, sup_t, atoms):
    return jnp.concatenate(
        [
            jnp.sum(jnp.where(sup_t[k : k + 1] == atoms, matrix, 0.0), axis=0, keepdims=True)
            for k in range(SLOTS)
        ],
        axis=0,
    )


def refine_kernel(step, sizes, shards_ref, ids_ref, *refs):
    ny, nx, plen = sizes
    x_refs, (mine_ref, other_ref), refs = refs[:nx], refs[nx : nx + 2], refs[nx + 2 :]
    height, width = x_refs[0].shape
    rows = height - 16
    piece = mine_ref.shape[2]
    blocks = rows // 32
    chunk = min(256, width)
    core = ids_ref[2]
    order = atom_rows(core, piece)
    if step == 0:
        (grad_out,) = refs
        last = mine_ref.shape[1] - 1
        names = [ref[j, last].astype(F32)[0:1] for ref in (mine_ref, other_ref) for j in range(ny)]
        names = jnp.concatenate(names, axis=0)
        for j in range(nx):
            for t in range(0, nx * rows, width):
                grad_out[j, SLOTS:, t : t + width] = names
    elif step == 1:
        parts_ref, grad_out, codes_out = refs
    else:
        parts_ref, codes_ref, *home_outs, msg_out, usage_out, codes_out = refs
    low = lax.broadcasted_iota(jnp.int32, (MAIN, 128), 1) < 64
    for s in range(nx):
        source = (ids_ref[1] - s) & (nx - 1)
        at = pl.ds(pl.multiple_of(source * 128, 128), 128)
        mine = slice(s * 128, (s + 1) * 128)
        codes_t, sup_t = read_side(x_refs[s], rows)
        if step > 0:
            moved = parts_ref[0, :SLOTS, at]
            for j in range(1, nx):
                moved = moved + parts_ref[j, :SLOTS, at]
            moved = 1.5 * (moved / plen)
        if step == 1:
            codes_t = codes_t + moved
            codes_out[:, mine] = codes_t
        if step == 2:
            codes_t = codes_ref[:, mine] + moved
            if s == 0:
                codes_out[...] = codes_t
        upright = code_matrix(codes_t, sup_t, order)
        matrix = jnp.transpose(upright).astype(BF16)
        scores = []
        outs = [[] for _ in range(width // chunk)]
        for b in range(blocks):
            base = s * 2 * blocks + 2 * b
            at_a = shards_ref[base]
            at_b = shards_ref[base + 1]
            part = matrix[b * 32 : (b + 1) * 32]
            total = None
            for j in range(width // chunk):
                c0 = j * chunk
                atoms = jnp.concatenate(
                    [
                        ref[:, z, :, c0 : c0 + chunk].reshape(ny * piece, chunk)
                        for z in (at_a, at_b)
                        for ref in (mine_ref, other_ref)
                    ],
                    axis=0,
                )
                rebuilt = jnp.dot(part, atoms, preferred_element_type=F32)
                x = x_refs[s][b * 32 : (b + 1) * 32, c0 : c0 + chunk].astype(F32)
                resid = (x - rebuilt).astype(BF16)
                if step < 2:
                    score = lax.dot_general(resid, atoms, NT, preferred_element_type=F32)
                    total = score if total is None else total + score
                else:
                    outs[j].append(resid)
            scores.append(total)
        if step < 2:
            grad_t = pick(jnp.transpose(jnp.concatenate(scores, axis=0)), sup_t, order)
            for j in range(nx):
                grad_out[j, :SLOTS, at] = grad_t
            continue
        merged_t = pick(upright.astype(BF16).astype(F32), sup_t, order)
        side_t = jnp.concatenate([merged_t, sup_t], axis=0).astype(BF16)
        for j in range(width // chunk):
            full = jnp.concatenate(outs[j], axis=0)
            home_outs[s][:, j * chunk : (j + 1) * chunk] = full
            for t in range(chunk // 128):
                u = (j * chunk) // 128 + t
                tile = full[:, t * 128 : (t + 1) * 128].astype(F32)
                top, bottom = tile[:MAIN], tile[MAIN:]
                even = jnp.where(low, top, pltpu.roll(bottom, 64, 1))
                odd = jnp.where(low, pltpu.roll(top, 64, 1), bottom)
                msg_out[2 * u, source, :MAIN, :] = even.astype(BF16)
                msg_out[2 * u + 1, source, :MAIN, :] = odd.astype(BF16)
                msg_out[2 * u, source, MAIN:, :] = side_t
                msg_out[2 * u + 1, source, MAIN:, :] = side_t
        if s == 0:
            usage_out[...] = jnp.zeros_like(usage_out)
            plain = lax.broadcasted_iota(jnp.int32, (256, 128), 0).astype(F32)
            wide = code_matrix(codes_t, sup_t, plain).astype(BF16).astype(F32)
            wide = jnp.transpose(wide * wide)
            for b in range(blocks):
                base = s * 2 * blocks + 2 * b
                squares = jnp.sum(wide[b * 32 : (b + 1) * 32], axis=0, keepdims=True)
                usage_out[pl.ds(shards_ref[base], 1), :] += squares[:, :128]
                usage_out[pl.ds(shards_ref[base + 1], 1), :] += squares[:, 128:]


def stats_kernel(ny, nx, shards_ref, ids_ref, msg_ref, usage_ref, out_ref, acc_ref):
    acc_ref[...] = jnp.zeros_like(acc_ref)
    atom = lax.broadcasted_iota(jnp.int32, (256, 128), 0).astype(F32).astype(BF16)
    low = lax.broadcasted_iota(jnp.int32, (32, 128), 1) < 64
    low_all = lax.broadcasted_iota(jnp.int32, (128, 128), 1) < 64

    def one(q, carry):
        weights = msg_ref[q, MAIN : MAIN + 16, :]
        matrix = jnp.zeros((256, 128), BF16)
        for k in range(SLOTS):
            matrix = jnp.where(
                weights[SLOTS + k : SLOTS + k + 1, :] == atom, weights[k : k + 1, :], matrix
            )
        source = q // nx
        base = ((q % nx * 2 + ((source & 1) ^ ids_ref[2])) * ny + (source >> 1)) * 8
        none = jnp.zeros((32, 128), F32)
        for pair in range(2):
            x = msg_ref[q, pair * 32 : pair * 32 + 32, :].astype(F32)
            parts = [none, none, none, none]
            parts[pair], parts[pair + 2] = jnp.where(low, x, 0.0), jnp.where(low, 0.0, x)
            wide = jnp.concatenate(parts, axis=0).astype(BF16)
            out = jnp.dot(matrix, wide, preferred_element_type=F32)
            for h in range(2):
                values = out[h * 128 : (h + 1) * 128, :]
                at0 = pl.multiple_of(shards_ref[base + pair * 2 + h] * 128, 128)
                at1 = pl.multiple_of(shards_ref[base + pair * 2 + 4 + h] * 128, 128)
                acc_ref[pl.ds(at0, 128), :] += jnp.where(low_all, values, 0.0)
                acc_ref[pl.ds(at1, 128), :] += jnp.where(low_all, 0.0, values)
        return carry

    lax.fori_loop(0, msg_ref.shape[0], one, 0, unroll=4)
    low = lax.broadcasted_iota(jnp.int32, (MAIN, 128), 1) < 64
    row = lax.broadcasted_iota(jnp.int32, (16, 128), 0)
    for s in range(out_ref.shape[0]):
        full = acc_ref[s * 128 : (s + 1) * 128, :]
        full = full + pltpu.roll(full, 64, 1)
        out_ref[s, :MAIN, :] = jnp.where(low, full[:MAIN], full[MAIN:]).astype(BF16)
        out_ref[s, MAIN:, :] = two_parts(usage_ref[s : s + 1, :], row)


def two_parts(used, row):
    high = used.astype(BF16).astype(F32)
    return jnp.where(row == 0, high, jnp.where(row == 1, used - high, 0.0)).astype(BF16)


def summed(parts_ref, at):
    total = parts_ref[(0,) + at].astype(F32)
    for z in range(1, parts_ref.shape[0]):
        total = total + parts_ref[(z,) + at].astype(F32)
    return total


def total_kernel(parts_ref, out_ref):
    total = summed(parts_ref, ())
    row = lax.broadcasted_iota(jnp.int32, (16, 128), 0)
    main = total[:MAIN].astype(BF16)
    side = two_parts(total[MAIN : MAIN + 1] + total[MAIN + 1 : MAIN + 2], row)
    for q in range(out_ref.shape[0]):
        out_ref[q, :MAIN, :] = main
        out_ref[q, MAIN:, :] = side


def home_kernel(ids_ref, *refs):
    *parts, out_ref = refs
    width = parts[0].shape[1]
    for j, part in enumerate(parts):
        start = pl.multiple_of(((ids_ref[1] + j) & (len(parts) - 1)) * width, 128)
        out_ref[:, pl.ds(start, width)] = part[...]


def renew_kernel(sizes, parts_ref, dict_ref, out_ref, moved_ref):
    ny, nx = sizes
    plen = dict_ref.shape[1]
    used = jnp.zeros((16, 128), F32)
    for q in range(parts_ref.shape[0]):
        used = used + parts_ref[q, MAIN:, :].astype(F32)
    column = jnp.transpose(jnp.broadcast_to(used[0:1, :] + used[1:2, :], (128, 128)))
    gain = 3.0 / (column + 1.0)
    low = lax.broadcasted_iota(jnp.int32, (MAIN, 128), 1) < 64
    squares = jnp.zeros((128, 128), F32)
    for t in range(plen // 128):
        q = ((t % ny) * nx + t // ny) * 2
        even = parts_ref[q, :MAIN, :].astype(F32)
        odd = parts_ref[q + 1, :MAIN, :].astype(F32)
        top = jnp.where(low, even, pltpu.roll(odd, 64, 1))
        bottom = jnp.where(low, pltpu.roll(even, 64, 1), odd)
        stats = jnp.concatenate([top, bottom], axis=0)
        moved = dict_ref[:, t * 128 : (t + 1) * 128].astype(F32) + gain * stats
        moved_ref[:, t * 128 : (t + 1) * 128] = moved
        squares = squares + moved * moved
    scale = lax.rsqrt(jnp.sum(squares, axis=1, keepdims=True) / plen + 1e-05)
    for t in range(plen // 128):
        out_ref[:, t * 128 : (t + 1) * 128] = (
            moved_ref[:, t * 128 : (t + 1) * 128] * scale
        ).astype(BF16)


def call(kernel, ins, outs, scratch, *args, us=1):
    spaces = {"v": pltpu.VMEM, "s": pltpu.SMEM}
    return pl.pallas_call(
        kernel,
        out_shape=outs,
        in_specs=[pl.BlockSpec(memory_space=spaces[i]) for i in ins],
        out_specs=jax.tree.map(lambda _: pl.BlockSpec(memory_space=pltpu.VMEM), outs),
        scratch_shapes=scratch,
        cost_estimate=pl.CostEstimate(
            flops=us * 10**9, bytes_accessed=us * 3 * 10**6, transcendentals=0
        ),
        compiler_params=pltpu.CompilerParams(vmem_limit_bytes=VMEM_LIMIT),
    )(*args)


def exchange(x, axes):
    return lax.all_to_all(x, axes, split_axis=0, concat_axis=0, tiled=True)


def spread(x, axes, count):
    return exchange(jnp.broadcast_to(x[None], (count, *x.shape)), axes)


def body(ny, nx, nz, patches, codes, support, block_shards, dictionary):
    rows, plen = patches.shape
    blocks = block_shards.shape[0]
    width = plen // nx
    nc = 2
    piece = SHARD // (ny * nc)
    sds = jax.ShapeDtypeStruct
    y, x, c = (lax.axis_index(a) for a in ("y", "x", "c"))
    ids = jnp.stack([y, x, c]).astype(jnp.int32)
    packed = call(
        pack_kernel,
        "ssvvv",
        tuple(sds((rows + 16, width), BF16) for _ in range(nx)),
        [],
        block_shards.T, ids, patches, codes.T, support.T,
    )
    own = lax.dynamic_slice(dictionary, ((y * nc + c) * piece, x * width), (piece, width))
    by_z = spread(own, "z", nz).reshape(nz, piece, width)
    def ahead(sent, j):
        return lax.ppermute(sent, "x", [(i, (i + j) % nx) for i in range(nx)])

    held = [packed[0]] + [None if j == nx // 2 else ahead(packed[j], j) for j in range(1, nx)]
    by_z, far, *near = lax.optimization_barrier(
        (by_z, packed[nx // 2], *(h for h in held[1:] if h is not None))
    )
    own_names = jnp.pad(
        block_shards.reshape(1, 1, -1).astype(BF16),
        ((0, 0), (0, piece - 1), (0, width - 2 * blocks)),
    )
    mine = spread(jnp.concatenate([by_z, own_names], axis=0), "y", ny)
    near.insert(nx // 2 - 1, ahead(far, nx // 2))
    held = [packed[0], *near]
    mine, *held = lax.optimization_barrier((mine, *held))
    other = lax.ppermute(mine, "c", [(0, 1), (1, 0)])
    names = jnp.concatenate([h[rows : rows + 1, 256 : 256 + 2 * blocks] for h in held], axis=1)
    near_shards = names.astype(jnp.int32).reshape(-1)
    common = (near_shards, ids, *held, mine, other)
    sizes = (ny, nx, plen)
    takes = "ss" + "v" * (nx + 2)
    grads = sds((nx, SLOTS, nx * rows), F32)
    first = call(
        lambda *r: refine_kernel(0, sizes, *r),
        takes,
        sds((nx, SLOTS + ny * nc, nx * rows), F32),
        [],
        *common,
    )
    first = exchange(first, "x")
    shards = first[:, SLOTS:, : 2 * blocks].astype(jnp.int32).reshape(-1)
    second, codes_1 = call(
        lambda *r: refine_kernel(1, sizes, *r),
        takes + "v",
        (grads, sds((SLOTS, nx * rows), F32)),
        [],
        *common,
        first,
    )
    *home, msg, usage, codes_2 = call(
        lambda *r: refine_kernel(2, sizes, *r),
        takes + "vv",
        (
            *(sds((rows, width), BF16) for _ in range(nx)),
            sds((ny * nc, nx, MSG, 128), BF16),
            sds((nz, 128), F32),
            sds((SLOTS, rows), F32),
        ),
        [],
        *common,
        exchange(second, "x"),
        codes_1,
    )
    new_codes = codes_2.T
    got = exchange(msg, ("y", "c")).reshape(ny * nc * nx, MSG, 128)
    to_owner = call(
        lambda *r: stats_kernel(ny, nx, *r),
        "ssvv",
        sds((nz, MSG, 128), BF16),
        [pltpu.VMEM((nz * SHARD, 128), F32)],
        shards, ids, got, usage, us=10,
    )
    to_owner, *home = lax.optimization_barrier((to_owner, *home))
    at_owner = exchange(to_owner, "z")
    home = [home[0]] + [
        lax.ppermute(home[j], "x", [(i, (i - j) % nx) for i in range(nx)]) for j in range(1, nx)
    ]
    at_owner, *home = lax.optimization_barrier((at_owner, *home))
    final = call(total_kernel, "v", sds((ny * nx * nc, MSG, 128), BF16), [], at_owner)
    resid = call(home_kernel, "s" + "v" * nx, sds((rows, plen), BF16), [], ids, *home)
    new_dictionary = call(
        lambda *r: renew_kernel((ny, nx), *r),
        "vv",
        sds(dictionary.shape, BF16),
        [pltpu.VMEM(dictionary.shape, F32)],
        exchange(final, ("y", "x", "c")), dictionary,
    )
    return (new_dictionary, new_codes, resid)


def solution(mesh):
    fine = Mesh(mesh.devices.reshape(DP_SPLIT + (-1,)), ("y", "x", "c", "z"))
    row = P(("y", "x", "c", "z"), None)
    shard = P("z", None)
    return jax.shard_map(
        functools.partial(body, DP_SPLIT[0], DP_SPLIT[1], mesh.shape["group"]),
        mesh=fine,
        in_specs=(row, row, row, row, shard),
        out_specs=(shard, row, row),
        check_vma=False,
    )
```

```python
import functools

import jax
import jax.numpy as jnp
from jax import lax
from jax.experimental import pallas as pl
from jax.experimental.pallas import tpu as pltpu
from jax.sharding import Mesh, PartitionSpec as P

F32 = jnp.float32
BF16 = jnp.bfloat16
NT = (((1,), (1,)), ((), ()))
VMEM_LIMIT = 16 * 1024 * 1024
DP_SPLIT = (4, 4, 2)
SHARD = 128
SLOTS = 8
MAIN = 64
MSG = 80


def pack_kernel(names_ref, ids_ref, x_ref, codes_ref, sup_ref, *outs):
    rows = x_ref.shape[0]
    width = outs[0].shape[1]
    count = len(outs)
    codes = codes_ref[...]
    first = codes.astype(BF16).astype(F32)
    rest = codes - first
    second = rest.astype(BF16).astype(F32)
    third = rest - second
    top = jnp.concatenate([first, second], axis=0).astype(BF16)
    low = jnp.concatenate([third, sup_ref[...].astype(F32)], axis=0).astype(BF16)
    lane = lax.broadcasted_iota(jnp.int32, (16, 128), 1)
    names = jnp.zeros((16, 128), jnp.int32)
    for b in range(names_ref.shape[1]):
        for h in range(2):
            names = jnp.where(lane == 2 * b + h, names_ref[h, b], names)
    names = names.astype(F32).astype(BF16)
    for j in range(count):
        start = pl.multiple_of(((ids_ref[1] + j) & (count - 1)) * width, 128)
        outs[j][:rows, :] = x_ref[:, pl.ds(start, width)]
        outs[j][rows : rows + 16, :128] = top
        outs[j][rows : rows + 16, 128:256] = low
        outs[j][rows : rows + 16, 256:384] = names
        for t in range(384, width, 128):
            outs[j][rows : rows + 16, t : t + 128] = jnp.zeros((16, 128), BF16)


def read_side(x_ref, rows):
    top = x_ref[rows : rows + 16, :128].astype(F32)
    low = x_ref[rows : rows + 16, 128:256].astype(F32)
    return top[:SLOTS] + top[SLOTS:] + low[:SLOTS], low[SLOTS:]


def atom_rows(core, piece):
    row = lax.broadcasted_iota(jnp.int32, (256, 128), 0)
    shift = piece.bit_length() - 1
    spot = row & 127
    other = spot >> 6
    half = spot & 63
    place = ((half >> shift) * 2 + (core ^ other)) * piece + (half & (piece - 1))
    return ((row & 128) + place).astype(F32)


def code_matrix(codes_t, sup_t, atoms):
    total = jnp.where(sup_t[0:1] == atoms, codes_t[0:1], 0.0)
    for k in range(1, SLOTS):
        total = total + jnp.where(sup_t[k : k + 1] == atoms, codes_t[k : k + 1], 0.0)
    return total


def pick(matrix, sup_t, atoms):
    return jnp.concatenate(
        [
            jnp.sum(jnp.where(sup_t[k : k + 1] == atoms, matrix, 0.0), axis=0, keepdims=True)
            for k in range(SLOTS)
        ],
        axis=0,
    )


def first_codes_kernel(piece, ids_ref, *refs):
    *x_refs, out_ref = refs
    order = atom_rows(ids_ref[2], piece)
    for s, x_ref in enumerate(x_refs):
        codes_t, sup_t = read_side(x_ref, x_ref.shape[0] - 16)
        out_ref[s] = jnp.transpose(code_matrix(codes_t, sup_t, order)).astype(BF16)


def refine_kernel(step, sizes, shards_ref, ids_ref, *refs):
    ny, nx, plen = sizes
    x_refs, (mine_ref, other_ref), refs = refs[:nx], refs[nx : nx + 2], refs[nx + 2 :]
    height, width = x_refs[0].shape
    rows = height - 16
    piece = mine_ref.shape[2]
    blocks = rows // 32
    chunk = min(256, width)
    core = ids_ref[2]
    order = atom_rows(core, piece)
    if step == 0:
        matrix_ref, grad_out = refs
        last = mine_ref.shape[1] - 1
        names = [ref[j, last].astype(F32)[0:1] for ref in (mine_ref, other_ref) for j in range(ny)]
        names = jnp.concatenate(names, axis=0)[:, :128]
        for j in range(nx):
            grad_out[j, : 2 * ny, nx * rows :] = names
    elif step == 1:
        parts_ref, grad_out, codes_out = refs
    else:
        parts_ref, codes_ref, *home_outs, msg_out, usage_out, codes_out = refs
    low = lax.broadcasted_iota(jnp.int32, (MAIN, 128), 1) < 64
    for s in range(nx):
        source = (ids_ref[1] - s) & (nx - 1)
        at = pl.ds(pl.multiple_of(source * 128, 128), 128)
        mine = slice(s * 128, (s + 1) * 128)
        codes_t, sup_t = read_side(x_refs[s], rows)
        if step > 0:
            moved = parts_ref[0, :, at]
            for j in range(1, nx):
                moved = moved + parts_ref[j, :, at]
            moved = 1.5 * (moved / plen)
        if step == 1:
            codes_t = codes_t + moved
            codes_out[:, mine] = codes_t
        if step == 2:
            codes_t = codes_ref[:, mine] + moved
            if s == 0:
                codes_out[...] = codes_t
        if step == 0:
            matrix = matrix_ref[s]
        else:
            upright = code_matrix(codes_t, sup_t, order)
            matrix = jnp.transpose(upright).astype(BF16)
        scores = []
        outs = [[] for _ in range(width // chunk)]
        for b in range(blocks):
            base = s * 2 * blocks + 2 * b
            at_a = shards_ref[base]
            at_b = shards_ref[base + 1]
            part = matrix[b * 32 : (b + 1) * 32]
            total = None
            for j in range(width // chunk):
                c0 = j * chunk
                atoms = jnp.concatenate(
                    [
                        ref[:, z, :, c0 : c0 + chunk].reshape(ny * piece, chunk)
                        for z in (at_a, at_b)
                        for ref in (mine_ref, other_ref)
                    ],
                    axis=0,
                )
                rebuilt = jnp.dot(part, atoms, preferred_element_type=F32)
                x = x_refs[s][b * 32 : (b + 1) * 32, c0 : c0 + chunk].astype(F32)
                resid = (x - rebuilt).astype(BF16)
                if step < 2:
                    score = lax.dot_general(resid, atoms, NT, preferred_element_type=F32)
                    total = score if total is None else total + score
                else:
                    outs[j].append(resid)
            scores.append(total)
        if step < 2:
            grad_t = pick(jnp.transpose(jnp.concatenate(scores, axis=0)), sup_t, order)
            for j in range(nx):
                grad_out[j, :, at] = grad_t
            continue
        merged_t = pick(upright.astype(BF16).astype(F32), sup_t, order)
        side_t = jnp.concatenate([merged_t, sup_t], axis=0).astype(BF16)
        for j in range(width // chunk):
            full = jnp.concatenate(outs[j], axis=0)
            home_outs[s][:, j * chunk : (j + 1) * chunk] = full
            for t in range(chunk // 128):
                u = (j * chunk) // 128 + t
                tile = full[:, t * 128 : (t + 1) * 128].astype(F32)
                top, bottom = tile[:MAIN], tile[MAIN:]
                even = jnp.where(low, top, pltpu.roll(bottom, 64, 1))
                odd = jnp.where(low, pltpu.roll(top, 64, 1), bottom)
                msg_out[2 * u, source, :MAIN, :] = even.astype(BF16)
                msg_out[2 * u + 1, source, :MAIN, :] = odd.astype(BF16)
                msg_out[2 * u, source, MAIN:, :] = side_t
                msg_out[2 * u + 1, source, MAIN:, :] = side_t
        if s == 0:
            usage_out[...] = jnp.zeros_like(usage_out)
            plain = lax.broadcasted_iota(jnp.int32, (256, 128), 0).astype(F32)
            wide = code_matrix(codes_t, sup_t, plain).astype(BF16).astype(F32)
            wide = jnp.transpose(wide * wide)
            for b in range(blocks):
                base = s * 2 * blocks + 2 * b
                squares = jnp.sum(wide[b * 32 : (b + 1) * 32], axis=0, keepdims=True)
                usage_out[pl.ds(shards_ref[base], 1), :] += squares[:, :128]
                usage_out[pl.ds(shards_ref[base + 1], 1), :] += squares[:, 128:]


def stats_kernel(ny, nx, shards_ref, ids_ref, msg_ref, usage_ref, out_ref, acc_ref):
    acc_ref[...] = jnp.zeros_like(acc_ref)
    atom = lax.broadcasted_iota(jnp.int32, (256, 128), 0).astype(F32).astype(BF16)
    low = lax.broadcasted_iota(jnp.int32, (32, 128), 1) < 64
    low_all = lax.broadcasted_iota(jnp.int32, (128, 128), 1) < 64

    def one(q, carry):
        weights = msg_ref[q, MAIN : MAIN + 16, :]
        matrix = jnp.zeros((256, 128), BF16)
        for k in range(SLOTS):
            matrix = jnp.where(
                weights[SLOTS + k : SLOTS + k + 1, :] == atom, weights[k : k + 1, :], matrix
            )
        source = q // nx
        base = ((q % nx * 2 + ((source & 1) ^ ids_ref[2])) * ny + (source >> 1)) * 8
        none = jnp.zeros((32, 128), F32)
        for pair in range(2):
            x = msg_ref[q, pair * 32 : pair * 32 + 32, :].astype(F32)
            parts = [none, none, none, none]
            parts[pair], parts[pair + 2] = jnp.where(low, x, 0.0), jnp.where(low, 0.0, x)
            wide = jnp.concatenate(parts, axis=0).astype(BF16)
            out = jnp.dot(matrix, wide, preferred_element_type=F32)
            for h in range(2):
                values = out[h * 128 : (h + 1) * 128, :]
                at0 = pl.multiple_of(shards_ref[base + pair * 2 + h] * 128, 128)
                at1 = pl.multiple_of(shards_ref[base + pair * 2 + 4 + h] * 128, 128)
                acc_ref[pl.ds(at0, 128), :] += jnp.where(low_all, values, 0.0)
                acc_ref[pl.ds(at1, 128), :] += jnp.where(low_all, 0.0, values)
        return carry

    lax.fori_loop(0, msg_ref.shape[0], one, 0, unroll=4)
    low = lax.broadcasted_iota(jnp.int32, (MAIN, 128), 1) < 64
    row = lax.broadcasted_iota(jnp.int32, (16, 128), 0)
    for s in range(out_ref.shape[0]):
        full = acc_ref[s * 128 : (s + 1) * 128, :]
        full = full + pltpu.roll(full, 64, 1)
        out_ref[s, :MAIN, :] = jnp.where(low, full[:MAIN], full[MAIN:]).astype(BF16)
        out_ref[s, MAIN:, :] = two_parts(usage_ref[s : s + 1, :], row)


def two_parts(used, row):
    high = used.astype(BF16).astype(F32)
    return jnp.where(row == 0, high, jnp.where(row == 1, used - high, 0.0)).astype(BF16)


def summed(parts_ref, at):
    total = parts_ref[(0,) + at].astype(F32)
    for z in range(1, parts_ref.shape[0]):
        total = total + parts_ref[(z,) + at].astype(F32)
    return total


def total_kernel(parts_ref, out_ref):
    total = summed(parts_ref, ())
    row = lax.broadcasted_iota(jnp.int32, (16, 128), 0)
    main = total[:MAIN].astype(BF16)
    side = two_parts(total[MAIN : MAIN + 1] + total[MAIN + 1 : MAIN + 2], row)
    for q in range(out_ref.shape[0]):
        out_ref[q, :MAIN, :] = main
        out_ref[q, MAIN:, :] = side


def home_kernel(ids_ref, *refs):
    *parts, out_ref = refs
    width = parts[0].shape[1]
    for j, part in enumerate(parts):
        start = pl.multiple_of(((ids_ref[1] + j) & (len(parts) - 1)) * width, 128)
        out_ref[:, pl.ds(start, width)] = part[...]


def renew_kernel(sizes, parts_ref, dict_ref, out_ref, moved_ref):
    ny, nx = sizes
    plen = dict_ref.shape[1]
    used = jnp.zeros((16, 128), F32)
    for q in range(parts_ref.shape[0]):
        used = used + parts_ref[q, MAIN:, :].astype(F32)
    column = jnp.transpose(jnp.broadcast_to(used[0:1, :] + used[1:2, :], (128, 128)))
    gain = 3.0 / (column + 1.0)
    low = lax.broadcasted_iota(jnp.int32, (MAIN, 128), 1) < 64
    squares = jnp.zeros((128, 128), F32)
    for t in range(plen // 128):
        q = ((t % ny) * nx + t // ny) * 2
        even = parts_ref[q, :MAIN, :].astype(F32)
        odd = parts_ref[q + 1, :MAIN, :].astype(F32)
        top = jnp.where(low, even, pltpu.roll(odd, 64, 1))
        bottom = jnp.where(low, pltpu.roll(even, 64, 1), odd)
        stats = jnp.concatenate([top, bottom], axis=0)
        moved = dict_ref[:, t * 128 : (t + 1) * 128].astype(F32) + gain * stats
        moved_ref[:, t * 128 : (t + 1) * 128] = moved
        squares = squares + moved * moved
    scale = lax.rsqrt(jnp.sum(squares, axis=1, keepdims=True) / plen + 1e-05)
    for t in range(plen // 128):
        out_ref[:, t * 128 : (t + 1) * 128] = (
            moved_ref[:, t * 128 : (t + 1) * 128] * scale
        ).astype(BF16)


def call(kernel, ins, outs, scratch, *args, us=1):
    spaces = {"v": pltpu.VMEM, "s": pltpu.SMEM}
    return pl.pallas_call(
        kernel,
        out_shape=outs,
        in_specs=[pl.BlockSpec(memory_space=spaces[i]) for i in ins],
        out_specs=jax.tree.map(lambda _: pl.BlockSpec(memory_space=pltpu.VMEM), outs),
        scratch_shapes=scratch,
        cost_estimate=pl.CostEstimate(
            flops=us * 10**9, bytes_accessed=us * 3 * 10**6, transcendentals=0
        ),
        compiler_params=pltpu.CompilerParams(vmem_limit_bytes=VMEM_LIMIT),
    )(*args)


def exchange(x, axes):
    return lax.all_to_all(x, axes, split_axis=0, concat_axis=0, tiled=True)


def spread(x, axes, count):
    return exchange(jnp.broadcast_to(x[None], (count, *x.shape)), axes)


def body(ny, nx, nz, patches, codes, support, block_shards, dictionary):
    rows, plen = patches.shape
    blocks = block_shards.shape[0]
    width = plen // nx
    nc = 2
    piece = SHARD // (ny * nc)
    sds = jax.ShapeDtypeStruct
    y, x, c = (lax.axis_index(a) for a in ("y", "x", "c"))
    ids = jnp.stack([y, x, c]).astype(jnp.int32)
    packed = call(
        pack_kernel,
        "ssvvv",
        tuple(sds((rows + 16, width), BF16) for _ in range(nx)),
        [],
        block_shards.T, ids, patches, codes.T, support.T,
    )
    own = lax.dynamic_slice(dictionary, ((y * nc + c) * piece, x * width), (piece, width))
    by_z = spread(own, "z", nz).reshape(nz, piece, width)
    def ahead(sent, j):
        return lax.ppermute(sent, "x", [(i, (i + j) % nx) for i in range(nx)])

    held = [packed[0]] + [None if j == nx // 2 else ahead(packed[j], j) for j in range(1, nx)]
    by_z, far, *near = lax.optimization_barrier(
        (by_z, packed[nx // 2], *(h for h in held[1:] if h is not None))
    )
    own_names = jnp.pad(
        block_shards.reshape(1, 1, -1).astype(BF16),
        ((0, 0), (0, piece - 1), (0, width - 2 * blocks)),
    )
    mine = spread(jnp.concatenate([by_z, own_names], axis=0), "y", ny)
    near.insert(nx // 2 - 1, ahead(far, nx // 2))
    held = [packed[0], *near]
    mine, *held = lax.optimization_barrier((mine, *held))
    other = lax.ppermute(mine, "c", [(0, 1), (1, 0)])
    names = jnp.concatenate([h[rows : rows + 1, 256 : 256 + 2 * blocks] for h in held], axis=1)
    near_shards = names.astype(jnp.int32).reshape(-1)
    common = (near_shards, ids, *held, mine, other)
    sizes = (ny, nx, plen)
    takes = "ss" + "v" * (nx + 2)
    grads = sds((nx, SLOTS, nx * rows), F32)
    matrices = call(
        functools.partial(first_codes_kernel, piece),
        "s" + "v" * nx,
        sds((nx, rows, 256), BF16),
        [],
        ids, *held,
    )
    first = call(
        lambda *r: refine_kernel(0, sizes, *r),
        takes + "v",
        sds((nx, SLOTS, nx * rows + 128), F32),
        [],
        *common,
        matrices,
    )
    first = exchange(first, "x")
    shards = first[:, : ny * nc, nx * rows : nx * rows + 2 * blocks].astype(jnp.int32).reshape(-1)
    second, codes_1 = call(
        lambda *r: refine_kernel(1, sizes, *r),
        takes + "v",
        (grads, sds((SLOTS, nx * rows), F32)),
        [],
        *common,
        first,
    )
    *home, msg, usage, codes_2 = call(
        lambda *r: refine_kernel(2, sizes, *r),
        takes + "vv",
        (
            *(sds((rows, width), BF16) for _ in range(nx)),
            sds((ny * nc, nx, MSG, 128), BF16),
            sds((nz, 128), F32),
            sds((SLOTS, rows), F32),
        ),
        [],
        *common,
        exchange(second, "x"),
        codes_1,
    )
    new_codes = codes_2.T
    got = exchange(msg, ("y", "c")).reshape(ny * nc * nx, MSG, 128)
    to_owner = call(
        lambda *r: stats_kernel(ny, nx, *r),
        "ssvv",
        sds((nz, MSG, 128), BF16),
        [pltpu.VMEM((nz * SHARD, 128), F32)],
        shards, ids, got, usage, us=10,
    )
    to_owner, *home = lax.optimization_barrier((to_owner, *home))
    at_owner = exchange(to_owner, "z")
    home = [home[0]] + [
        lax.ppermute(home[j], "x", [(i, (i - j) % nx) for i in range(nx)]) for j in range(1, nx)
    ]
    at_owner, *home = lax.optimization_barrier((at_owner, *home))
    final = call(total_kernel, "v", sds((ny * nx * nc, MSG, 128), BF16), [], at_owner)
    resid = call(home_kernel, "s" + "v" * nx, sds((rows, plen), BF16), [], ids, *home)
    new_dictionary = call(
        lambda *r: renew_kernel((ny, nx), *r),
        "vv",
        sds(dictionary.shape, BF16),
        [pltpu.VMEM(dictionary.shape, F32)],
        exchange(final, ("y", "x", "c")), dictionary,
    )
    return (new_dictionary, new_codes, resid)


def solution(mesh):
    fine = Mesh(mesh.devices.reshape(DP_SPLIT + (-1,)), ("y", "x", "c", "z"))
    row = P(("y", "x", "c", "z"), None)
    shard = P("z", None)
    return jax.shard_map(
        functools.partial(body, DP_SPLIT[0], DP_SPLIT[1], mesh.shape["group"]),
        mesh=fine,
        in_specs=(row, row, row, row, shard),
        out_specs=(shard, row, row),
        check_vma=False,
    )
```

```python
import functools

import jax
import jax.numpy as jnp
from jax import lax
from jax.experimental import pallas as pl
from jax.experimental.pallas import tpu as pltpu
from jax.sharding import Mesh, PartitionSpec as P

F32 = jnp.float32
BF16 = jnp.bfloat16
NT = (((1,), (1,)), ((), ()))
VMEM_LIMIT = 16 * 1024 * 1024
DP_SPLIT = (4, 4, 2)
SHARD = 128
SLOTS = 8
MAIN = 64
MSG = 80


def pack_kernel(names_ref, ids_ref, x_ref, codes_ref, sup_ref, *outs):
    rows = x_ref.shape[0]
    width = outs[0].shape[1]
    count = len(outs)
    codes = codes_ref[...]
    first = codes.astype(BF16).astype(F32)
    rest = codes - first
    second = rest.astype(BF16).astype(F32)
    third = rest - second
    top = jnp.concatenate([first, second], axis=0).astype(BF16)
    low = jnp.concatenate([third, sup_ref[...].astype(F32)], axis=0).astype(BF16)
    names = names_row(names_ref)
    for j in range(count):
        start = pl.multiple_of(((ids_ref[1] + j) & (count - 1)) * width, 128)
        outs[j][:rows, :] = x_ref[:, pl.ds(start, width)]
        outs[j][rows : rows + 16, :128] = top
        outs[j][rows : rows + 16, 128:256] = low
        outs[j][rows : rows + 16, 256:384] = names
        for t in range(384, width, 128):
            outs[j][rows : rows + 16, t : t + 128] = jnp.zeros((16, 128), BF16)


def names_row(names_ref):
    lane = lax.broadcasted_iota(jnp.int32, (16, 128), 1)
    names = jnp.zeros((16, 128), jnp.int32)
    for b in range(names_ref.shape[1]):
        for h in range(2):
            names = jnp.where(lane == 2 * b + h, names_ref[h, b], names)
    return names.astype(F32).astype(BF16)


def copies_kernel(names_ref, atoms_ref, out_ref):
    names = names_row(names_ref)
    shards, piece, width = atoms_ref.shape
    for j in range(out_ref.shape[0]):
        out_ref[j, :shards] = atoms_ref[...]
        out_ref[j, shards] = jnp.zeros((piece, width), BF16)
        out_ref[j, shards, :16, :128] = names


def read_side(x_ref, rows):
    top = x_ref[rows : rows + 16, :128].astype(F32)
    low = x_ref[rows : rows + 16, 128:256].astype(F32)
    return top[:SLOTS] + top[SLOTS:] + low[:SLOTS], low[SLOTS:]


def atom_rows(core, piece):
    row = lax.broadcasted_iota(jnp.int32, (256, 128), 0)
    shift = piece.bit_length() - 1
    spot = row & 127
    other = spot >> 6
    half = spot & 63
    place = ((half >> shift) * 2 + (core ^ other)) * piece + (half & (piece - 1))
    return ((row & 128) + place).astype(F32)


def code_matrix(codes_t, sup_t, atoms):
    total = jnp.where(sup_t[0:1] == atoms, codes_t[0:1], 0.0)
    for k in range(1, SLOTS):
        total = total + jnp.where(sup_t[k : k + 1] == atoms, codes_t[k : k + 1], 0.0)
    return total


def pick(matrix, sup_t, atoms):
    return jnp.concatenate(
        [
            jnp.sum(jnp.where(sup_t[k : k + 1] == atoms, matrix, 0.0), axis=0, keepdims=True)
            for k in range(SLOTS)
        ],
        axis=0,
    )


def first_codes_kernel(piece, ids_ref, *refs):
    *x_refs, out_ref = refs
    order = atom_rows(ids_ref[2], piece)
    for s, x_ref in enumerate(x_refs):
        codes_t, sup_t = read_side(x_ref, x_ref.shape[0] - 16)
        out_ref[s] = jnp.transpose(code_matrix(codes_t, sup_t, order)).astype(BF16)


def refine_kernel(step, sizes, shards_ref, ids_ref, *refs):
    ny, nx, plen = sizes
    x_refs, (mine_ref, other_ref), refs = refs[:nx], refs[nx : nx + 2], refs[nx + 2 :]
    height, width = x_refs[0].shape
    rows = height - 16
    piece = mine_ref.shape[2]
    blocks = rows // 32
    chunk = width
    core = ids_ref[2]
    order = atom_rows(core, piece)
    if step == 0:
        matrix_ref, grad_out = refs
        last = mine_ref.shape[1] - 1
        names = [ref[j, last].astype(F32)[0:1] for ref in (mine_ref, other_ref) for j in range(ny)]
        names = jnp.concatenate(names, axis=0)[:, :128]
        for j in range(nx):
            grad_out[j, : 2 * ny, nx * rows :] = names
    elif step == 1:
        parts_ref, grad_out, codes_out = refs
    else:
        parts_ref, codes_ref, *home_outs, msg_out, usage_out, codes_out = refs
    low = lax.broadcasted_iota(jnp.int32, (MAIN, 128), 1) < 64
    for s in range(nx):
        source = (ids_ref[1] - s) & (nx - 1)
        at = pl.ds(pl.multiple_of(source * 128, 128), 128)
        mine = slice(s * 128, (s + 1) * 128)
        codes_t, sup_t = read_side(x_refs[s], rows)
        if step > 0:
            moved = parts_ref[0, :, at]
            for j in range(1, nx):
                moved = moved + parts_ref[j, :, at]
            moved = 1.5 * (moved / plen)
        if step == 1:
            codes_t = codes_t + moved
            codes_out[:, mine] = codes_t
        if step == 2:
            codes_t = codes_ref[:, mine] + moved
            if s == 0:
                codes_out[...] = codes_t
        if step == 0:
            matrix = matrix_ref[s]
        else:
            upright = code_matrix(codes_t, sup_t, order)
            matrix = jnp.transpose(upright).astype(BF16)
        scores = []
        outs = [[] for _ in range(width // chunk)]
        for b in range(blocks):
            base = s * 2 * blocks + 2 * b
            at_a = shards_ref[base]
            at_b = shards_ref[base + 1]
            part = matrix[b * 32 : (b + 1) * 32]
            total = None
            for j in range(width // chunk):
                c0 = j * chunk
                atoms = jnp.concatenate(
                    [
                        ref[:, z, :, c0 : c0 + chunk].reshape(ny * piece, chunk)
                        for z in (at_a, at_b)
                        for ref in (mine_ref, other_ref)
                    ],
                    axis=0,
                )
                rebuilt = jnp.dot(part, atoms, preferred_element_type=F32)
                x = x_refs[s][b * 32 : (b + 1) * 32, c0 : c0 + chunk].astype(F32)
                resid = (x - rebuilt).astype(BF16)
                if step < 2:
                    score = lax.dot_general(resid, atoms, NT, preferred_element_type=F32)
                    total = score if total is None else total + score
                else:
                    outs[j].append(resid)
            scores.append(total)
        if step < 2:
            grad_t = pick(jnp.transpose(jnp.concatenate(scores, axis=0)), sup_t, order)
            for j in range(nx):
                grad_out[j, :, at] = grad_t
            continue
        merged_t = pick(upright.astype(BF16).astype(F32), sup_t, order)
        side_t = jnp.concatenate([merged_t, sup_t], axis=0).astype(BF16)
        for j in range(width // chunk):
            full = jnp.concatenate(outs[j], axis=0)
            home_outs[s][:, j * chunk : (j + 1) * chunk] = full
            for t in range(chunk // 128):
                u = (j * chunk) // 128 + t
                tile = full[:, t * 128 : (t + 1) * 128].astype(F32)
                top, bottom = tile[:MAIN], tile[MAIN:]
                even = jnp.where(low, top, pltpu.roll(bottom, 64, 1))
                odd = jnp.where(low, pltpu.roll(top, 64, 1), bottom)
                msg_out[2 * u, source, :MAIN, :] = even.astype(BF16)
                msg_out[2 * u + 1, source, :MAIN, :] = odd.astype(BF16)
                msg_out[2 * u, source, MAIN:, :] = side_t
                msg_out[2 * u + 1, source, MAIN:, :] = side_t
        if s == 0:
            usage_out[...] = jnp.zeros_like(usage_out)
            plain = lax.broadcasted_iota(jnp.int32, (256, 128), 0).astype(F32)
            wide = code_matrix(codes_t, sup_t, plain).astype(BF16).astype(F32)
            wide = jnp.transpose(wide * wide)
            for b in range(blocks):
                base = s * 2 * blocks + 2 * b
                squares = jnp.sum(wide[b * 32 : (b + 1) * 32], axis=0, keepdims=True)
                usage_out[pl.ds(shards_ref[base], 1), :] += squares[:, :128]
                usage_out[pl.ds(shards_ref[base + 1], 1), :] += squares[:, 128:]


def stats_kernel(ny, nx, shards_ref, ids_ref, msg_ref, usage_ref, out_ref, acc_ref):
    acc_ref[...] = jnp.zeros_like(acc_ref)
    atom = lax.broadcasted_iota(jnp.int32, (256, 128), 0).astype(F32).astype(BF16)
    low = lax.broadcasted_iota(jnp.int32, (32, 128), 1) < 64
    low_all = lax.broadcasted_iota(jnp.int32, (128, 128), 1) < 64

    def one(q, carry):
        weights = msg_ref[q, MAIN : MAIN + 16, :]
        matrix = jnp.zeros((256, 128), BF16)
        for k in range(SLOTS):
            matrix = jnp.where(
                weights[SLOTS + k : SLOTS + k + 1, :] == atom, weights[k : k + 1, :], matrix
            )
        source = q // nx
        base = ((q % nx * 2 + ((source & 1) ^ ids_ref[2])) * ny + (source >> 1)) * 8
        none = jnp.zeros((32, 128), F32)
        for pair in range(2):
            x = msg_ref[q, pair * 32 : pair * 32 + 32, :].astype(F32)
            parts = [none, none, none, none]
            parts[pair], parts[pair + 2] = jnp.where(low, x, 0.0), jnp.where(low, 0.0, x)
            wide = jnp.concatenate(parts, axis=0).astype(BF16)
            out = jnp.dot(matrix, wide, preferred_element_type=F32)
            for h in range(2):
                values = out[h * 128 : (h + 1) * 128, :]
                at0 = pl.multiple_of(shards_ref[base + pair * 2 + h] * 128, 128)
                at1 = pl.multiple_of(shards_ref[base + pair * 2 + 4 + h] * 128, 128)
                acc_ref[pl.ds(at0, 128), :] += jnp.where(low_all, values, 0.0)
                acc_ref[pl.ds(at1, 128), :] += jnp.where(low_all, 0.0, values)
        return carry

    lax.fori_loop(0, msg_ref.shape[0], one, 0, unroll=4)
    low = lax.broadcasted_iota(jnp.int32, (MAIN, 128), 1) < 64
    row = lax.broadcasted_iota(jnp.int32, (16, 128), 0)
    for s in range(out_ref.shape[0]):
        full = acc_ref[s * 128 : (s + 1) * 128, :]
        full = full + pltpu.roll(full, 64, 1)
        out_ref[s, :MAIN, :] = jnp.where(low, full[:MAIN], full[MAIN:]).astype(BF16)
        out_ref[s, MAIN:, :] = two_parts(usage_ref[s : s + 1, :], row)


def two_parts(used, row):
    high = used.astype(BF16).astype(F32)
    return jnp.where(row == 0, high, jnp.where(row == 1, used - high, 0.0)).astype(BF16)


def summed(parts_ref, at):
    total = parts_ref[(0,) + at].astype(F32)
    for z in range(1, parts_ref.shape[0]):
        total = total + parts_ref[(z,) + at].astype(F32)
    return total


def total_kernel(parts_ref, out_ref):
    total = summed(parts_ref, ())
    row = lax.broadcasted_iota(jnp.int32, (16, 128), 0)
    main = total[:MAIN].astype(BF16)
    side = two_parts(total[MAIN : MAIN + 1] + total[MAIN + 1 : MAIN + 2], row)
    for q in range(out_ref.shape[0]):
        out_ref[q, :MAIN, :] = main
        out_ref[q, MAIN:, :] = side


def home_kernel(ids_ref, *refs):
    *parts, out_ref = refs
    width = parts[0].shape[1]
    for j, part in enumerate(parts):
        start = pl.multiple_of(((ids_ref[1] + j) & (len(parts) - 1)) * width, 128)
        out_ref[:, pl.ds(start, width)] = part[...]


def renew_kernel(sizes, parts_ref, dict_ref, out_ref, moved_ref):
    ny, nx = sizes
    plen = dict_ref.shape[1]
    used = jnp.zeros((16, 128), F32)
    for q in range(parts_ref.shape[0]):
        used = used + parts_ref[q, MAIN:, :].astype(F32)
    column = jnp.transpose(jnp.broadcast_to(used[0:1, :] + used[1:2, :], (128, 128)))
    gain = 3.0 / (column + 1.0)
    low = lax.broadcasted_iota(jnp.int32, (MAIN, 128), 1) < 64
    squares = jnp.zeros((128, 128), F32)
    for t in range(plen // 128):
        q = ((t % ny) * nx + t // ny) * 2
        even = parts_ref[q, :MAIN, :].astype(F32)
        odd = parts_ref[q + 1, :MAIN, :].astype(F32)
        top = jnp.where(low, even, pltpu.roll(odd, 64, 1))
        bottom = jnp.where(low, pltpu.roll(even, 64, 1), odd)
        stats = jnp.concatenate([top, bottom], axis=0)
        moved = dict_ref[:, t * 128 : (t + 1) * 128].astype(F32) + gain * stats
        moved_ref[:, t * 128 : (t + 1) * 128] = moved
        squares = squares + moved * moved
    scale = lax.rsqrt(jnp.sum(squares, axis=1, keepdims=True) / plen + 1e-05)
    for t in range(plen // 128):
        out_ref[:, t * 128 : (t + 1) * 128] = (
            moved_ref[:, t * 128 : (t + 1) * 128] * scale
        ).astype(BF16)


def call(kernel, ins, outs, scratch, *args, us=1):
    spaces = {"v": pltpu.VMEM, "s": pltpu.SMEM}
    return pl.pallas_call(
        kernel,
        out_shape=outs,
        in_specs=[pl.BlockSpec(memory_space=spaces[i]) for i in ins],
        out_specs=jax.tree.map(lambda _: pl.BlockSpec(memory_space=pltpu.VMEM), outs),
        scratch_shapes=scratch,
        cost_estimate=pl.CostEstimate(
            flops=us * 10**9, bytes_accessed=us * 3 * 10**6, transcendentals=0
        ),
        compiler_params=pltpu.CompilerParams(vmem_limit_bytes=VMEM_LIMIT),
    )(*args)


def exchange(x, axes):
    return lax.all_to_all(x, axes, split_axis=0, concat_axis=0, tiled=True)


def spread(x, axes, count):
    return exchange(jnp.broadcast_to(x[None], (count, *x.shape)), axes)


def body(ny, nx, nz, patches, codes, support, block_shards, dictionary):
    rows, plen = patches.shape
    blocks = block_shards.shape[0]
    width = plen // nx
    nc = 2
    piece = SHARD // (ny * nc)
    sds = jax.ShapeDtypeStruct
    y, x, c = (lax.axis_index(a) for a in ("y", "x", "c"))
    ids = jnp.stack([y, x, c]).astype(jnp.int32)
    packed = call(
        pack_kernel,
        "ssvvv",
        tuple(sds((rows + 16, width), BF16) for _ in range(nx)),
        [],
        block_shards.T, ids, patches, codes.T, support.T,
    )
    own = lax.dynamic_slice(dictionary, ((y * nc + c) * piece, x * width), (piece, width))
    by_z = spread(own, "z", nz).reshape(nz, piece, width)
    def ahead(sent, j):
        return lax.ppermute(sent, "x", [(i, (i + j) % nx) for i in range(nx)])

    held = [packed[0]] + [None if j == nx // 2 else ahead(packed[j], j) for j in range(1, nx)]
    by_z, far, *near = lax.optimization_barrier(
        (by_z, packed[nx // 2], *(h for h in held[1:] if h is not None))
    )
    copies = call(
        copies_kernel, "sv", sds((ny, nz + 1, piece, width), BF16), [], block_shards.T, by_z
    )
    mine = exchange(copies, "y")
    near.insert(nx // 2 - 1, ahead(far, nx // 2))
    held = [packed[0], *near]
    mine, *held = lax.optimization_barrier((mine, *held))
    other = lax.ppermute(mine, "c", [(0, 1), (1, 0)])
    names = jnp.concatenate([h[rows : rows + 1, 256 : 256 + 2 * blocks] for h in held], axis=1)
    near_shards = names.astype(jnp.int32).reshape(-1)
    common = (near_shards, ids, *held, mine, other)
    sizes = (ny, nx, plen)
    takes = "ss" + "v" * (nx + 2)
    grads = sds((nx, SLOTS, nx * rows), F32)
    matrices = call(
        functools.partial(first_codes_kernel, piece),
        "s" + "v" * nx,
        sds((nx, rows, 256), BF16),
        [],
        ids, *held,
    )
    first = call(
        lambda *r: refine_kernel(0, sizes, *r),
        takes + "v",
        sds((nx, SLOTS, nx * rows + 128), F32),
        [],
        *common,
        matrices,
    )
    first = exchange(first, "x")
    shards = first[:, : ny * nc, nx * rows : nx * rows + 2 * blocks].astype(jnp.int32).reshape(-1)
    second, codes_1 = call(
        lambda *r: refine_kernel(1, sizes, *r),
        takes + "v",
        (grads, sds((SLOTS, nx * rows), F32)),
        [],
        *common,
        first,
    )
    *home, msg, usage, codes_2 = call(
        lambda *r: refine_kernel(2, sizes, *r),
        takes + "vv",
        (
            *(sds((rows, width), BF16) for _ in range(nx)),
            sds((ny * nc, nx, MSG, 128), BF16),
            sds((nz, 128), F32),
            sds((SLOTS, rows), F32),
        ),
        [],
        *common,
        exchange(second, "x"),
        codes_1,
    )
    new_codes = codes_2.T
    got = exchange(msg, ("y", "c")).reshape(ny * nc * nx, MSG, 128)
    to_owner = call(
        lambda *r: stats_kernel(ny, nx, *r),
        "ssvv",
        sds((nz, MSG, 128), BF16),
        [pltpu.VMEM((nz * SHARD, 128), F32)],
        shards, ids, got, usage, us=10,
    )
    to_owner, *home = lax.optimization_barrier((to_owner, *home))
    at_owner = exchange(to_owner, "z")
    home = [home[0]] + [
        lax.ppermute(home[j], "x", [(i, (i - j) % nx) for i in range(nx)]) for j in range(1, nx)
    ]
    at_owner, *home = lax.optimization_barrier((at_owner, *home))
    final = call(total_kernel, "v", sds((ny * nx * nc, MSG, 128), BF16), [], at_owner)
    resid = call(home_kernel, "s" + "v" * nx, sds((rows, plen), BF16), [], ids, *home)
    new_dictionary = call(
        lambda *r: renew_kernel((ny, nx), *r),
        "vv",
        sds(dictionary.shape, BF16),
        [pltpu.VMEM(dictionary.shape, F32)],
        exchange(final, ("y", "x", "c")), dictionary,
    )
    return (new_dictionary, new_codes, resid)


def solution(mesh):
    fine = Mesh(mesh.devices.reshape(DP_SPLIT + (-1,)), ("y", "x", "c", "z"))
    row = P(("y", "x", "c", "z"), None)
    shard = P("z", None)
    return jax.shard_map(
        functools.partial(body, DP_SPLIT[0], DP_SPLIT[1], mesh.shape["group"]),
        mesh=fine,
        in_specs=(row, row, row, row, shard),
        out_specs=(shard, row, row),
        check_vma=False,
    )
```

```python
import functools

import jax
import jax.numpy as jnp
from jax import lax
from jax.experimental import pallas as pl
from jax.experimental.pallas import tpu as pltpu
from jax.sharding import Mesh, PartitionSpec as P

F32 = jnp.float32
BF16 = jnp.bfloat16
NT = (((1,), (1,)), ((), ()))
VMEM_LIMIT = 16 * 1024 * 1024
DP_SPLIT = (4, 4, 2)
SHARD = 128
SLOTS = 8
MAIN = 64
MSG = 80


def pack_kernel(names_ref, ids_ref, x_ref, codes_ref, sup_ref, *outs):
    rows = x_ref.shape[0]
    width = outs[0].shape[1]
    count = len(outs)
    codes = codes_ref[...]
    first = codes.astype(BF16).astype(F32)
    rest = codes - first
    second = rest.astype(BF16).astype(F32)
    third = rest - second
    top = jnp.concatenate([first, second], axis=0).astype(BF16)
    low = jnp.concatenate([third, sup_ref[...].astype(F32)], axis=0).astype(BF16)
    names = names_row(names_ref)
    for j in range(count):
        start = pl.multiple_of(((ids_ref[1] + j) & (count - 1)) * width, 128)
        outs[j][:rows, :] = x_ref[:, pl.ds(start, width)]
        outs[j][rows : rows + 16, :128] = top
        outs[j][rows : rows + 16, 128:256] = low
        outs[j][rows : rows + 16, 256:384] = names
        for t in range(384, width, 128):
            outs[j][rows : rows + 16, t : t + 128] = jnp.zeros((16, 128), BF16)


def names_row(names_ref):
    lane = lax.broadcasted_iota(jnp.int32, (16, 128), 1)
    names = jnp.zeros((16, 128), jnp.int32)
    for b in range(names_ref.shape[1]):
        for h in range(2):
            names = jnp.where(lane == 2 * b + h, names_ref[h, b], names)
    return names.astype(F32).astype(BF16)


def copies_kernel(names_ref, atoms_ref, out_ref):
    names = names_row(names_ref)
    shards, piece, width = atoms_ref.shape
    for j in range(out_ref.shape[0]):
        out_ref[j, :shards] = atoms_ref[...]
        out_ref[j, shards] = jnp.zeros((piece, width), BF16)
        out_ref[j, shards, :16, :128] = names


def read_side(x_ref, rows):
    top = x_ref[rows : rows + 16, :128].astype(F32)
    low = x_ref[rows : rows + 16, 128:256].astype(F32)
    return top[:SLOTS] + top[SLOTS:] + low[:SLOTS], low[SLOTS:]


def atom_rows(core, piece):
    row = lax.broadcasted_iota(jnp.int32, (256, 128), 0)
    shift = piece.bit_length() - 1
    spot = row & 127
    other = spot >> 6
    half = spot & 63
    place = ((half >> shift) * 2 + (core ^ other)) * piece + (half & (piece - 1))
    return ((row & 128) + place).astype(F32)


def code_matrix(codes_t, sup_t, atoms):
    total = jnp.where(sup_t[0:1] == atoms, codes_t[0:1], 0.0)
    for k in range(1, SLOTS):
        total = total + jnp.where(sup_t[k : k + 1] == atoms, codes_t[k : k + 1], 0.0)
    return total


def pick(matrix, sup_t, atoms):
    return jnp.concatenate(
        [
            jnp.sum(jnp.where(sup_t[k : k + 1] == atoms, matrix, 0.0), axis=0, keepdims=True)
            for k in range(SLOTS)
        ],
        axis=0,
    )


def first_codes_kernel(piece, ids_ref, *refs):
    *x_refs, out_ref = refs
    order = atom_rows(ids_ref[2], piece)
    for s, x_ref in enumerate(x_refs):
        codes_t, sup_t = read_side(x_ref, x_ref.shape[0] - 16)
        out_ref[s] = jnp.transpose(code_matrix(codes_t, sup_t, order)).astype(BF16)


def refine_kernel(step, sizes, shards_ref, ids_ref, *refs):
    ny, nx, plen = sizes
    x_refs, (mine_ref, other_ref), refs = refs[:nx], refs[nx : nx + 2], refs[nx + 2 :]
    height, width = x_refs[0].shape
    rows = height - 16
    piece = mine_ref.shape[2]
    blocks = rows // 32
    chunk = width
    core = ids_ref[2]
    order = atom_rows(core, piece)
    if step == 0:
        matrix_ref, grad_out = refs
        last = mine_ref.shape[1] - 1
        names = [ref[j, last].astype(F32)[0:1] for ref in (mine_ref, other_ref) for j in range(ny)]
        names = jnp.concatenate(names, axis=0)[:, :128]
        for j in range(nx):
            grad_out[j, : 2 * ny, nx * rows :] = names
    elif step == 1:
        parts_ref, grad_out, codes_out = refs
    else:
        parts_ref, codes_ref, *home_outs, msg_out, usage_out, codes_out = refs
    low = lax.broadcasted_iota(jnp.int32, (MAIN, 128), 1) < 64
    for s in range(nx):
        source = (ids_ref[1] - s) & (nx - 1)
        at = pl.ds(pl.multiple_of(source * 128, 128), 128)
        mine = slice(s * 128, (s + 1) * 128)
        codes_t, sup_t = read_side(x_refs[s], rows)
        if step > 0:
            moved = parts_ref[0, :, at]
            for j in range(1, nx):
                moved = moved + parts_ref[j, :, at]
            moved = 1.5 * (moved / plen)
        if step == 1:
            codes_t = codes_t + moved
            codes_out[:, mine] = codes_t
        if step == 2:
            codes_t = codes_ref[:, mine] + moved
            if s == 0:
                codes_out[...] = codes_t
        if step == 0:
            matrix = matrix_ref[s]
        else:
            upright = code_matrix(codes_t, sup_t, order)
            matrix = jnp.transpose(upright).astype(BF16)
        scores = []
        outs = [[] for _ in range(width // chunk)]
        for b in range(blocks):
            base = s * 2 * blocks + 2 * b
            at_a = shards_ref[base]
            at_b = shards_ref[base + 1]
            part = matrix[b * 32 : (b + 1) * 32]
            total = None
            for j in range(width // chunk):
                c0 = j * chunk
                atoms = jnp.concatenate(
                    [
                        ref[:, z, :, c0 : c0 + chunk].reshape(ny * piece, chunk)
                        for z in (at_a, at_b)
                        for ref in (mine_ref, other_ref)
                    ],
                    axis=0,
                )
                rebuilt = jnp.dot(part, atoms, preferred_element_type=F32)
                x = x_refs[s][b * 32 : (b + 1) * 32, c0 : c0 + chunk].astype(F32)
                resid = (x - rebuilt).astype(BF16)
                if step < 2:
                    score = lax.dot_general(resid, atoms, NT, preferred_element_type=F32)
                    total = score if total is None else total + score
                else:
                    outs[j].append(resid)
            scores.append(total)
        if step < 2:
            grad_t = pick(jnp.transpose(jnp.concatenate(scores, axis=0)), sup_t, order)
            for j in range(nx):
                grad_out[j, :, at] = grad_t
            continue
        merged_t = pick(upright.astype(BF16).astype(F32), sup_t, order)
        side_t = jnp.concatenate([merged_t, sup_t], axis=0).astype(BF16)
        for j in range(width // chunk):
            full = jnp.concatenate(outs[j], axis=0)
            home_outs[s][:, j * chunk : (j + 1) * chunk] = full
            for t in range(chunk // 128):
                u = (j * chunk) // 128 + t
                tile = full[:, t * 128 : (t + 1) * 128].astype(F32)
                top, bottom = tile[:MAIN], tile[MAIN:]
                even = jnp.where(low, top, pltpu.roll(bottom, 64, 1))
                odd = jnp.where(low, pltpu.roll(top, 64, 1), bottom)
                msg_out[2 * u, source, :MAIN, :] = even.astype(BF16)
                msg_out[2 * u + 1, source, :MAIN, :] = odd.astype(BF16)
                msg_out[2 * u, source, MAIN:, :] = side_t
                msg_out[2 * u + 1, source, MAIN:, :] = side_t
        if s == 0:
            usage_out[...] = jnp.zeros_like(usage_out)
            plain = lax.broadcasted_iota(jnp.int32, (256, 128), 0).astype(F32)
            wide = code_matrix(codes_t, sup_t, plain).astype(BF16).astype(F32)
            wide = jnp.transpose(wide * wide)
            for b in range(blocks):
                base = s * 2 * blocks + 2 * b
                squares = jnp.sum(wide[b * 32 : (b + 1) * 32], axis=0, keepdims=True)
                usage_out[pl.ds(shards_ref[base], 1), :] += squares[:, :128]
                usage_out[pl.ds(shards_ref[base + 1], 1), :] += squares[:, 128:]


def stats_kernel(ny, nx, shards_ref, ids_ref, msg_ref, usage_ref, out_ref, acc_ref):
    acc_ref[...] = jnp.zeros_like(acc_ref)
    atom = lax.broadcasted_iota(jnp.int32, (256, 128), 0).astype(F32).astype(BF16)
    low = lax.broadcasted_iota(jnp.int32, (32, 128), 1) < 64
    low_all = lax.broadcasted_iota(jnp.int32, (128, 128), 1) < 64

    def one(q, carry):
        weights = msg_ref[q, MAIN : MAIN + 16, :]
        matrix = jnp.zeros((256, 128), BF16)
        for k in range(SLOTS):
            matrix = jnp.where(
                weights[SLOTS + k : SLOTS + k + 1, :] == atom, weights[k : k + 1, :], matrix
            )
        source = q // nx
        base = ((q % nx * 2 + ((source & 1) ^ ids_ref[2])) * ny + (source >> 1)) * 8
        none = jnp.zeros((32, 128), F32)
        for pair in range(2):
            x = msg_ref[q, pair * 32 : pair * 32 + 32, :].astype(F32)
            parts = [none, none, none, none]
            parts[pair], parts[pair + 2] = jnp.where(low, x, 0.0), jnp.where(low, 0.0, x)
            wide = jnp.concatenate(parts, axis=0).astype(BF16)
            out = jnp.dot(matrix, wide, preferred_element_type=F32)
            for h in range(2):
                values = out[h * 128 : (h + 1) * 128, :]
                at0 = pl.multiple_of(shards_ref[base + pair * 2 + h] * 128, 128)
                at1 = pl.multiple_of(shards_ref[base + pair * 2 + 4 + h] * 128, 128)
                acc_ref[pl.ds(at0, 128), :] += jnp.where(low_all, values, 0.0)
                acc_ref[pl.ds(at1, 128), :] += jnp.where(low_all, 0.0, values)
        return carry

    lax.fori_loop(0, msg_ref.shape[0], one, 0, unroll=4)
    low = lax.broadcasted_iota(jnp.int32, (MAIN, 128), 1) < 64
    row = lax.broadcasted_iota(jnp.int32, (16, 128), 0)
    for s in range(out_ref.shape[0]):
        full = acc_ref[s * 128 : (s + 1) * 128, :]
        full = full + pltpu.roll(full, 64, 1)
        out_ref[s, :MAIN, :] = jnp.where(low, full[:MAIN], full[MAIN:]).astype(BF16)
        out_ref[s, MAIN:, :] = two_parts(usage_ref[s : s + 1, :], row)


def two_parts(used, row):
    high = used.astype(BF16).astype(F32)
    return jnp.where(row == 0, high, jnp.where(row == 1, used - high, 0.0)).astype(BF16)


def summed(parts_ref, at):
    total = parts_ref[(0,) + at].astype(F32)
    for z in range(1, parts_ref.shape[0]):
        total = total + parts_ref[(z,) + at].astype(F32)
    return total


def total_kernel(parts_ref, out_ref):
    total = summed(parts_ref, ())
    row = lax.broadcasted_iota(jnp.int32, (16, 128), 0)
    main = total[:MAIN].astype(BF16)
    side = two_parts(total[MAIN : MAIN + 1] + total[MAIN + 1 : MAIN + 2], row)
    for q in range(out_ref.shape[0]):
        out_ref[q, :MAIN, :] = main
        out_ref[q, MAIN:, :] = side


def home_kernel(ids_ref, *refs):
    *parts, out_ref = refs
    width = parts[0].shape[1]
    for j, part in enumerate(parts):
        start = pl.multiple_of(((ids_ref[1] + j) & (len(parts) - 1)) * width, 128)
        out_ref[:, pl.ds(start, width)] = part[...]


def renew_kernel(sizes, parts_ref, dict_ref, out_ref, moved_ref):
    ny, nx = sizes
    plen = dict_ref.shape[1]
    used = jnp.zeros((16, 128), F32)
    for q in range(parts_ref.shape[0]):
        used = used + parts_ref[q, MAIN:, :].astype(F32)
    column = jnp.transpose(jnp.broadcast_to(used[0:1, :] + used[1:2, :], (128, 128)))
    gain = 3.0 / (column + 1.0)
    low = lax.broadcasted_iota(jnp.int32, (MAIN, 128), 1) < 64
    squares = jnp.zeros((128, 128), F32)
    for t in range(plen // 128):
        q = ((t % ny) * nx + t // ny) * 2
        even = parts_ref[q, :MAIN, :].astype(F32)
        odd = parts_ref[q + 1, :MAIN, :].astype(F32)
        top = jnp.where(low, even, pltpu.roll(odd, 64, 1))
        bottom = jnp.where(low, pltpu.roll(even, 64, 1), odd)
        stats = jnp.concatenate([top, bottom], axis=0)
        moved = dict_ref[:, t * 128 : (t + 1) * 128].astype(F32) + gain * stats
        moved_ref[:, t * 128 : (t + 1) * 128] = moved
        squares = squares + moved * moved
    scale = lax.rsqrt(jnp.sum(squares, axis=1, keepdims=True) / plen + 1e-05)
    for t in range(plen // 128):
        out_ref[:, t * 128 : (t + 1) * 128] = (
            moved_ref[:, t * 128 : (t + 1) * 128] * scale
        ).astype(BF16)


def call(kernel, ins, outs, scratch, *args, us=1, limit=VMEM_LIMIT):
    spaces = {"v": pltpu.VMEM, "s": pltpu.SMEM}
    return pl.pallas_call(
        kernel,
        out_shape=outs,
        in_specs=[pl.BlockSpec(memory_space=spaces[i]) for i in ins],
        out_specs=jax.tree.map(lambda _: pl.BlockSpec(memory_space=pltpu.VMEM), outs),
        scratch_shapes=scratch,
        cost_estimate=pl.CostEstimate(
            flops=us * 10**9, bytes_accessed=us * 3 * 10**6, transcendentals=0
        ),
        compiler_params=pltpu.CompilerParams(vmem_limit_bytes=limit),
    )(*args)


def exchange(x, axes):
    return lax.all_to_all(x, axes, split_axis=0, concat_axis=0, tiled=True)


def spread(x, axes, count):
    return exchange(jnp.broadcast_to(x[None], (count, *x.shape)), axes)


def body(ny, nx, nz, patches, codes, support, block_shards, dictionary):
    rows, plen = patches.shape
    blocks = block_shards.shape[0]
    width = plen // nx
    nc = 2
    piece = SHARD // (ny * nc)
    sds = jax.ShapeDtypeStruct
    y, x, c = (lax.axis_index(a) for a in ("y", "x", "c"))
    ids = jnp.stack([y, x, c]).astype(jnp.int32)
    packed = call(
        pack_kernel,
        "ssvvv",
        tuple(sds((rows + 16, width), BF16) for _ in range(nx)),
        [],
        block_shards.T, ids, patches, codes.T, support.T, limit=56 * 1024 * 1024,
    )
    own = lax.dynamic_slice(dictionary, ((y * nc + c) * piece, x * width), (piece, width))
    by_z = spread(own, "z", nz).reshape(nz, piece, width)
    def ahead(sent, j):
        return lax.ppermute(sent, "x", [(i, (i + j) % nx) for i in range(nx)])

    held = [packed[0]] + [None if j == nx // 2 else ahead(packed[j], j) for j in range(1, nx)]
    by_z, far, *near = lax.optimization_barrier(
        (by_z, packed[nx // 2], *(h for h in held[1:] if h is not None))
    )
    copies = call(
        copies_kernel, "sv", sds((ny, nz + 1, piece, width), BF16), [], block_shards.T, by_z
    )
    mine = exchange(copies, "y")
    near.insert(nx // 2 - 1, ahead(far, nx // 2))
    held = [packed[0], *near]
    mine, *held = lax.optimization_barrier((mine, *held))
    other = lax.ppermute(mine, "c", [(0, 1), (1, 0)])
    names = jnp.concatenate([h[rows : rows + 1, 256 : 256 + 2 * blocks] for h in held], axis=1)
    near_shards = names.astype(jnp.int32).reshape(-1)
    common = (near_shards, ids, *held, mine, other)
    sizes = (ny, nx, plen)
    takes = "ss" + "v" * (nx + 2)
    grads = sds((nx, SLOTS, nx * rows), F32)
    matrices = call(
        functools.partial(first_codes_kernel, piece),
        "s" + "v" * nx,
        sds((nx, rows, 256), BF16),
        [],
        ids, *held,
    )
    first = call(
        lambda *r: refine_kernel(0, sizes, *r),
        takes + "v",
        sds((nx, SLOTS, nx * rows + 128), F32),
        [],
        *common,
        matrices,
    )
    first = exchange(first, "x")
    shards = first[:, : ny * nc, nx * rows : nx * rows + 2 * blocks].astype(jnp.int32).reshape(-1)
    second, codes_1 = call(
        lambda *r: refine_kernel(1, sizes, *r),
        takes + "v",
        (grads, sds((SLOTS, nx * rows), F32)),
        [],
        *common,
        first,
    )
    *home, msg, usage, codes_2 = call(
        lambda *r: refine_kernel(2, sizes, *r),
        takes + "vv",
        (
            *(sds((rows, width), BF16) for _ in range(nx)),
            sds((ny * nc, nx, MSG, 128), BF16),
            sds((nz, 128), F32),
            sds((SLOTS, rows), F32),
        ),
        [],
        *common,
        exchange(second, "x"),
        codes_1,
    )
    new_codes = codes_2.T
    got = exchange(msg, ("y", "c")).reshape(ny * nc * nx, MSG, 128)
    to_owner = call(
        lambda *r: stats_kernel(ny, nx, *r),
        "ssvv",
        sds((nz, MSG, 128), BF16),
        [pltpu.VMEM((nz * SHARD, 128), F32)],
        shards, ids, got, usage, us=10,
    )
    to_owner, *home = lax.optimization_barrier((to_owner, *home))
    at_owner = exchange(to_owner, "z")
    home = [home[0]] + [
        lax.ppermute(home[j], "x", [(i, (i - j) % nx) for i in range(nx)]) for j in range(1, nx)
    ]
    at_owner, *home = lax.optimization_barrier((at_owner, *home))
    final = call(total_kernel, "v", sds((ny * nx * nc, MSG, 128), BF16), [], at_owner)
    resid = call(home_kernel, "s" + "v" * nx, sds((rows, plen), BF16), [], ids, *home)
    new_dictionary = call(
        lambda *r: renew_kernel((ny, nx), *r),
        "vv",
        sds(dictionary.shape, BF16),
        [pltpu.VMEM(dictionary.shape, F32)],
        exchange(final, ("y", "x", "c")), dictionary,
    )
    return (new_dictionary, new_codes, resid)


def solution(mesh):
    fine = Mesh(mesh.devices.reshape(DP_SPLIT + (-1,)), ("y", "x", "c", "z"))
    row = P(("y", "x", "c", "z"), None)
    shard = P("z", None)
    return jax.shard_map(
        functools.partial(body, DP_SPLIT[0], DP_SPLIT[1], mesh.shape["group"]),
        mesh=fine,
        in_specs=(row, row, row, row, shard),
        out_specs=(shard, row, row),
        check_vma=False,
    )
```
